128 devices in a mesh: dp: 16 (over x_lo, y, core), inner: 8 (over z, x_hi).
Axes of the slice: x: 4 (x_hi: 2, x_lo: 2; x = x_hi * 2 + x_lo), y: 4, z: 4, core: 2. Of those that a mesh axis runs over, the one named last changes fastest.
Arguments:
- features: bfloat16 [32768, 4096], P(('dp', 'inner')), may hold values from -6 to 6
- proj_weight: bfloat16 [4096, 128], replicated, may hold values from -0.09375 to 0.09375
- partner: int32 [32768], P(('dp', 'inner')), may hold values from 0 to 32767, as said below
Outputs:
- loss: float32 [], replicated
- grad_weight: float32 [4096, 128], replicated
The draws below stay inside these ranges and needn't reach their ends.
Inputs may be any that keep to these rules, and one draw needn't show every extreme that they name: partner pairs the views: partner[partner[i]] == i and partner[i] != i; partners may lie on any device.
All inputs are finite; a program needn't handle non-finite values.
Results may differ from the reference program's by a relative error of at most 0.0006.
The reference program's roundings to bfloat16 on the way count: a program that leaves them out, or rounds other values in their place, can miss the bound.
Values may be sent and summed in bfloat16 or wider, within the bound.
A program may use at most 128 MiB of HBM per device.

```python
import math
import jax
import jax.numpy as jnp
from jax import lax

D = 4096
PROJ = 128
VIEWS = 32768


def draw_partner(key, part):
    key = jax.random.fold_in(key, 1)
    order = jax.random.permutation(key, VIEWS).astype(jnp.int32)
    first = order[0::2]
    second = order[1::2]
    result = jnp.zeros((VIEWS,), jnp.int32)
    result = result.at[first].set(second)
    return result.at[second].set(first)


def steps_of(key, shape, split, smallest, high):
    factor_of, own = 1.0, jax.random.fold_in(key, 6)
    for axis_at, blocks in split:
        heights = jnp.exp(jax.random.uniform(jax.random.fold_in(own, axis_at), (blocks,), jnp.float32, smallest / len(split), high / len(split)))
        factor_of = factor_of * jnp.repeat(heights, shape[axis_at] // blocks).reshape([-1 if axis == axis_at else 1 for axis in range(len(shape))])
    return factor_of


def noise(rng, dims, spread, most, cuts=(), held_as=jnp.bfloat16):
    values = spread * jax.random.normal(rng, dims, jnp.float32)
    if cuts:
        values = values * steps_of(rng, dims, cuts, -0.22, 0.18)
    return jnp.clip(values, -most, most).astype(held_as)


def setup_inputs(seed: int = 0) -> dict:
    key_list = jax.random.split(jax.random.key(seed), 4)
    features = noise(key_list[0], (VIEWS, D), 1.0, 6.0, ((0, 128),))
    proj_weight = noise(key_list[1], (D, PROJ), D ** -0.5, 0.09375)
    partner = draw_partner(jax.random.fold_in(key_list[3], 71), 0)
    return dict(features=features, proj_weight=proj_weight, partner=partner)


def reference(features, proj_weight, partner):
    inv_tau = 5.0
    z = jnp.dot(features, proj_weight, preferred_element_type=jnp.float32)
    norm = jnp.sqrt(lax.optimization_barrier(jnp.sum(z * z, axis=1, keepdims=True)) + 1e-06)
    u = z / norm
    ub = u.astype(jnp.bfloat16)
    views = ub.shape[0]
    block = math.gcd(512, views)
    count = views // block
    blocks = ub.reshape(count, block, ub.shape[1])
    starts = jnp.arange(count, dtype=jnp.int32) * block
    col_ids = jnp.arange(views, dtype=jnp.int32)

    def row_sums(item):
        rows_blk, first = item
        scores = jnp.dot(rows_blk, ub.T, preferred_element_type=jnp.float32) * inv_tau
        mask = col_ids[None, :] == (first + jnp.arange(block, dtype=jnp.int32))[:, None]
        expo = jnp.where(mask, jnp.float32(0.0), jnp.exp(scores - inv_tau))
        return lax.optimization_barrier(jnp.sum(expo, axis=1))
    rowsum = lax.map(row_sums, (blocks, starts)).reshape(views)
    lse = inv_tau + jnp.log(rowsum)
    paired = ub[partner]
    pos = lax.optimization_barrier(jnp.sum(ub.astype(jnp.float32) * paired.astype(jnp.float32), axis=1)) * inv_tau
    loss = jnp.mean(lse - pos)

    def grad_rows(item):
        rows_blk, first, lse_blk = item
        scores = jnp.dot(rows_blk, ub.T, preferred_element_type=jnp.float32) * inv_tau
        mask = col_ids[None, :] == (first + jnp.arange(block, dtype=jnp.int32))[:, None]
        probs = jnp.where(mask, jnp.float32(0.0), jnp.exp(scores - lse_blk[:, None])).astype(jnp.bfloat16)
        trans = jnp.where(mask, jnp.float32(0.0), jnp.exp(scores - lse[None, :])).astype(jnp.bfloat16)
        return jnp.dot(probs, ub, preferred_element_type=jnp.float32) + jnp.dot(trans, ub, preferred_element_type=jnp.float32)
    terms = lax.map(grad_rows, (blocks, starts, lse.reshape(count, block))).reshape(views, ub.shape[1])
    du = inv_tau * (terms - 2.0 * paired.astype(jnp.float32))
    dz = ((du - u * lax.optimization_barrier(jnp.sum(u * du, axis=1, keepdims=True))) / norm).astype(jnp.bfloat16)
    grad = jnp.dot(features.T, dz, preferred_element_type=jnp.float32) / jnp.sqrt(jnp.float32(views))
    return (loss, grad)
```

```python
import jax
import jax.numpy as jnp
from jax import lax
from jax.experimental import pallas as pl
from jax.experimental.pallas import tpu as pltpu
from jax.sharding import PartitionSpec as P

MESH = pl.DeviceIdType.MESH
F32 = jnp.float32
BF16 = jnp.bfloat16
VIEWS = 32768
D = 4096
HALF = D // 2
PROJ = 128
OWN = 256
SLOT = OWN + 16
INV_TAU = 5.0
SCALE2 = INV_TAU * 1.4426950408889634
NT = (((1,), (1,)), ((), ()))
TN = (((0,), (0,)), ((), ()))
EXACT = lax.Precision.HIGHEST

ROW_OFFS = [(dx, dc) for dc in range(2) for dx in range(4)]
ROW_OF = {off: slot for slot, off in enumerate(ROW_OFFS)}
COL_OFFS = sorted(
    [(dy, dz) for dy in range(4) for dz in range(4)],
    key=lambda o: (min(o[0], 4 - o[0]) + min(o[1], 4 - o[1]), o),
)
COL_OF = {off: slot for slot, off in enumerate(COL_OFFS)}
PARTS = ("x", "y", "z", "m")
PART_ROWS = HALF // len(PARTS)
RING_ROWS = PART_ROWS // 4
TILE = RING_ROWS // 16


def neg_col(off):
    return ((-off[0]) % 4, (-off[1]) % 4)


def neg_row(off):
    return ((-off[0]) % 4, off[1])


def coords():
    dp, inner = lax.axis_index("dp"), lax.axis_index("inner")
    x = (inner % 2) * 2 + dp // 8
    return x, (dp // 2) % 4, inner // 2, dp % 2


def device_at(x, y, z, c):
    return ((x % 2) * 8 + y * 2 + c, z * 2 + x // 2)


def peer(dx=0, dy=0, dz=0, dc=0):
    x, y, z, c = coords()
    return device_at((x + dx) % 4, (y + dy) % 4, (z + dz) % 4, (c + dc) % 2)


def ring_peer(part, d):
    c = coords()[3]
    if part == "x":
        return peer(dx=d)
    if part == "y":
        return peer(dy=d)
    if part == "z":
        return peer(dz=d)
    return peer(dx=d * (1 - c), dy=d * c)


def plane_peer(part, d1, d2):
    c = coords()[3]
    if part == "x":
        return peer(dy=d1, dz=d2)
    if part == "y":
        return peer(dx=d1, dz=d2)
    if part == "z":
        return peer(dx=d1, dy=d2)
    return peer(dx=d1 * c, dy=d1 * (1 - c), dz=d2)


def part_place(part):
    x, y, z, c = coords()
    if part == "x":
        return x, y, z
    if part == "y":
        return y, x, z
    if part == "z":
        return z, x, y
    return x * (1 - c) + y * c, y * (1 - c) + x * c, z


def all_peers():
    offs = []
    for dx in range(4):
        for dy in range(4):
            for dz in range(4):
                if (dx, dy, dz) != (0, 0, 0) and 0 in (dx, dy, dz):
                    offs.append((dx, dy, dz, 0))
    offs += [(dx, 0, 0, 1) for dx in range(4)]
    return offs


def send(src, dst, send_sem, recv_sem, device):
    copy = pltpu.make_async_remote_copy(
        src_ref=src, dst_ref=dst, send_sem=send_sem, recv_sem=recv_sem,
        device_id=device, device_id_type=MESH,
    )
    copy.start()


def wait_bytes(ref, sem):
    pltpu.make_async_copy(ref, ref, sem).wait()


def kernel(
    f_hbm, w_hbm, code_ref, g_hbm, loss_ref,
    feat, weight, feat_sib, u_ref, norm_ref, rows, cols, expo, acc,
    sums, sums_in, wts, wts_in, wide, paired, uw, quad, quad_sib, quad_ring,
    dz_own, dz_sib, grad, g1_in, g1, g2_in, out, loss1, loss2,
    load_sem, x_send, col_recv, row_recv, feat_recv, sum_recv, wt_recv, loss_recv1, loss_recv2,
    qs_recv, qr_recv, dz_recv, g1_recv, g2_recv, ag_recv, ring_recv, rel_recv, store_sem,
):
    x, y, z, c = coords()
    barrier = pltpu.get_barrier_semaphore()
    peers = all_peers()
    for off in peers:
        pl.semaphore_signal(barrier, inc=1, device_id=peer(*off), device_id_type=MESH)
    load_w = pltpu.make_async_copy(w_hbm, weight, load_sem.at[0])
    load_f = pltpu.make_async_copy(f_hbm, feat, load_sem.at[1])
    load_w.start()
    load_f.start()
    load_w.wait()
    load_f.wait()

    zed = jnp.dot(feat[...], weight[...], preferred_element_type=F32)
    norm = jnp.sqrt(jnp.sum(zed * zed, axis=1, keepdims=True) + 1e-06)
    u = zed / norm
    u_ref[...] = u
    norm_ref[...] = jnp.broadcast_to(norm, (OWN, PROJ))
    ub = u.astype(BF16)
    rows[0:OWN, :] = ub
    rows[OWN:SLOT, :] = code_ref[...]
    cols[0:OWN, :] = ub
    pl.semaphore_wait(barrier, len(peers))

    def row_slot(slot):
        return rows.at[pl.ds(slot * SLOT, SLOT)]

    def col_slot(slot):
        return cols.at[pl.ds(slot * OWN, OWN)]

    for dx in (2, 1, 3):
        to = ROW_OF[neg_row((dx, 0))]
        send(row_slot(0), row_slot(to), x_send.at[0], row_recv.at[to], peer(dx=dx))
    send(row_slot(0), row_slot(4), x_send.at[0], row_recv.at[4], peer(dc=1))
    for slot in range(1, 16):
        dy, dz = COL_OFFS[slot]
        to = COL_OF[neg_col((dy, dz))]
        send(col_slot(0), col_slot(to), x_send.at[1], col_recv.at[to], peer(dy=dy, dz=dz))
    send(
        feat.at[:, pl.ds(pl.multiple_of((1 - c) * HALF, HALF), HALF)], feat_sib,
        x_send.at[2], feat_recv.at[0], peer(dc=1),
    )

    def lanes(e):
        total = e[:, 0:PROJ]
        for q in range(1, e.shape[1] // PROJ):
            total = total + e[:, q * PROJ : (q + 1) * PROJ]
        return total

    def scores(slot, first):
        return jnp.exp2(
            lax.dot_general(
                rows[slot * SLOT : slot * SLOT + OWN, :], cols[pl.ds(first, OWN), :], NT,
                preferred_element_type=F32,
            )
            * SCALE2
        )

    for slot in (0, 4, 1, 3, 2, 5, 7, 6):
        if slot:
            wait_bytes(row_slot(slot), row_recv.at[slot])
        if slot in (1, 2, 3):
            send(row_slot(slot), row_slot(4 + slot), x_send.at[0], row_recv.at[4 + slot], peer(dc=1))
        e = scores(slot, 0)
        if slot == 0:
            at_row = lax.broadcasted_iota(jnp.int32, (OWN, OWN), 0)
            at_col = lax.broadcasted_iota(jnp.int32, (OWN, OWN), 1)
            e = jnp.where(at_row == at_col, 0.0, e)
        expo[slot * OWN : (slot + 1) * OWN, 0:OWN] = e.astype(BF16)
        acc[slot * OWN : (slot + 1) * OWN, :] = lanes(e)

    def pass1(step, carry):
        first = pl.multiple_of(step * OWN, OWN)
        wait_bytes(cols.at[pl.ds(first, OWN)], col_recv.at[step])
        for slot in range(8):
            e = scores(slot, first)
            expo[slot * OWN : (slot + 1) * OWN, pl.ds(first, OWN)] = e.astype(BF16)
            acc[slot * OWN : (slot + 1) * OWN, :] += lanes(e)
        return carry

    lax.fori_loop(1, 16, pass1, 0)

    ones = jnp.ones((8, PROJ), F32)
    for slot in range(8):
        part = lax.dot_general(
            ones, acc[slot * OWN : (slot + 1) * OWN, :], NT,
            preferred_element_type=F32, precision=EXACT,
        )
        sums[slot : slot + 1, :] = part[0:1, :]
    for slot in (2, 6, 1, 3, 5, 7, 4):
        dx, dc = ROW_OFFS[slot]
        to = ROW_OF[neg_row((dx, dc))]
        send(sums, sums_in.at[to], x_send.at[3], sum_recv.at[to], peer(dx=dx, dc=dc))

    for slot in range(16):
        wide[:, slot * PROJ : (slot + 1) * PROJ] = cols[slot * OWN : (slot + 1) * OWN, :]
    sel_row = lax.broadcasted_iota(jnp.int32, (16, PROJ), 0)
    lane = lax.broadcasted_iota(jnp.int32, (OWN, PROJ), 1).astype(F32)

    def column_of(code, at):
        halves = [
            lax.dot_general(
                code, jnp.where(sel_row == at + h, 1.0, 0.0).astype(BF16), TN,
                preferred_element_type=F32,
            )
            for h in range(2)
        ]
        return jnp.concatenate(halves, axis=0)

    def partners(slot, pos):
        code = rows[slot * SLOT + OWN : (slot + 1) * SLOT, :]
        owner, place = column_of(code, 0), column_of(code, 2)
        hot = jnp.concatenate(
            [jnp.where(place == lane, 1.0, 0.0), jnp.where(place == lane + PROJ, 1.0, 0.0)], axis=1
        ).astype(BF16)
        found = jnp.dot(hot, wide[...], preferred_element_type=F32)
        total = jnp.zeros((OWN, PROJ), F32)
        for k in range(16):
            dy, dz = COL_OFFS[k]
            dp, inner = peer(dy=dy, dz=dz)
            here = (dp * 8 + inner).astype(F32)
            total = total + jnp.where(owner == here, found[:, k * PROJ : (k + 1) * PROJ], 0.0)
        paired[slot * OWN : (slot + 1) * OWN, :] = total
        own = rows[slot * SLOT : slot * SLOT + OWN, :].astype(F32)
        return pos + own * total

    pos = jnp.zeros((OWN, PROJ), F32)
    for slot in range(4):
        pos = partners(slot, pos)

    for slot in range(1, 8):
        wait_bytes(sums_in.at[slot], sum_recv.at[slot])
    for slot in range(8):
        dx, dc = ROW_OFFS[slot]
        total = sums[slot : slot + 1, :]
        for sender in range(1, 8):
            ox, oc = ROW_OFFS[sender]
            at = ROW_OF[((dx - ox) % 4, (dc - oc) % 2)]
            total = total + sums_in[sender, at : at + 1, :]
        wts[slot : slot + 1, :] = 1.0 / total
        if slot == 0:
            log_sum = jnp.sum(jnp.log(total))
    for slot in range(1, 16):
        dy, dz = COL_OFFS[slot]
        to = COL_OF[neg_col((dy, dz))]
        send(wts, wts_in.at[to], x_send.at[4], wt_recv.at[to], peer(dy=dy, dz=dz))

    for slot in range(4, 8):
        pos = partners(slot, pos)
    loss_part = log_sum - INV_TAU * jnp.sum(pos)
    me1 = x * 2 + c
    loss1[me1] = jnp.full((8, PROJ), loss_part, F32)
    for slot in range(1, 8):
        dx, dc = ROW_OFFS[slot]
        to = ROW_OF[neg_row((dx, dc))]
        send(loss1.at[me1], loss1.at[me1], x_send.at[5], loss_recv1.at[to], peer(dx=dx, dc=dc))

    sel8 = jnp.where(lax.broadcasted_iota(jnp.int32, (8, PROJ), 0) == 0, 1.0, 0.0)

    def weigh(slot, table):
        w = lax.dot_general(table, sel8, TN, preferred_element_type=F32, precision=EXACT)
        block = cols[slot * OWN : (slot + 1) * OWN, :]
        uw[slot * OWN : (slot + 1) * OWN, 0:PROJ] = block
        uw[slot * OWN : (slot + 1) * OWN, PROJ : 2 * PROJ] = (block.astype(F32) * w).astype(BF16)

    weigh(0, wts[...])
    for slot in range(1, 16):
        wait_bytes(wts_in.at[slot], wt_recv.at[slot])
        weigh(slot, wts_in[slot])

    def terms(slot):
        both = jnp.dot(
            expo[slot * OWN : (slot + 1) * OWN, :], uw[...], preferred_element_type=F32
        )
        sel = jnp.where(lax.broadcasted_iota(jnp.int32, (8, PROJ), 0) == slot, 1.0, 0.0)
        w = lax.dot_general(wts[...], sel, TN, preferred_element_type=F32, precision=EXACT)
        return (
            w * both[:, 0:PROJ] + both[:, PROJ : 2 * PROJ]
            - 2.0 * paired[slot * OWN : (slot + 1) * OWN, :]
        )

    def quad_slot(slot):
        return quad.at[pl.ds(slot * OWN, OWN)]

    for slot in (6, 5, 7, 4):
        quad[slot * OWN : (slot + 1) * OWN, :] = terms(slot)
        send(quad_slot(slot), quad_sib.at[slot - 4], x_send.at[6], qs_recv.at[slot - 4], peer(dc=1))
    for slot in (2, 1, 3, 0):
        part = terms(slot)
        wait_bytes(quad_sib.at[slot], qs_recv.at[slot])
        quad[slot * OWN : (slot + 1) * OWN, :] = part + quad_sib[slot]
        if slot:
            to = (-slot) % 4
            send(quad_slot(slot), quad_ring.at[to], x_send.at[7], qr_recv.at[to], peer(dx=slot))

    for slot in range(1, 8):
        wait_bytes(loss1.at[0], loss_recv1.at[slot])
    total = loss1[0]
    for k in range(1, 8):
        total = total + loss1[k]
    me2 = y * 4 + z
    loss2[me2] = total
    for slot in range(1, 16):
        dy, dz = COL_OFFS[slot]
        to = COL_OF[neg_col((dy, dz))]
        send(loss2.at[me2], loss2.at[me2], x_send.at[8], loss_recv2.at[to], peer(dy=dy, dz=dz))

    summed = quad[0:OWN, :]
    for d in (1, 3, 2):
        wait_bytes(quad_ring.at[d], qr_recv.at[d])
        summed = summed + quad_ring[d]
    du = INV_TAU * summed
    uu = u_ref[...]
    dz_own[...] = (
        (du - uu * jnp.sum(uu * du, axis=1, keepdims=True)) / norm_ref[...]
    ).astype(BF16)
    send(dz_own, dz_sib, x_send.at[9], dz_recv.at[0], peer(dc=1))

    mine = pl.multiple_of(c * HALF, HALF)
    grad[...] = lax.dot_general(
        feat[:, pl.ds(mine, HALF)], dz_own[...], TN, preferred_element_type=F32
    )
    wait_bytes(feat_sib, feat_recv.at[0])
    wait_bytes(dz_sib, dz_recv.at[0])
    grad[...] += lax.dot_general(feat_sib[...], dz_sib[...], TN, preferred_element_type=F32)

    def ring_block(part, t):
        return pl.ds(pl.multiple_of(part * PART_ROWS + t * RING_ROWS, RING_ROWS), RING_ROWS)

    places = [part_place(name) for name in PARTS]
    for d in (2, 1, 3):
        for p, name in enumerate(PARTS):
            t = places[p][0]
            at = (-d) % 4
            send(
                grad.at[ring_block(p, (t + d) % 4)], g1_in.at[p, at],
                x_send.at[10], g1_recv.at[p, at], ring_peer(name, d),
            )
    for p, name in enumerate(PARTS):
        t, s1, s2 = places[p]
        total = grad[ring_block(p, t), :]
        for d in range(1, 4):
            wait_bytes(g1_in.at[p, d], g1_recv.at[p, d])
            total = total + g1_in[p, d]
        g1[p] = total
        for slot in range(15, 0, -1):
            d1, d2 = COL_OFFS[slot]
            to = COL_OF[neg_col((d1, d2))]
            at = ((s1 + d1) % 4) * 4 + (s2 + d2) % 4
            send(
                g1.at[p, pl.ds(pl.multiple_of(at * TILE, TILE), TILE)],
                g2_in.at[p, pl.ds(to * TILE, TILE)],
                x_send.at[11], g2_recv.at[p], plane_peer(name, d1, d2),
            )
    base = c * HALF
    for p, name in enumerate(PARTS):
        t, s1, s2 = places[p]
        total = g1[p, pl.ds(pl.multiple_of((s1 * 4 + s2) * TILE, TILE), TILE), :]
        wait_bytes(g2_in.at[p, pl.ds(TILE, 15 * TILE)], g2_recv.at[p])
        for slot in range(1, 16):
            total = total + g2_in[p, slot * TILE : (slot + 1) * TILE, :]
        at = pl.ds(
            pl.multiple_of(base + p * PART_ROWS + t * RING_ROWS + (s1 * 4 + s2) * TILE, TILE), TILE
        )
        out[at, :] = total * (1.0 / VIEWS**0.5)
        for slot in range(15, 0, -1):
            d1, d2 = COL_OFFS[slot]
            send(out.at[at], out.at[at], x_send.at[12], ag_recv.at[p], plane_peer(name, d1, d2))

    def out_block(p, t, first=base):
        return out.at[
            pl.ds(pl.multiple_of(first + p * PART_ROWS + t * RING_ROWS, RING_ROWS), RING_ROWS)
        ]

    for p, name in enumerate(PARTS):
        t = places[p][0]
        wait_bytes(out.at[pl.ds(0, 15 * TILE)], ag_recv.at[p])
        block = out_block(p, t)
        for d in (2, 1, 3):
            at = (-d) % 4
            send(block, block, x_send.at[13], ring_recv.at[p, at], ring_peer(name, d))
        send(block, block, x_send.at[14], rel_recv.at[p, 0], peer(dc=1))
    for d in (1, 3, 2):
        for p, name in enumerate(PARTS):
            t = places[p][0]
            block = out_block(p, (t + d) % 4)
            wait_bytes(block, ring_recv.at[p, d])
            send(block, block, x_send.at[14], rel_recv.at[p, d], peer(dc=1))
    half = out.at[pl.ds(pl.multiple_of(base, HALF), HALF)]
    store1 = pltpu.make_async_copy(
        half, g_hbm.at[pl.ds(pl.multiple_of(base, HALF), HALF)], store_sem.at[0]
    )
    store1.start()

    for slot in range(1, 16):
        wait_bytes(loss2.at[0], loss_recv2.at[slot])
    total = loss2[0]
    for k in range(1, 16):
        total = total + loss2[k]
    loss_ref[...] = total * (1.0 / VIEWS)

    for d in (0, 1, 3, 2):
        for p in range(len(PARTS)):
            wait_bytes(out.at[pl.ds(0, RING_ROWS)], rel_recv.at[p, d])
    other = pl.multiple_of((1 - c) * HALF, HALF)
    store2 = pltpu.make_async_copy(
        out.at[pl.ds(other, HALF)], g_hbm.at[pl.ds(other, HALF)], store_sem.at[1]
    )
    store2.start()

    wait_bytes(rows.at[pl.ds(0, 7 * SLOT)], x_send.at[0])
    wait_bytes(cols.at[pl.ds(0, 15 * OWN)], x_send.at[1])
    wait_bytes(feat_sib, x_send.at[2])
    wait_bytes(sums_in.at[pl.ds(0, 7)], x_send.at[3])
    wait_bytes(wts_in.at[pl.ds(0, 15)], x_send.at[4])
    wait_bytes(loss1.at[pl.ds(0, 7)], x_send.at[5])
    wait_bytes(quad_sib, x_send.at[6])
    wait_bytes(quad_ring.at[pl.ds(0, 3)], x_send.at[7])
    wait_bytes(loss2.at[pl.ds(0, 15)], x_send.at[8])
    wait_bytes(dz_sib, x_send.at[9])
    wait_bytes(grad.at[pl.ds(0, 12 * RING_ROWS)], x_send.at[10])
    wait_bytes(grad.at[pl.ds(0, 60 * TILE)], x_send.at[11])
    wait_bytes(grad.at[pl.ds(0, 60 * TILE)], x_send.at[12])
    wait_bytes(grad.at[pl.ds(0, 12 * RING_ROWS)], x_send.at[13])
    wait_bytes(grad, x_send.at[14])
    store1.wait()
    store2.wait()


def per_device(features, proj_weight, partner):
    code = jnp.concatenate([partner // OWN, partner % OWN]).reshape(4, PROJ)
    code = jnp.pad(code, ((0, 12), (0, 0))).astype(BF16)
    dma = pltpu.SemaphoreType.DMA
    grad, loss = pl.pallas_call(
        kernel,
        out_shape=(
            jax.ShapeDtypeStruct((D, PROJ), F32),
            jax.ShapeDtypeStruct((8, PROJ), F32),
        ),
        in_specs=[
            pl.BlockSpec(memory_space=pl.ANY),
            pl.BlockSpec(memory_space=pl.ANY),
            pl.BlockSpec(memory_space=pltpu.VMEM),
        ],
        out_specs=(pl.BlockSpec(memory_space=pl.ANY), pl.BlockSpec(memory_space=pltpu.VMEM)),
        scratch_shapes=[
            pltpu.VMEM((OWN, D), BF16),
            pltpu.VMEM((D, PROJ), BF16),
            pltpu.VMEM((OWN, HALF), BF16),
            pltpu.VMEM((OWN, PROJ), F32),
            pltpu.VMEM((OWN, PROJ), F32),
            pltpu.VMEM((8 * SLOT, PROJ), BF16),
            pltpu.VMEM((16 * OWN, PROJ), BF16),
            pltpu.VMEM((8 * OWN, 16 * OWN), BF16),
            pltpu.VMEM((8 * OWN, PROJ), F32),
            pltpu.VMEM((8, OWN), F32),
            pltpu.VMEM((8, 8, OWN), F32),
            pltpu.VMEM((8, OWN), F32),
            pltpu.VMEM((16, 8, OWN), F32),
            pltpu.VMEM((OWN, 16 * PROJ), BF16),
            pltpu.VMEM((8 * OWN, PROJ), F32),
            pltpu.VMEM((16 * OWN, 2 * PROJ), BF16),
            pltpu.VMEM((8 * OWN, PROJ), F32),
            pltpu.VMEM((4, OWN, PROJ), F32),
            pltpu.VMEM((4, OWN, PROJ), F32),
            pltpu.VMEM((OWN, PROJ), BF16),
            pltpu.VMEM((OWN, PROJ), BF16),
            pltpu.VMEM((HALF, PROJ), F32),
            pltpu.VMEM((4, 4, RING_ROWS, PROJ), F32),
            pltpu.VMEM((4, RING_ROWS, PROJ), F32),
            pltpu.VMEM((4, RING_ROWS, PROJ), F32),
            pltpu.VMEM((D, PROJ), F32),
            pltpu.VMEM((8, 8, PROJ), F32),
            pltpu.VMEM((16, 8, PROJ), F32),
            dma((2,)),
            dma((15,)),
            dma((16,)),
            dma((8,)),
            dma((1,)),
            dma((8,)),
            dma((16,)),
            dma((8,)),
            dma((16,)),
            dma((4,)),
            dma((4,)),
            dma((1,)),
            dma((4, 4)),
            dma((4,)),
            dma((4,)),
            dma((4, 4)),
            dma((4, 4)),
            dma((2,)),
        ],
        compiler_params=pltpu.CompilerParams(
            collective_id=0, has_side_effects=True, vmem_limit_bytes=56 * 2**20
        ),
        name="simclr_head",
    )(features, proj_weight, code)
    return loss[0, 0], grad


def solution(mesh):
    placed = (P(("dp", "inner"), None), P(), P(("dp", "inner")))
    return jax.shard_map(
        per_device, mesh=mesh, in_specs=placed, out_specs=(P(), P()), check_vma=False
    )
```

```python
import jax
import jax.numpy as jnp
from jax import lax
from jax.experimental import pallas as pl
from jax.experimental.pallas import tpu as pltpu
from jax.sharding import PartitionSpec as P

MESH = pl.DeviceIdType.MESH
F32 = jnp.float32
BF16 = jnp.bfloat16
VIEWS = 32768
D = 4096
HALF = D // 2
QUARTER = D // 4
PROJ = 128
OWN = 256
GROUP = 4 * OWN
SLOT = OWN + 16
INV_TAU = 5.0
SCALE2 = INV_TAU * 1.4426950408889634
NT = (((1,), (1,)), ((), ()))
TN = (((0,), (0,)), ((), ()))

ROW_OFFS = [(dx, dc) for dc in range(2) for dx in range(4)]
ROW_OF = {off: slot for slot, off in enumerate(ROW_OFFS)}
COL_OFFS = sorted(
    [(dy, dz) for dy in range(4) for dz in range(4)],
    key=lambda o: (min(o[0], 4 - o[0]) + min(o[1], 4 - o[1]), o),
)
COL_OF = {off: slot for slot, off in enumerate(COL_OFFS)}
RING_AXIS = {slot: int(off[0] == 0) for slot, off in enumerate(COL_OFFS) if slot and 0 in off}
PARTS = ("x", "y", "z", "m")
PART_ROWS = HALF // len(PARTS)
RING_ROWS = PART_ROWS // 4
TILE = RING_ROWS // 16


def neg_col(off):
    return ((-off[0]) % 4, (-off[1]) % 4)


def neg_row(off):
    return ((-off[0]) % 4, off[1])


def coords():
    dp, inner = lax.axis_index("dp"), lax.axis_index("inner")
    x = (inner % 2) * 2 + dp // 8
    return x, (dp // 2) % 4, inner // 2, dp % 2


def device_at(x, y, z, c):
    return ((x % 2) * 8 + y * 2 + c, z * 2 + x // 2)


def peer(dx=0, dy=0, dz=0, dc=0):
    x, y, z, c = coords()
    return device_at((x + dx) % 4, (y + dy) % 4, (z + dz) % 4, (c + dc) % 2)


def ring_peer(part, d):
    c = coords()[3]
    if part == "x":
        return peer(dx=d)
    if part == "y":
        return peer(dy=d)
    if part == "z":
        return peer(dz=d)
    return peer(dx=d * (1 - c), dy=d * c)


def plane_peer(part, d1, d2):
    c = coords()[3]
    if part == "x":
        return peer(dy=d1, dz=d2)
    if part == "y":
        return peer(dx=d1, dz=d2)
    if part == "z":
        return peer(dx=d1, dy=d2)
    return peer(dx=d1 * c, dy=d1 * (1 - c), dz=d2)


def part_place(part):
    x, y, z, c = coords()
    if part == "x":
        return x, y, z
    if part == "y":
        return y, x, z
    if part == "z":
        return z, x, y
    return x * (1 - c) + y * c, y * (1 - c) + x * c, z


def all_peers():
    offs = []
    for dx in range(4):
        for dy in range(4):
            for dz in range(4):
                if (dx, dy, dz) != (0, 0, 0) and 0 in (dx, dy, dz):
                    offs.append((dx, dy, dz, 0))
    offs += [(dx, 0, 0, 1) for dx in range(4)]
    return offs


def send(src, dst, send_sem, recv_sem, device):
    copy = pltpu.make_async_remote_copy(
        src_ref=src, dst_ref=dst, send_sem=send_sem, recv_sem=recv_sem,
        device_id=device, device_id_type=MESH,
    )
    copy.start()


def wait_bytes(ref, sem):
    pltpu.make_async_copy(ref, ref, sem).wait()


def kernel(
    f_hbm, w_hbm, partner_ref, g_ref, loss_ref,
    feat, weight, feat_sib, u_ref, norm_ref, rows, cols, expo, acc,
    sums, sums_in, wts, wts_in, wide, paired, uw, quad, quad_sib, quad_ring,
    dz_own, dz_sib, grad, g1_in, g1, g2_in, out, loss1, loss2,
    load_sem, x_send, col_recv, row_recv, feat_recv, sum_recv, wt_recv, loss_recv1, loss_recv2,
    qs_recv, qr_recv, dz_recv, g1_recv, g2_recv, ag_recv, ring_recv, rel_recv, store_sem,
):
    sent = [
        (rows.at[pl.ds(0, 7 * SLOT)], 0),
        (cols.at[pl.ds(0, 15 * OWN)], 1),
        (feat_sib, 2),
        (sums_in.at[pl.ds(0, 7)], 3),
        (wts_in.at[pl.ds(0, 15)], 4),
        (loss1.at[pl.ds(0, 7)], 5),
        (quad_sib, 6),
        (quad_ring.at[pl.ds(0, 3)], 7),
        (loss2.at[pl.ds(0, 15)], 8),
        (dz_sib, 9),
        (grad.at[pl.ds(0, 12 * RING_ROWS)], 10),
        (grad.at[pl.ds(0, 60 * TILE)], 11),
        (grad.at[pl.ds(0, 60 * TILE)], 12),
        (grad.at[pl.ds(0, 12 * RING_ROWS)], 13),
        (grad, 14),
    ]
    x, y, z, c = coords()
    loads = []
    for k in range(4):
        depth = pl.ds(k * QUARTER, QUARTER)
        loads.append(
            (
                pltpu.make_async_copy(w_hbm.at[depth], weight.at[depth], load_sem.at[k]),
                pltpu.make_async_copy(f_hbm.at[:, depth], feat.at[:, depth], load_sem.at[4 + k]),
            )
        )
    for pair in loads:
        for load in pair:
            load.start()
    barrier = pltpu.get_barrier_semaphore()
    peers = all_peers()
    for off in peers:
        pl.semaphore_signal(barrier, inc=1, device_id=peer(*off), device_id_type=MESH)

    owner_of, place_of = partner_ref[...] // OWN, partner_ref[...] % OWN
    at = lax.broadcasted_iota(jnp.int32, (16, PROJ), 0)
    code = jnp.zeros((16, PROJ), F32)
    for k, row in enumerate((owner_of[0:1], owner_of[1:2], place_of[0:1], place_of[1:2])):
        code = jnp.where(at == k, row.astype(F32), code)
    rows[OWN:SLOT, :] = code.astype(BF16)

    zed = None
    for k, pair in enumerate(loads):
        for load in pair:
            load.wait()
        term = jnp.dot(
            feat[:, k * QUARTER : (k + 1) * QUARTER], weight[k * QUARTER : (k + 1) * QUARTER, :],
            preferred_element_type=F32,
        )
        zed = term if zed is None else zed + term
    norm = jnp.sqrt(jnp.sum(zed * zed, axis=1, keepdims=True) + 1e-06)
    u = zed / norm
    u_ref[...] = u
    norm_ref[...] = jnp.broadcast_to(norm, (OWN, PROJ))
    ub = u.astype(BF16)
    rows[0:OWN, :] = ub
    cols[0:OWN, :] = ub
    pl.semaphore_wait(barrier, len(peers))

    def row_slot(slot):
        return rows.at[pl.ds(slot * SLOT, SLOT)]

    def col_slot(slot):
        return cols.at[pl.ds(slot * OWN, OWN)]

    def col_half(slot, half):
        return cols.at[pl.ds(slot * OWN + half * (OWN // 2), OWN // 2)]

    for dx in (1, 3, 2):
        to = ROW_OF[neg_row((dx, 0))]
        send(row_slot(0), row_slot(to), x_send.at[0], row_recv.at[to], peer(dx=dx))
    send(row_slot(0), row_slot(4), x_send.at[0], row_recv.at[4], peer(dc=1))
    for turn in range(2):
        for d in (1, 3, 2):
            for axis in range(2):
                half = axis ^ turn
                off = (d, 0) if axis == 0 else (0, d)
                to = COL_OF[neg_col(off)]
                send(
                    col_half(0, half), col_half(to, half), x_send.at[1],
                    col_recv.at[to, half], peer(dy=off[0], dz=off[1]),
                )

    def pass_on(axis, d):
        off = (d, 0) if axis == 0 else (0, d)
        slot = COL_OF[off]
        wait_bytes(col_half(slot, axis), col_recv.at[slot, axis])
        for e in (1, 3, 2):
            hop = (0, e) if axis == 0 else (e, 0)
            to = COL_OF[((off[0] - hop[0]) % 4, (off[1] - hop[1]) % 4)]
            send(
                col_half(slot, axis), col_half(to, axis), x_send.at[1],
                col_recv.at[to, axis], peer(dy=hop[0], dz=hop[1]),
            )

    def pass_row(slot):
        wait_bytes(row_slot(slot), row_recv.at[slot])
        send(row_slot(slot), row_slot(4 + slot), x_send.at[0], row_recv.at[4 + slot], peer(dc=1))

    for d in (1, 3, 2):
        pass_on(0, d)
        pass_on(1, d)
        pass_row(d)
    send(
        feat.at[:, pl.ds(pl.multiple_of((1 - c) * HALF, HALF), HALF)], feat_sib,
        x_send.at[2], feat_recv.at[0], peer(dc=1),
    )

    def lanes(e):
        total = e[:, 0:PROJ]
        for q in range(1, e.shape[1] // PROJ):
            total = total + e[:, q * PROJ : (q + 1) * PROJ]
        return total

    def scores(slot, first):
        return jnp.exp2(
            lax.dot_general(
                rows[slot * SLOT : slot * SLOT + OWN, :], cols[pl.ds(first, GROUP), :], NT,
                preferred_element_type=F32,
            )
            * SCALE2
        )

    for slot in range(1, 4):
        wait_bytes(col_half(slot, 1 - RING_AXIS[slot]), col_recv.at[slot, 1 - RING_AXIS[slot]])
    for slot in (0, 4, 1, 3, 2, 5, 7, 6):
        if slot > 3:
            wait_bytes(row_slot(slot), row_recv.at[slot])
        e = scores(slot, 0)
        if slot == 0:
            at_row = lax.broadcasted_iota(jnp.int32, (OWN, GROUP), 0)
            at_col = lax.broadcasted_iota(jnp.int32, (OWN, GROUP), 1)
            e = jnp.where(at_row == at_col, 0.0, e)
        expo[slot * OWN : (slot + 1) * OWN, 0:GROUP] = e.astype(BF16)
        acc[slot * OWN : (slot + 1) * OWN, :] = lanes(e)

    for group in range(1, 4):
        for slot in range(4 * group, 4 * group + 4):
            for half in range(2):
                if slot not in RING_AXIS or half != RING_AXIS[slot]:
                    wait_bytes(col_half(slot, half), col_recv.at[slot, half])
        for slot in range(8):
            e = scores(slot, group * GROUP)
            expo[slot * OWN : (slot + 1) * OWN, group * GROUP : (group + 1) * GROUP] = e.astype(BF16)
            acc[slot * OWN : (slot + 1) * OWN, :] += lanes(e)

    eye = lax.broadcasted_iota(jnp.int32, (PROJ, PROJ), 0) == lax.broadcasted_iota(
        jnp.int32, (PROJ, PROJ), 1
    )

    def to_row(column):
        return jnp.sum(jnp.where(eye, column, 0.0), axis=0, keepdims=True)

    def to_column(row):
        halves = [
            jnp.sum(jnp.where(eye, row[:, h * PROJ : (h + 1) * PROJ], 0.0), axis=1, keepdims=True)
            for h in range(2)
        ]
        return jnp.broadcast_to(jnp.concatenate(halves, axis=0), (OWN, PROJ))

    for slot in range(8):
        for h in range(2):
            first = slot * OWN + h * PROJ
            column = jnp.sum(acc[first : first + PROJ, :], axis=1, keepdims=True)
            sums[slot : slot + 1, h * PROJ : (h + 1) * PROJ] = to_row(column)
    for slot in (2, 6, 1, 3, 5, 7, 4):
        dx, dc = ROW_OFFS[slot]
        to = ROW_OF[neg_row((dx, dc))]
        send(sums, sums_in.at[to], x_send.at[3], sum_recv.at[to], peer(dx=dx, dc=dc))

    for slot in range(16):
        wide[:, slot * PROJ : (slot + 1) * PROJ] = cols[slot * OWN : (slot + 1) * OWN, :]
    lane = lax.broadcasted_iota(jnp.int32, (OWN, PROJ), 1).astype(F32)

    def partners(slot, pos):
        code = rows[slot * SLOT + OWN : (slot + 1) * SLOT, :].astype(F32)
        owner = to_column(jnp.concatenate([code[0:1], code[1:2]], axis=1))
        place = to_column(jnp.concatenate([code[2:3], code[3:4]], axis=1))
        hot = jnp.concatenate(
            [jnp.where(place == lane, 1.0, 0.0), jnp.where(place == lane + PROJ, 1.0, 0.0)], axis=1
        ).astype(BF16)
        found = jnp.dot(hot, wide[...], preferred_element_type=F32)
        total = jnp.zeros((OWN, PROJ), F32)
        for k in range(16):
            dy, dz = COL_OFFS[k]
            dp, inner = peer(dy=dy, dz=dz)
            here = (dp * 8 + inner).astype(F32)
            total = total + jnp.where(owner == here, found[:, k * PROJ : (k + 1) * PROJ], 0.0)
        paired[slot * OWN : (slot + 1) * OWN, :] = total
        own = rows[slot * SLOT : slot * SLOT + OWN, :].astype(F32)
        return pos + own * total

    pos = jnp.zeros((OWN, PROJ), F32)
    for slot in range(4):
        pos = partners(slot, pos)

    for slot in range(1, 8):
        wait_bytes(sums_in.at[slot], sum_recv.at[slot])
    for slot in range(8):
        dx, dc = ROW_OFFS[slot]
        total = sums[slot : slot + 1, :]
        for sender in range(1, 8):
            ox, oc = ROW_OFFS[sender]
            at = ROW_OF[((dx - ox) % 4, (dc - oc) % 2)]
            total = total + sums_in[sender, at : at + 1, :]
        wts[slot : slot + 1, :] = 1.0 / total
        if slot == 0:
            log_sum = jnp.sum(jnp.log(total))
    for slot in range(1, 16):
        dy, dz = COL_OFFS[slot]
        to = COL_OF[neg_col((dy, dz))]
        send(wts, wts_in.at[to], x_send.at[4], wt_recv.at[to], peer(dy=dy, dz=dz))

    for slot in range(4, 8):
        pos = partners(slot, pos)
    loss_part = log_sum - INV_TAU * jnp.sum(pos)
    me1 = x * 2 + c
    loss1[me1] = jnp.full((8, PROJ), loss_part, F32)
    for slot in range(1, 8):
        dx, dc = ROW_OFFS[slot]
        to = ROW_OF[neg_row((dx, dc))]
        send(loss1.at[me1], loss1.at[me1], x_send.at[5], loss_recv1.at[to], peer(dx=dx, dc=dc))

    def weigh(slot, row):
        block = cols[slot * OWN : (slot + 1) * OWN, :]
        uw[slot * OWN : (slot + 1) * OWN, 0:PROJ] = block
        uw[slot * OWN : (slot + 1) * OWN, PROJ : 2 * PROJ] = (
            block.astype(F32) * to_column(row)
        ).astype(BF16)

    weigh(0, wts[0:1, :])
    for slot in range(1, 16):
        wait_bytes(wts_in.at[slot], wt_recv.at[slot])
        weigh(slot, wts_in[slot, 0:1, :])

    def terms(slot):
        both = jnp.dot(
            expo[slot * OWN : (slot + 1) * OWN, :], uw[...], preferred_element_type=F32
        )
        w = to_column(wts[slot : slot + 1, :])
        return (
            w * both[:, 0:PROJ] + both[:, PROJ : 2 * PROJ]
            - 2.0 * paired[slot * OWN : (slot + 1) * OWN, :]
        )

    def quad_slot(slot):
        return quad.at[pl.ds(slot * OWN, OWN)]

    for slot in (6, 5, 2, 7, 1, 4, 3, 0):
        part = terms(slot)
        if slot > 3:
            quad[slot * OWN : (slot + 1) * OWN, :] = part
            send(
                quad_slot(slot), quad_sib.at[slot - 4], x_send.at[6], qs_recv.at[slot - 4],
                peer(dc=1),
            )
            continue
        wait_bytes(quad_sib.at[slot], qs_recv.at[slot])
        quad[slot * OWN : (slot + 1) * OWN, :] = part + quad_sib[slot]
        if slot:
            to = (-slot) % 4
            send(quad_slot(slot), quad_ring.at[to], x_send.at[7], qr_recv.at[to], peer(dx=slot))

    for slot in range(1, 8):
        wait_bytes(loss1.at[0], loss_recv1.at[slot])
    total = loss1[0]
    for k in range(1, 8):
        total = total + loss1[k]
    me2 = y * 4 + z
    loss2[me2] = total
    for slot in range(1, 16):
        dy, dz = COL_OFFS[slot]
        to = COL_OF[neg_col((dy, dz))]
        send(loss2.at[me2], loss2.at[me2], x_send.at[8], loss_recv2.at[to], peer(dy=dy, dz=dz))

    summed = quad[0:OWN, :]
    for d in (1, 3, 2):
        wait_bytes(quad_ring.at[d], qr_recv.at[d])
        summed = summed + quad_ring[d]
    du = INV_TAU * summed
    uu = u_ref[...]
    dz_own[...] = (
        (du - uu * jnp.sum(uu * du, axis=1, keepdims=True)) / norm_ref[...]
    ).astype(BF16)
    send(dz_own, dz_sib, x_send.at[9], dz_recv.at[0], peer(dc=1))

    mine = pl.multiple_of(c * HALF, HALF)
    grad[...] = lax.dot_general(
        feat[:, pl.ds(mine, HALF)], dz_own[...], TN, preferred_element_type=F32
    )
    wait_bytes(feat_sib, feat_recv.at[0])
    wait_bytes(dz_sib, dz_recv.at[0])
    grad[...] += lax.dot_general(feat_sib[...], dz_sib[...], TN, preferred_element_type=F32)

    def ring_block(part, t):
        return pl.ds(pl.multiple_of(part * PART_ROWS + t * RING_ROWS, RING_ROWS), RING_ROWS)

    places = [part_place(name) for name in PARTS]
    for d in (2, 1, 3):
        for p, name in enumerate(PARTS):
            t = places[p][0]
            at = (-d) % 4
            send(
                grad.at[ring_block(p, (t + d) % 4)], g1_in.at[p, at],
                x_send.at[10], g1_recv.at[p, at], ring_peer(name, d),
            )
    for p, name in enumerate(PARTS):
        t, s1, s2 = places[p]
        total = grad[ring_block(p, t), :]
        for d in range(1, 4):
            wait_bytes(g1_in.at[p, d], g1_recv.at[p, d])
            total = total + g1_in[p, d]
        g1[p] = total
        for slot in range(15, 0, -1):
            d1, d2 = COL_OFFS[slot]
            to = COL_OF[neg_col((d1, d2))]
            at = ((s1 + d1) % 4) * 4 + (s2 + d2) % 4
            send(
                g1.at[p, pl.ds(pl.multiple_of(at * TILE, TILE), TILE)],
                g2_in.at[p, pl.ds(to * TILE, TILE)],
                x_send.at[11], g2_recv.at[p], plane_peer(name, d1, d2),
            )
    base = c * HALF
    for p, name in enumerate(PARTS):
        t, s1, s2 = places[p]
        total = g1[p, pl.ds(pl.multiple_of((s1 * 4 + s2) * TILE, TILE), TILE), :]
        wait_bytes(g2_in.at[p, pl.ds(TILE, 15 * TILE)], g2_recv.at[p])
        for slot in range(1, 16):
            total = total + g2_in[p, slot * TILE : (slot + 1) * TILE, :]
        at = pl.ds(
            pl.multiple_of(base + p * PART_ROWS + t * RING_ROWS + (s1 * 4 + s2) * TILE, TILE), TILE
        )
        out[at, :] = total * (1.0 / VIEWS**0.5)
        for slot in range(15, 0, -1):
            d1, d2 = COL_OFFS[slot]
            send(out.at[at], out.at[at], x_send.at[12], ag_recv.at[p], plane_peer(name, d1, d2))

    def out_block(p, t, first=base):
        return out.at[
            pl.ds(pl.multiple_of(first + p * PART_ROWS + t * RING_ROWS, RING_ROWS), RING_ROWS)
        ]

    for p, name in enumerate(PARTS):
        t = places[p][0]
        wait_bytes(out.at[pl.ds(0, 15 * TILE)], ag_recv.at[p])
        block = out_block(p, t)
        for d in (2, 1, 3):
            at = (-d) % 4
            send(block, block, x_send.at[13], ring_recv.at[p, at], ring_peer(name, d))
        send(block, block, x_send.at[14], rel_recv.at[p, 0], peer(dc=1))
    for d in (1, 3, 2):
        for p, name in enumerate(PARTS):
            t = places[p][0]
            block = out_block(p, (t + d) % 4)
            wait_bytes(block, ring_recv.at[p, d])
            send(block, block, x_send.at[14], rel_recv.at[p, d], peer(dc=1))
    half = out.at[pl.ds(pl.multiple_of(base, HALF), HALF)]
    store1 = pltpu.make_async_copy(
        half, g_ref.at[pl.ds(pl.multiple_of(base, HALF), HALF)], store_sem.at[0]
    )
    store1.start()

    for slot in range(1, 16):
        wait_bytes(loss2.at[0], loss_recv2.at[slot])
    total = loss2[0]
    for k in range(1, 16):
        total = total + loss2[k]
    loss_ref[...] = total[0:1, 0:1] * (1.0 / VIEWS)

    for d in (0, 1, 3, 2):
        for p in range(len(PARTS)):
            wait_bytes(out.at[pl.ds(0, RING_ROWS)], rel_recv.at[p, d])
    other = pl.multiple_of((1 - c) * HALF, HALF)
    store2 = pltpu.make_async_copy(
        out.at[pl.ds(other, HALF)], g_ref.at[pl.ds(other, HALF)], store_sem.at[1]
    )
    store2.start()

    for ref, at in sent:
        wait_bytes(ref, x_send.at[at])
    store1.wait()
    store2.wait()


def per_device(features, proj_weight, partner):
    dma = pltpu.SemaphoreType.DMA
    grad, loss = pl.pallas_call(
        kernel,
        out_shape=(
            jax.ShapeDtypeStruct((D, PROJ), F32),
            jax.ShapeDtypeStruct((1, 1), F32),
        ),
        in_specs=[
            pl.BlockSpec(memory_space=pl.ANY),
            pl.BlockSpec(memory_space=pl.ANY),
            pl.BlockSpec(memory_space=pltpu.VMEM),
        ],
        out_specs=(pl.BlockSpec(memory_space=pl.ANY), pl.BlockSpec(memory_space=pltpu.VMEM)),
        scratch_shapes=[
            pltpu.VMEM((OWN, D), BF16),
            pltpu.VMEM((D, PROJ), BF16),
            pltpu.VMEM((OWN, HALF), BF16),
            pltpu.VMEM((OWN, PROJ), F32),
            pltpu.VMEM((OWN, PROJ), F32),
            pltpu.VMEM((8 * SLOT, PROJ), BF16),
            pltpu.VMEM((16 * OWN, PROJ), BF16),
            pltpu.VMEM((8 * OWN, 16 * OWN), BF16),
            pltpu.VMEM((8 * OWN, PROJ), F32),
            pltpu.VMEM((8, OWN), F32),
            pltpu.VMEM((8, 8, OWN), F32),
            pltpu.VMEM((8, OWN), F32),
            pltpu.VMEM((16, 8, OWN), F32),
            pltpu.VMEM((OWN, 16 * PROJ), BF16),
            pltpu.VMEM((8 * OWN, PROJ), F32),
            pltpu.VMEM((16 * OWN, 2 * PROJ), BF16),
            pltpu.VMEM((8 * OWN, PROJ), F32),
            pltpu.VMEM((4, OWN, PROJ), F32),
            pltpu.VMEM((4, OWN, PROJ), F32),
            pltpu.VMEM((OWN, PROJ), BF16),
            pltpu.VMEM((OWN, PROJ), BF16),
            pltpu.VMEM((HALF, PROJ), F32),
            pltpu.VMEM((4, 4, RING_ROWS, PROJ), F32),
            pltpu.VMEM((4, RING_ROWS, PROJ), F32),
            pltpu.VMEM((4, RING_ROWS, PROJ), F32),
            pltpu.VMEM((D, PROJ), F32),
            pltpu.VMEM((8, 8, PROJ), F32),
            pltpu.VMEM((16, 8, PROJ), F32),
            dma((8,)),
            dma((15,)),
            dma((16, 2)),
            dma((8,)),
            dma((1,)),
            dma((8,)),
            dma((16,)),
            dma((8,)),
            dma((16,)),
            dma((4,)),
            dma((4,)),
            dma((1,)),
            dma((4, 4)),
            dma((4,)),
            dma((4,)),
            dma((4, 4)),
            dma((4, 4)),
            dma((2,)),
        ],
        compiler_params=pltpu.CompilerParams(
            collective_id=0, has_side_effects=True, vmem_limit_bytes=56 * 2**20
        ),
        name="simclr_head",
    )(features, proj_weight, partner.reshape(2, PROJ))
    return loss.reshape(()), grad


def solution(mesh):
    placed = (P(("dp", "inner"), None), P(), P(("dp", "inner")))
    return jax.shard_map(
        per_device, mesh=mesh, in_specs=placed, out_specs=(P(), P()), check_vma=False
    )
```

```python
import jax
import jax.numpy as jnp
from jax import lax
from jax.experimental import pallas as pl
from jax.experimental.pallas import tpu as pltpu
from jax.sharding import PartitionSpec as P

MESH = pl.DeviceIdType.MESH
F32 = jnp.float32
BF16 = jnp.bfloat16
VIEWS = 32768
D = 4096
HALF = D // 2
QUARTER = D // 4
PROJ = 128
OWN = 256
GROUP = 4 * OWN
SLOT = OWN + 16
INV_TAU = 5.0
SCALE2 = INV_TAU * 1.4426950408889634
NT = (((1,), (1,)), ((), ()))
TN = (((0,), (0,)), ((), ()))

ROW_OFFS = [(dx, dc) for dc in range(2) for dx in range(4)]
ROW_OF = {off: slot for slot, off in enumerate(ROW_OFFS)}
COL_OFFS = sorted(
    [(dy, dz) for dy in range(4) for dz in range(4)],
    key=lambda o: (min(o[0], 4 - o[0]) + min(o[1], 4 - o[1]), o),
)
COL_OF = {off: slot for slot, off in enumerate(COL_OFFS)}
RING_AXIS = {slot: int(off[0] == 0) for slot, off in enumerate(COL_OFFS) if slot and 0 in off}
TILES = (16, 8, 8)
STARTS = (0, 1024, 1536)


def neg_col(off):
    return ((-off[0]) % 4, (-off[1]) % 4)


def neg_row(off):
    return ((-off[0]) % 4, off[1])


def coords():
    dp, inner = lax.axis_index("dp"), lax.axis_index("inner")
    x = (inner % 2) * 2 + dp // 8
    return x, (dp // 2) % 4, inner // 2, dp % 2


def device_at(x, y, z, c):
    return ((x % 2) * 8 + y * 2 + c, z * 2 + x // 2)


class Torus:
    def __init__(self):
        x, y, z, c = coords()
        self.xs, self.ys, self.zs = ([(v + d) % 4 for d in range(4)] for v in (x, y, z))
        self.cs = [c, 1 - c]
        self.x_dp = [v % 2 * 8 for v in self.xs]
        self.x_inner = [v // 2 for v in self.xs]
        self.y_dp = [v * 2 for v in self.ys]
        self.z_inner = [v * 2 for v in self.zs]

    def peer(self, dx=0, dy=0, dz=0, dc=0):
        return (
            self.x_dp[dx] + self.y_dp[dy] + self.cs[dc],
            self.z_inner[dz] + self.x_inner[dx],
        )

    def pick(self, a, b):
        return a * self.cs[1] + b * self.cs[0]

    def pick_peer(self, a, b):
        return self.pick(a[0], b[0]), self.pick(a[1], b[1])

    def ring_at(self, part, d):
        if part == 2:
            return self.zs[d]
        ends = (self.xs[d], self.ys[d])
        return self.pick(*(ends if part == 0 else ends[::-1]))

    def plane_at(self, part, d1, d2):
        if part == 2:
            return self.xs[d1] * 4 + self.ys[d2]
        ends = (self.ys[d1], self.xs[d1])
        return self.pick(*(ends if part == 0 else ends[::-1])) * 4 + self.zs[d2]

    def ring_peer(self, part, d):
        if part == 2:
            return self.peer(dz=d)
        ends = (self.peer(dx=d), self.peer(dy=d))
        return self.pick_peer(*(ends if part == 0 else ends[::-1]))

    def plane_peer(self, part, d1, d2):
        if part == 2:
            return self.peer(dx=d1, dy=d2)
        ends = (self.peer(dy=d1, dz=d2), self.peer(dx=d1, dz=d2))
        return self.pick_peer(*(ends if part == 0 else ends[::-1]))


def ring_peers():
    offs = [off for d in (1, 3, 2) for off in ((d, 0, 0, 0), (0, d, 0, 0), (0, 0, d, 0))]
    return offs + [(0, 0, 0, 1)]


def send(src, dst, send_sem, recv_sem, device):
    copy = pltpu.make_async_remote_copy(
        src_ref=src, dst_ref=dst, send_sem=send_sem, recv_sem=recv_sem,
        device_id=device, device_id_type=MESH,
    )
    copy.start()


def wait_bytes(ref, sem):
    pltpu.make_async_copy(ref, ref, sem).wait()


def kernel(
    f_hbm, w_hbm, partner_ref, g_ref, loss_ref,
    feat, weight, feat_sib, u_ref, norm_ref, rows, cols, expo, acc,
    sums, sums_in, wts, wts_in, wide, paired, uw, quad, quad_sib, quad_ring,
    dz_own, dz_sib, grad, g1_in_a, g1_in_b, g1_in_c, g1_a, g1_b, g1_c,
    g2_in_a, g2_in_b, g2_in_c, out, loss1, loss2,
    load_sem, x_send, col_recv, row_recv, feat_recv, sum_recv, wt_recv, loss_recv1, loss_recv2,
    qs_recv, qr_recv, dz_recv, g1_recv, g2_recv, ag_recv, ring_recv, rel_recv, store_sem,
):
    sent = [
        (rows.at[pl.ds(0, 7 * SLOT)], 0),
        (cols.at[pl.ds(0, 15 * OWN)], 1),
        (feat_sib, 2),
        (sums_in.at[pl.ds(0, 7)], 3),
        (wts_in.at[pl.ds(0, 15)], 4),
        (loss1.at[pl.ds(0, 7)], 5),
        (quad_sib, 6),
        (quad_ring.at[pl.ds(0, 3)], 7),
        (loss2.at[pl.ds(0, 15)], 8),
        (dz_sib, 9),
        (grad.at[pl.ds(0, 3 * HALF // 4)], 10),
        (grad.at[pl.ds(0, 15 * sum(TILES))], 11),
        (grad.at[pl.ds(0, 15 * sum(TILES))], 12),
        (grad.at[pl.ds(0, 3 * HALF // 4)], 13),
        (grad, 14),
    ]
    torus = Torus()
    peer = torus.peer
    x, y, z, c = torus.xs[0], torus.ys[0], torus.zs[0], torus.cs[0]
    loads = []
    for k in range(4):
        depth = pl.ds(k * QUARTER, QUARTER)
        loads.append(
            (
                pltpu.make_async_copy(w_hbm.at[depth], weight.at[depth], load_sem.at[k]),
                pltpu.make_async_copy(f_hbm.at[:, depth], feat.at[:, depth], load_sem.at[4 + k]),
            )
        )
    for pair in loads:
        for load in pair:
            load.start()
    barrier = pltpu.get_barrier_semaphore()
    peers = ring_peers()
    for off in peers:
        pl.semaphore_signal(barrier, inc=1, device_id=peer(*off), device_id_type=MESH)

    owner_of, place_of = partner_ref[...] // OWN, partner_ref[...] % OWN
    at = lax.broadcasted_iota(jnp.int32, (16, PROJ), 0)
    code = jnp.zeros((16, PROJ), F32)
    for k, row in enumerate((owner_of[0:1], owner_of[1:2], place_of[0:1], place_of[1:2])):
        code = jnp.where(at == k, row.astype(F32), code)
    rows[OWN:SLOT, :] = code.astype(BF16)

    zed = None
    for k, pair in enumerate(loads):
        for load in pair:
            load.wait()
        term = jnp.dot(
            feat[:, k * QUARTER : (k + 1) * QUARTER], weight[k * QUARTER : (k + 1) * QUARTER, :],
            preferred_element_type=F32,
        )
        zed = term if zed is None else zed + term
    norm = jnp.sqrt(jnp.sum(zed * zed, axis=1, keepdims=True) + 1e-06)
    u = zed / norm
    u_ref[...] = u
    norm_ref[...] = jnp.broadcast_to(norm, (OWN, PROJ))
    ub = u.astype(BF16)
    rows[0:OWN, :] = ub
    cols[0:OWN, :] = ub
    pl.semaphore_wait(barrier, len(peers))

    def row_slot(slot):
        return rows.at[pl.ds(slot * SLOT, SLOT)]

    def col_slot(slot):
        return cols.at[pl.ds(slot * OWN, OWN)]

    def col_half(slot, half):
        return cols.at[pl.ds(slot * OWN + half * (OWN // 2), OWN // 2)]

    for dx in (1, 3, 2):
        to = ROW_OF[neg_row((dx, 0))]
        send(row_slot(0), row_slot(to), x_send.at[0], row_recv.at[to], peer(dx=dx))
    send(row_slot(0), row_slot(4), x_send.at[0], row_recv.at[4], peer(dc=1))
    for turn in range(2):
        for d in (1, 3, 2):
            for axis in range(2):
                half = axis ^ turn
                off = (d, 0) if axis == 0 else (0, d)
                to = COL_OF[neg_col(off)]
                send(
                    col_half(0, half), col_half(to, half), x_send.at[1],
                    col_recv.at[to, half], peer(dy=off[0], dz=off[1]),
                )

    def pass_on(axis, d):
        off = (d, 0) if axis == 0 else (0, d)
        slot = COL_OF[off]
        wait_bytes(col_half(slot, axis), col_recv.at[slot, axis])
        for e in (1, 3, 2):
            hop = (0, e) if axis == 0 else (e, 0)
            to = COL_OF[((off[0] - hop[0]) % 4, (off[1] - hop[1]) % 4)]
            send(
                col_half(slot, axis), col_half(to, axis), x_send.at[1],
                col_recv.at[to, axis], peer(dy=hop[0], dz=hop[1]),
            )

    def pass_row(slot):
        wait_bytes(row_slot(slot), row_recv.at[slot])
        send(row_slot(slot), row_slot(4 + slot), x_send.at[0], row_recv.at[4 + slot], peer(dc=1))

    for d in (1, 3, 2):
        pass_on(0, d)
        pass_on(1, d)
        pass_row(d)
    send(
        feat.at[:, pl.ds(pl.multiple_of((1 - c) * HALF, HALF), HALF)], feat_sib,
        x_send.at[2], feat_recv.at[0], peer(dc=1),
    )

    def lanes(e):
        total = e[:, 0:PROJ]
        for q in range(1, e.shape[1] // PROJ):
            total = total + e[:, q * PROJ : (q + 1) * PROJ]
        return total

    def scores(slot, first):
        return jnp.exp2(
            lax.dot_general(
                rows[slot * SLOT : slot * SLOT + OWN, :], cols[pl.ds(first, GROUP), :], NT,
                preferred_element_type=F32,
            )
            * SCALE2
        )

    for slot in range(1, 4):
        wait_bytes(col_half(slot, 1 - RING_AXIS[slot]), col_recv.at[slot, 1 - RING_AXIS[slot]])
    for slot in (0, 4, 1, 3, 2, 5, 7, 6):
        if slot > 3:
            wait_bytes(row_slot(slot), row_recv.at[slot])
        e = scores(slot, 0)
        if slot == 0:
            at_row = lax.broadcasted_iota(jnp.int32, (OWN, GROUP), 0)
            at_col = lax.broadcasted_iota(jnp.int32, (OWN, GROUP), 1)
            e = jnp.where(at_row == at_col, 0.0, e)
        expo[slot * OWN : (slot + 1) * OWN, 0:GROUP] = e.astype(BF16)
        acc[slot * OWN : (slot + 1) * OWN, :] = lanes(e)

    for group in range(1, 4):
        for slot in range(4 * group, 4 * group + 4):
            for half in range(2):
                if slot not in RING_AXIS or half != RING_AXIS[slot]:
                    wait_bytes(col_half(slot, half), col_recv.at[slot, half])
        for slot in range(8):
            e = scores(slot, group * GROUP)
            expo[slot * OWN : (slot + 1) * OWN, group * GROUP : (group + 1) * GROUP] = e.astype(BF16)
            acc[slot * OWN : (slot + 1) * OWN, :] += lanes(e)

    eye = lax.broadcasted_iota(jnp.int32, (PROJ, PROJ), 0) == lax.broadcasted_iota(
        jnp.int32, (PROJ, PROJ), 1
    )

    def to_row(column):
        return jnp.sum(jnp.where(eye, column, 0.0), axis=0, keepdims=True)

    def to_column(row):
        halves = [
            jnp.sum(jnp.where(eye, row[:, h * PROJ : (h + 1) * PROJ], 0.0), axis=1, keepdims=True)
            for h in range(2)
        ]
        return jnp.broadcast_to(jnp.concatenate(halves, axis=0), (OWN, PROJ))

    for slot in range(8):
        for h in range(2):
            first = slot * OWN + h * PROJ
            column = jnp.sum(acc[first : first + PROJ, :], axis=1, keepdims=True)
            sums[slot : slot + 1, h * PROJ : (h + 1) * PROJ] = to_row(column)
    for slot in (2, 6, 1, 3, 5, 7, 4):
        dx, dc = ROW_OFFS[slot]
        to = ROW_OF[neg_row((dx, dc))]
        send(sums, sums_in.at[to], x_send.at[3], sum_recv.at[to], peer(dx=dx, dc=dc))

    for slot in range(16):
        wide[:, slot * PROJ : (slot + 1) * PROJ] = cols[slot * OWN : (slot + 1) * OWN, :]
    lane = lax.broadcasted_iota(jnp.int32, (OWN, PROJ), 1).astype(F32)

    def partners(slot, pos):
        code = rows[slot * SLOT + OWN : (slot + 1) * SLOT, :].astype(F32)
        owner = to_column(jnp.concatenate([code[0:1], code[1:2]], axis=1))
        place = to_column(jnp.concatenate([code[2:3], code[3:4]], axis=1))
        hot = jnp.concatenate(
            [jnp.where(place == lane, 1.0, 0.0), jnp.where(place == lane + PROJ, 1.0, 0.0)], axis=1
        ).astype(BF16)
        found = jnp.dot(hot, wide[...], preferred_element_type=F32)
        total = jnp.zeros((OWN, PROJ), F32)
        for k in range(16):
            dy, dz = COL_OFFS[k]
            dp, inner = peer(dy=dy, dz=dz)
            here = (dp * 8 + inner).astype(F32)
            total = total + jnp.where(owner == here, found[:, k * PROJ : (k + 1) * PROJ], 0.0)
        paired[slot * OWN : (slot + 1) * OWN, :] = total
        own = rows[slot * SLOT : slot * SLOT + OWN, :].astype(F32)
        return pos + own * total

    pos = jnp.zeros((OWN, PROJ), F32)
    for slot in range(4):
        pos = partners(slot, pos)

    for slot in range(1, 8):
        wait_bytes(sums_in.at[slot], sum_recv.at[slot])
    for slot in range(8):
        dx, dc = ROW_OFFS[slot]
        total = sums[slot : slot + 1, :]
        for sender in range(1, 8):
            ox, oc = ROW_OFFS[sender]
            at = ROW_OF[((dx - ox) % 4, (dc - oc) % 2)]
            total = total + sums_in[sender, at : at + 1, :]
        wts[slot : slot + 1, :] = 1.0 / total
        if slot == 0:
            log_sum = jnp.sum(jnp.log(total))
    for slot in range(1, 16):
        dy, dz = COL_OFFS[slot]
        to = COL_OF[neg_col((dy, dz))]
        send(wts, wts_in.at[to], x_send.at[4], wt_recv.at[to], peer(dy=dy, dz=dz))

    for slot in range(4, 8):
        pos = partners(slot, pos)
    loss_part = log_sum - INV_TAU * jnp.sum(pos)
    me1 = x * 2 + c
    loss1[me1] = jnp.full((8, PROJ), loss_part, F32)
    for slot in range(1, 8):
        dx, dc = ROW_OFFS[slot]
        to = ROW_OF[neg_row((dx, dc))]
        send(loss1.at[me1], loss1.at[me1], x_send.at[5], loss_recv1.at[to], peer(dx=dx, dc=dc))

    def weigh(slot, row):
        block = cols[slot * OWN : (slot + 1) * OWN, :]
        uw[slot * OWN : (slot + 1) * OWN, 0:PROJ] = block
        uw[slot * OWN : (slot + 1) * OWN, PROJ : 2 * PROJ] = (
            block.astype(F32) * to_column(row)
        ).astype(BF16)

    weigh(0, wts[0:1, :])
    for slot in range(1, 16):
        wait_bytes(wts_in.at[slot], wt_recv.at[slot])
        weigh(slot, wts_in[slot, 0:1, :])

    def terms(slot):
        both = jnp.dot(
            expo[slot * OWN : (slot + 1) * OWN, :], uw[...], preferred_element_type=F32
        )
        w = to_column(wts[slot : slot + 1, :])
        return (
            w * both[:, 0:PROJ] + both[:, PROJ : 2 * PROJ]
            - 2.0 * paired[slot * OWN : (slot + 1) * OWN, :]
        )

    def quad_slot(slot):
        return quad.at[pl.ds(slot * OWN, OWN)]

    for slot in (6, 5, 2, 7, 1, 4, 3, 0):
        part = terms(slot)
        if slot > 3:
            quad[slot * OWN : (slot + 1) * OWN, :] = part
            send(
                quad_slot(slot), quad_sib.at[slot - 4], x_send.at[6], qs_recv.at[slot - 4],
                peer(dc=1),
            )
            continue
        wait_bytes(quad_sib.at[slot], qs_recv.at[slot])
        quad[slot * OWN : (slot + 1) * OWN, :] = part + quad_sib[slot]
        if slot:
            to = (-slot) % 4
            send(quad_slot(slot), quad_ring.at[to], x_send.at[7], qr_recv.at[to], peer(dx=slot))

    summed = quad[0:OWN, :]
    for d in (1, 3, 2):
        wait_bytes(quad_ring.at[d], qr_recv.at[d])
        summed = summed + quad_ring[d]
    du = INV_TAU * summed
    uu = u_ref[...]
    dz_own[...] = (
        (du - uu * jnp.sum(uu * du, axis=1, keepdims=True)) / norm_ref[...]
    ).astype(BF16)
    send(dz_own, dz_sib, x_send.at[9], dz_recv.at[0], peer(dc=1))

    mine = pl.multiple_of(c * HALF, HALF)
    grad[...] = lax.dot_general(
        feat[:, pl.ds(mine, HALF)], dz_own[...], TN, preferred_element_type=F32
    )
    wait_bytes(feat_sib, feat_recv.at[0])
    wait_bytes(dz_sib, dz_recv.at[0])
    grad[...] += lax.dot_general(feat_sib[...], dz_sib[...], TN, preferred_element_type=F32)

    g1_in, g1, g2_in = (g1_in_a, g1_in_b, g1_in_c), (g1_a, g1_b, g1_c), (g2_in_a, g2_in_b, g2_in_c)
    parts = (2, 1, 0)

    def ring_block(part, d, base=0):
        span = 16 * TILES[part]
        first = base + STARTS[part] + torus.ring_at(part, d) * span
        return pl.ds(pl.multiple_of(first, span), span)

    for d in (2, 1, 3):
        for part in parts:
            at = (-d) % 4
            send(
                grad.at[ring_block(part, d)], g1_in[part].at[at],
                x_send.at[10], g1_recv.at[part, at], torus.ring_peer(part, d),
            )

    for slot in range(1, 8):
        wait_bytes(loss1.at[0], loss_recv1.at[slot])
    total = loss1[0]
    for k in range(1, 8):
        total = total + loss1[k]
    me2 = y * 4 + z
    loss2[me2] = total
    for slot in range(1, 16):
        dy, dz = COL_OFFS[slot]
        to = COL_OF[neg_col((dy, dz))]
        send(loss2.at[me2], loss2.at[me2], x_send.at[8], loss_recv2.at[to], peer(dy=dy, dz=dz))

    for part in parts:
        total = grad[ring_block(part, 0), :]
        for d in (1, 3, 2):
            wait_bytes(g1_in[part].at[d], g1_recv.at[part, d])
            total = total + g1_in[part][d]
        g1[part][...] = total
        tile = TILES[part]
        for slot in range(15, 0, -1):
            d1, d2 = COL_OFFS[slot]
            to = COL_OF[neg_col((d1, d2))]
            at = pl.multiple_of(torus.plane_at(part, d1, d2) * tile, tile)
            send(
                g1[part].at[pl.ds(at, tile)], g2_in[part].at[pl.ds(to * tile, tile)],
                x_send.at[11], g2_recv.at[part], torus.plane_peer(part, d1, d2),
            )
    base = c * HALF
    for part in parts:
        tile = TILES[part]
        place = torus.plane_at(part, 0, 0) * tile
        total = g1[part][pl.ds(pl.multiple_of(place, tile), tile), :]
        wait_bytes(g2_in[part].at[pl.ds(tile, 15 * tile)], g2_recv.at[part])
        for slot in range(1, 16):
            total = total + g2_in[part][slot * tile : (slot + 1) * tile, :]
        first = base + STARTS[part] + torus.ring_at(part, 0) * 16 * tile + place
        at = pl.ds(pl.multiple_of(first, tile), tile)
        out[at, :] = total * (1.0 / VIEWS**0.5)
        for slot in range(15, 0, -1):
            d1, d2 = COL_OFFS[slot]
            send(
                out.at[at], out.at[at], x_send.at[12], ag_recv.at[part],
                torus.plane_peer(part, d1, d2),
            )

    def store(rows_of):
        pltpu.make_async_copy(out.at[rows_of], g_ref.at[rows_of], store_sem.at[0]).start()

    for part in parts:
        wait_bytes(out.at[pl.ds(0, 15 * TILES[part])], ag_recv.at[part])
        block = ring_block(part, 0, base)
        for d in (2, 1, 3):
            at = (-d) % 4
            send(
                out.at[block], out.at[block], x_send.at[13], ring_recv.at[part, at],
                torus.ring_peer(part, d),
            )
        send(out.at[block], out.at[block], x_send.at[14], rel_recv.at[part, 0], peer(dc=1))
        store(block)
    for d in (1, 3, 2):
        for part in parts:
            block = ring_block(part, d, base)
            wait_bytes(out.at[block], ring_recv.at[part, d])
            send(out.at[block], out.at[block], x_send.at[14], rel_recv.at[part, d], peer(dc=1))
            store(block)

    for slot in range(1, 16):
        wait_bytes(loss2.at[0], loss_recv2.at[slot])
    total = loss2[0]
    for k in range(1, 16):
        total = total + loss2[k]
    loss_ref[...] = total[0:1, 0:1] * (1.0 / VIEWS)

    other = torus.cs[1] * HALF
    for d in (0, 1, 3, 2):
        for part in parts:
            span = 16 * TILES[part]
            ends = (torus.ys[d], torus.xs[d])
            ring = torus.zs[d] if part == 2 else torus.pick(*(ends if part == 0 else ends[::-1]))
            block = pl.ds(pl.multiple_of(other + STARTS[part] + ring * span, span), span)
            wait_bytes(out.at[block], rel_recv.at[part, d])
            store(block)

    for ref, at in sent:
        wait_bytes(ref, x_send.at[at])
    wait_bytes(out, store_sem.at[0])


def per_device(features, proj_weight, partner):
    dma = pltpu.SemaphoreType.DMA
    grad, loss = pl.pallas_call(
        kernel,
        out_shape=(
            pltpu.VMEM((D, PROJ), F32),
            jax.ShapeDtypeStruct((1, 1), F32),
        ),
        in_specs=[
            pl.BlockSpec(memory_space=pl.ANY),
            pl.BlockSpec(memory_space=pl.ANY),
            pl.BlockSpec(memory_space=pltpu.VMEM),
        ],
        out_specs=(pl.BlockSpec(memory_space=pltpu.VMEM), pl.BlockSpec(memory_space=pltpu.VMEM)),
        scratch_shapes=[
            pltpu.VMEM((OWN, D), BF16),
            pltpu.VMEM((D, PROJ), BF16),
            pltpu.VMEM((OWN, HALF), BF16),
            pltpu.VMEM((OWN, PROJ), F32),
            pltpu.VMEM((OWN, PROJ), F32),
            pltpu.VMEM((8 * SLOT, PROJ), BF16),
            pltpu.VMEM((16 * OWN, PROJ), BF16),
            pltpu.VMEM((8 * OWN, 16 * OWN), BF16),
            pltpu.VMEM((8 * OWN, PROJ), F32),
            pltpu.VMEM((8, OWN), F32),
            pltpu.VMEM((8, 8, OWN), F32),
            pltpu.VMEM((8, OWN), F32),
            pltpu.VMEM((16, 8, OWN), F32),
            pltpu.VMEM((OWN, 16 * PROJ), BF16),
            pltpu.VMEM((8 * OWN, PROJ), F32),
            pltpu.VMEM((16 * OWN, 2 * PROJ), BF16),
            pltpu.VMEM((8 * OWN, PROJ), F32),
            pltpu.VMEM((4, OWN, PROJ), F32),
            pltpu.VMEM((4, OWN, PROJ), F32),
            pltpu.VMEM((OWN, PROJ), BF16),
            pltpu.VMEM((OWN, PROJ), BF16),
            pltpu.VMEM((HALF, PROJ), F32),
            *[pltpu.VMEM((4, 16 * tile, PROJ), F32) for tile in TILES],
            *[pltpu.VMEM((16 * tile, PROJ), F32) for tile in TILES],
            *[pltpu.VMEM((16 * tile, PROJ), F32) for tile in TILES],
            pltpu.VMEM((D, PROJ), F32),
            pltpu.VMEM((8, 8, PROJ), F32),
            pltpu.VMEM((16, 8, PROJ), F32),
            dma((8,)),
            dma((15,)),
            dma((16, 2)),
            dma((8,)),
            dma((1,)),
            dma((8,)),
            dma((16,)),
            dma((8,)),
            dma((16,)),
            dma((4,)),
            dma((4,)),
            dma((1,)),
            dma((3, 4)),
            dma((3,)),
            dma((3,)),
            dma((3, 4)),
            dma((3, 4)),
            dma((1,)),
        ],
        compiler_params=pltpu.CompilerParams(
            collective_id=0, has_side_effects=True, vmem_limit_bytes=56 * 2**20
        ),
        name="simclr_head",
    )(features, proj_weight, partner.reshape(2, PROJ))
    return loss.reshape(()), grad


def solution(mesh):
    placed = (P(("dp", "inner"), None), P(), P(("dp", "inner")))
    return jax.shard_map(
        per_device, mesh=mesh, in_specs=placed, out_specs=(P(), P()), check_vma=False
    )
```

```python
import jax
import jax.numpy as jnp
from jax import lax
from jax.experimental import pallas as pl
from jax.experimental.pallas import tpu as pltpu
from jax.sharding import PartitionSpec as P

MESH = pl.DeviceIdType.MESH
F32 = jnp.float32
BF16 = jnp.bfloat16
VIEWS = 32768
D = 4096
HALF = D // 2
QUARTER = D // 4
PROJ = 128
OWN = 256
GROUPS = ((0, 4), (4, 8), (8, 12), (12, 14), (14, 16))
SLOT = OWN + 16
INV_TAU = 5.0
SCALE2 = INV_TAU * 1.4426950408889634
NT = (((1,), (1,)), ((), ()))
TN = (((0,), (0,)), ((), ()))

ROW_OFFS = [(dx, dc) for dc in range(2) for dx in range(4)]
ROW_OF = {off: slot for slot, off in enumerate(ROW_OFFS)}
COL_OFFS = sorted(
    [(dy, dz) for dy in range(4) for dz in range(4)],
    key=lambda o: (0 not in o, min(o[0], 4 - o[0]) + min(o[1], 4 - o[1]), o),
)
COL_OF = {off: slot for slot, off in enumerate(COL_OFFS)}
RING_AXIS = {slot: int(off[0] == 0) for slot, off in enumerate(COL_OFFS) if slot and 0 in off}
TILES = (16, 8, 8)
STARTS = (0, 1024, 1536)


def neg_col(off):
    return ((-off[0]) % 4, (-off[1]) % 4)


def neg_row(off):
    return ((-off[0]) % 4, off[1])


def coords():
    dp, inner = lax.axis_index("dp"), lax.axis_index("inner")
    x = (inner % 2) * 2 + dp // 8
    return x, (dp // 2) % 4, inner // 2, dp % 2


def device_at(x, y, z, c):
    return ((x % 2) * 8 + y * 2 + c, z * 2 + x // 2)


class Torus:
    def __init__(self):
        x, y, z, c = coords()
        self.xs, self.ys, self.zs = ([(v + d) % 4 for d in range(4)] for v in (x, y, z))
        self.cs = [c, 1 - c]
        self.x_dp = [v % 2 * 8 for v in self.xs]
        self.x_inner = [v // 2 for v in self.xs]
        self.y_dp = [v * 2 for v in self.ys]
        self.z_inner = [v * 2 for v in self.zs]

    def peer(self, dx=0, dy=0, dz=0, dc=0):
        return (
            self.x_dp[dx] + self.y_dp[dy] + self.cs[dc],
            self.z_inner[dz] + self.x_inner[dx],
        )

    def pick(self, a, b):
        return a * self.cs[1] + b * self.cs[0]

    def pick_peer(self, a, b):
        return self.pick(a[0], b[0]), self.pick(a[1], b[1])

    def ring_at(self, part, d):
        if part == 2:
            return self.zs[d]
        ends = (self.xs[d], self.ys[d])
        return self.pick(*(ends if part == 0 else ends[::-1]))

    def plane_at(self, part, d1, d2):
        if part == 2:
            return self.xs[d1] * 4 + self.ys[d2]
        ends = (self.ys[d1], self.xs[d1])
        return self.pick(*(ends if part == 0 else ends[::-1])) * 4 + self.zs[d2]

    def ring_peer(self, part, d):
        if part == 2:
            return self.peer(dz=d)
        ends = (self.peer(dx=d), self.peer(dy=d))
        return self.pick_peer(*(ends if part == 0 else ends[::-1]))

    def plane_peer(self, part, d1, d2):
        if part == 2:
            return self.peer(dx=d1, dy=d2)
        ends = (self.peer(dy=d1, dz=d2), self.peer(dx=d1, dz=d2))
        return self.pick_peer(*(ends if part == 0 else ends[::-1]))


def ring_peers():
    offs = [off for d in (2, 1, 3) for off in ((d, 0, 0, 0), (0, d, 0, 0), (0, 0, d, 0))]
    return offs + [(0, 0, 0, 1)]


def send(src, dst, send_sem, recv_sem, device):
    copy = pltpu.make_async_remote_copy(
        src_ref=src, dst_ref=dst, send_sem=send_sem, recv_sem=recv_sem,
        device_id=device, device_id_type=MESH,
    )
    copy.start()


def wait_bytes(ref, sem):
    pltpu.make_async_copy(ref, ref, sem).wait()


def kernel(
    f_hbm, w_hbm, partner_hbm, out, loss_ref,
    partner_ref, feat, weight, feat_sib, u_ref, norm_ref, rows, cols, expo, acc,
    sums, sums_in, wts, wts_in, wide, paired, uw, quad, quad_sib, quad_ring,
    dz_own, dz_sib, grad, g1_in_a, g1_in_b, g1_in_c, g1_a, g1_b, g1_c,
    g2_in_a, g2_in_b, g2_in_c, loss1, loss2,
    load_sem, x_send, col_recv, row_recv, feat_recv, sum_recv, wt_recv, loss_recv1, loss_recv2,
    qs_recv, qr_recv, dz_recv, g1_recv, g2_recv, ag_recv, ring_recv, rel_recv,
):
    sent = [
        (rows.at[pl.ds(0, 7 * SLOT)], 0),
        (cols.at[pl.ds(0, 15 * OWN)], 1),
        (feat_sib, 2),
        (sums_in.at[pl.ds(0, 7)], 3),
        (wts_in.at[pl.ds(0, 15)], 4),
        (loss1.at[pl.ds(0, 7)], 5),
        (quad_sib, 6),
        (quad_ring.at[pl.ds(0, 3)], 7),
        (loss2.at[pl.ds(0, 15)], 8),
        (dz_sib, 9),
        (grad.at[pl.ds(0, 3 * HALF // 4)], 10),
        (grad.at[pl.ds(0, 15 * sum(TILES))], 11),
        (grad.at[pl.ds(0, 15 * sum(TILES))], 12),
        (grad.at[pl.ds(0, 3 * HALF // 4)], 13),
        (grad, 14),
    ]
    torus = Torus()
    peer = torus.peer
    x, y, z, c = torus.xs[0], torus.ys[0], torus.zs[0], torus.cs[0]
    loads = []
    for k in range(4):
        depth = pl.ds(k * QUARTER, QUARTER)
        loads.append(
            (
                pltpu.make_async_copy(w_hbm.at[depth], weight.at[depth], load_sem.at[k]),
                pltpu.make_async_copy(f_hbm.at[:, depth], feat.at[:, depth], load_sem.at[4 + k]),
            )
        )
    load_partner = pltpu.make_async_copy(partner_hbm, partner_ref, load_sem.at[8])
    load_partner.start()
    for pair in loads:
        for load in pair:
            load.start()
    barrier = pltpu.get_barrier_semaphore()
    peers = ring_peers()
    for off in peers:
        pl.semaphore_signal(barrier, inc=1, device_id=peer(*off), device_id_type=MESH)

    load_partner.wait()
    owner_of, place_of = partner_ref[...] // OWN, partner_ref[...] % OWN
    at = lax.broadcasted_iota(jnp.int32, (16, PROJ), 0)
    code = jnp.zeros((16, PROJ), F32)
    for k, row in enumerate((owner_of[0:1], owner_of[1:2], place_of[0:1], place_of[1:2])):
        code = jnp.where(at == k, row.astype(F32), code)
    rows[OWN:SLOT, :] = code.astype(BF16)

    zed = None
    for k, pair in enumerate(loads):
        for load in pair:
            load.wait()
        term = jnp.dot(
            feat[:, k * QUARTER : (k + 1) * QUARTER], weight[k * QUARTER : (k + 1) * QUARTER, :],
            preferred_element_type=F32,
        )
        zed = term if zed is None else zed + term
    norm = jnp.sqrt(jnp.sum(zed * zed, axis=1, keepdims=True) + 1e-06)
    u = zed / norm
    u_ref[...] = u
    norm_ref[...] = jnp.broadcast_to(norm, (OWN, PROJ))
    ub = u.astype(BF16)
    rows[0:OWN, :] = ub
    cols[0:OWN, :] = ub
    pl.semaphore_wait(barrier, len(peers))

    def row_slot(slot):
        return rows.at[pl.ds(slot * SLOT, SLOT)]

    def col_slot(slot):
        return cols.at[pl.ds(slot * OWN, OWN)]

    def col_half(slot, half):
        return cols.at[pl.ds(slot * OWN + half * (OWN // 2), OWN // 2)]

    for dx in (1, 3, 2):
        to = ROW_OF[neg_row((dx, 0))]
        send(row_slot(0), row_slot(to), x_send.at[0], row_recv.at[to], peer(dx=dx))
    send(row_slot(0), row_slot(4), x_send.at[0], row_recv.at[4], peer(dc=1))
    for turn in range(2):
        for d in (1, 3, 2):
            for axis in range(2):
                half = axis ^ turn
                off = (d, 0) if axis == 0 else (0, d)
                to = COL_OF[neg_col(off)]
                send(
                    col_half(0, half), col_half(to, half), x_send.at[1],
                    col_recv.at[to, half], peer(dy=off[0], dz=off[1]),
                )

    def pass_on(axis, d):
        off = (d, 0) if axis == 0 else (0, d)
        slot = COL_OF[off]
        wait_bytes(col_half(slot, axis), col_recv.at[slot, axis])
        for e in (1, 3, 2):
            hop = (0, e) if axis == 0 else (e, 0)
            to = COL_OF[((off[0] - hop[0]) % 4, (off[1] - hop[1]) % 4)]
            send(
                col_half(slot, axis), col_half(to, axis), x_send.at[1],
                col_recv.at[to, axis], peer(dy=hop[0], dz=hop[1]),
            )

    def pass_row(slot):
        wait_bytes(row_slot(slot), row_recv.at[slot])
        send(row_slot(slot), row_slot(4 + slot), x_send.at[0], row_recv.at[4 + slot], peer(dc=1))

    for d in (1, 3, 2):
        pass_on(0, d)
        pass_on(1, d)
        pass_row(d)
    send(
        feat.at[:, pl.ds(pl.multiple_of((1 - c) * HALF, HALF), HALF)], feat_sib,
        x_send.at[2], feat_recv.at[0], peer(dc=1),
    )

    def lanes(e):
        total = e[:, 0:PROJ]
        for q in range(1, e.shape[1] // PROJ):
            total = total + e[:, q * PROJ : (q + 1) * PROJ]
        return total

    def scores(slot, first, end):
        return jnp.exp2(
            lax.dot_general(
                rows[slot * SLOT : slot * SLOT + OWN, :], cols[first * OWN : end * OWN, :], NT,
                preferred_element_type=F32,
            )
            * SCALE2
        )

    for slot in range(1, 4):
        wait_bytes(col_half(slot, 1 - RING_AXIS[slot]), col_recv.at[slot, 1 - RING_AXIS[slot]])
    for slot in (0, 4, 1, 3, 2, 5, 7, 6):
        if slot > 3:
            wait_bytes(row_slot(slot), row_recv.at[slot])
        e = scores(slot, *GROUPS[0])
        if slot == 0:
            at_row = lax.broadcasted_iota(jnp.int32, e.shape, 0)
            at_col = lax.broadcasted_iota(jnp.int32, e.shape, 1)
            e = jnp.where(at_row == at_col, 0.0, e)
        expo[slot * OWN : (slot + 1) * OWN, 0 : GROUPS[0][1] * OWN] = e.astype(BF16)
        acc[slot * OWN : (slot + 1) * OWN, :] = lanes(e)

    for first, end in GROUPS[1:]:
        for slot in range(first, end):
            for half in range(2):
                if slot not in RING_AXIS or half != RING_AXIS[slot]:
                    wait_bytes(col_half(slot, half), col_recv.at[slot, half])
        for slot in range(8):
            e = scores(slot, first, end)
            expo[slot * OWN : (slot + 1) * OWN, first * OWN : end * OWN] = e.astype(BF16)
            acc[slot * OWN : (slot + 1) * OWN, :] += lanes(e)

    eye = lax.broadcasted_iota(jnp.int32, (PROJ, PROJ), 0) == lax.broadcasted_iota(
        jnp.int32, (PROJ, PROJ), 1
    )

    def to_row(column):
        return jnp.sum(jnp.where(eye, column, 0.0), axis=0, keepdims=True)

    def to_column(row):
        halves = [
            jnp.sum(jnp.where(eye, row[:, h * PROJ : (h + 1) * PROJ], 0.0), axis=1, keepdims=True)
            for h in range(2)
        ]
        return jnp.broadcast_to(jnp.concatenate(halves, axis=0), (OWN, PROJ))

    for slot in range(8):
        for h in range(2):
            first = slot * OWN + h * PROJ
            column = jnp.sum(acc[first : first + PROJ, :], axis=1, keepdims=True)
            sums[slot : slot + 1, h * PROJ : (h + 1) * PROJ] = to_row(column)
    for slot in (2, 6, 1, 3, 5, 7, 4):
        dx, dc = ROW_OFFS[slot]
        to = ROW_OF[neg_row((dx, dc))]
        send(sums, sums_in.at[to], x_send.at[3], sum_recv.at[to], peer(dx=dx, dc=dc))

    for slot in range(16):
        wide[:, slot * PROJ : (slot + 1) * PROJ] = cols[slot * OWN : (slot + 1) * OWN, :]
    lane = lax.broadcasted_iota(jnp.int32, (OWN, PROJ), 1).astype(F32)

    def partners(slot, pos):
        code = rows[slot * SLOT + OWN : (slot + 1) * SLOT, :].astype(F32)
        owner = to_column(jnp.concatenate([code[0:1], code[1:2]], axis=1))
        place = to_column(jnp.concatenate([code[2:3], code[3:4]], axis=1))
        hot = jnp.concatenate(
            [jnp.where(place == lane, 1.0, 0.0), jnp.where(place == lane + PROJ, 1.0, 0.0)], axis=1
        ).astype(BF16)
        found = jnp.dot(hot, wide[...], preferred_element_type=F32)
        total = jnp.zeros((OWN, PROJ), F32)
        for k in range(16):
            dy, dz = COL_OFFS[k]
            dp, inner = peer(dy=dy, dz=dz)
            here = (dp * 8 + inner).astype(F32)
            total = total + jnp.where(owner == here, found[:, k * PROJ : (k + 1) * PROJ], 0.0)
        paired[slot * OWN : (slot + 1) * OWN, :] = total
        own = rows[slot * SLOT : slot * SLOT + OWN, :].astype(F32)
        return pos + own * total

    pos = jnp.zeros((OWN, PROJ), F32)
    for slot in range(4):
        pos = partners(slot, pos)

    for slot in range(1, 8):
        wait_bytes(sums_in.at[slot], sum_recv.at[slot])
    for slot in range(8):
        dx, dc = ROW_OFFS[slot]
        total = sums[slot : slot + 1, :]
        for sender in range(1, 8):
            ox, oc = ROW_OFFS[sender]
            at = ROW_OF[((dx - ox) % 4, (dc - oc) % 2)]
            total = total + sums_in[sender, at : at + 1, :]
        wts[slot : slot + 1, :] = 1.0 / total
        if slot == 0:
            log_sum = jnp.sum(jnp.log(total))
    for slot in range(1, 16):
        dy, dz = COL_OFFS[slot]
        to = COL_OF[neg_col((dy, dz))]
        send(wts, wts_in.at[to], x_send.at[4], wt_recv.at[to], peer(dy=dy, dz=dz))

    for slot in range(4, 8):
        pos = partners(slot, pos)
    loss_part = log_sum - INV_TAU * jnp.sum(pos)
    me1 = x * 2 + c
    loss1[me1] = jnp.full((8, PROJ), loss_part, F32)
    for slot in range(1, 8):
        dx, dc = ROW_OFFS[slot]
        to = ROW_OF[neg_row((dx, dc))]
        send(loss1.at[me1], loss1.at[me1], x_send.at[5], loss_recv1.at[to], peer(dx=dx, dc=dc))

    def weigh(slot, row):
        block = cols[slot * OWN : (slot + 1) * OWN, :]
        uw[slot * OWN : (slot + 1) * OWN, 0:PROJ] = block
        uw[slot * OWN : (slot + 1) * OWN, PROJ : 2 * PROJ] = (
            block.astype(F32) * to_column(row)
        ).astype(BF16)

    weigh(0, wts[0:1, :])
    for slot in range(1, 16):
        wait_bytes(wts_in.at[slot], wt_recv.at[slot])
        weigh(slot, wts_in[slot, 0:1, :])

    def product(slot):
        return jnp.dot(
            expo[slot * OWN : (slot + 1) * OWN, :], uw[...], preferred_element_type=F32
        )

    def terms(slot, both):
        w = to_column(wts[slot : slot + 1, :])
        return (
            w * both[:, 0:PROJ] + both[:, PROJ : 2 * PROJ]
            - 2.0 * paired[slot * OWN : (slot + 1) * OWN, :]
        )

    def quad_slot(slot):
        return quad.at[pl.ds(slot * OWN, OWN)]

    slot, both = None, None
    for later in (6, 5, 7, 2, 4, 1, 3, 0, None):
        if slot is not None and slot < 4:
            wait_bytes(quad_sib.at[slot], qs_recv.at[slot])
        both_later = None if later is None else product(later)
        if slot is not None:
            part = terms(slot, both)
            if slot < 4:
                part = part + quad_sib[slot]
            quad[slot * OWN : (slot + 1) * OWN, :] = part
            if slot > 3:
                send(
                    quad_slot(slot), quad_sib.at[slot - 4], x_send.at[6], qs_recv.at[slot - 4],
                    peer(dc=1),
                )
            elif slot > 0:
                to = (-slot) % 4
                send(quad_slot(slot), quad_ring.at[to], x_send.at[7], qr_recv.at[to], peer(dx=slot))
        slot, both = later, both_later

    summed = quad[0:OWN, :]
    for d in (1, 3, 2):
        wait_bytes(quad_ring.at[d], qr_recv.at[d])
        summed = summed + quad_ring[d]
    du = INV_TAU * summed
    uu = u_ref[...]
    dz_own[...] = (
        (du - uu * jnp.sum(uu * du, axis=1, keepdims=True)) / norm_ref[...]
    ).astype(BF16)
    send(dz_own, dz_sib, x_send.at[9], dz_recv.at[0], peer(dc=1))

    mine = pl.multiple_of(c * HALF, HALF)
    grad[...] = lax.dot_general(
        feat[:, pl.ds(mine, HALF)], dz_own[...], TN, preferred_element_type=F32
    )
    wait_bytes(feat_sib, feat_recv.at[0])
    wait_bytes(dz_sib, dz_recv.at[0])
    g1_in, g1, g2_in = (g1_in_a, g1_in_b, g1_in_c), (g1_a, g1_b, g1_c), (g2_in_a, g2_in_b, g2_in_c)
    parts = (0, 1, 2)

    def ring_block(part, d, base=0):
        span = 16 * TILES[part]
        first = base + STARTS[part] + torus.ring_at(part, d) * span
        return pl.ds(pl.multiple_of(first, span), span)

    for part in parts:
        of = slice(STARTS[part], STARTS[part] + 64 * TILES[part])
        grad[of, :] += lax.dot_general(feat_sib[:, of], dz_sib[...], TN, preferred_element_type=F32)
        for d in (2, 1, 3):
            at = (-d) % 4
            send(
                grad.at[ring_block(part, d)], g1_in[part].at[at],
                x_send.at[10], g1_recv.at[part, at], torus.ring_peer(part, d),
            )

    for slot in range(1, 8):
        wait_bytes(loss1.at[0], loss_recv1.at[slot])
    total = loss1[0]
    for k in range(1, 8):
        total = total + loss1[k]
    me2 = y * 4 + z
    loss2[me2] = total
    for slot in range(1, 16):
        dy, dz = COL_OFFS[slot]
        to = COL_OF[neg_col((dy, dz))]
        send(loss2.at[me2], loss2.at[me2], x_send.at[8], loss_recv2.at[to], peer(dy=dy, dz=dz))

    for part in parts:
        total = grad[ring_block(part, 0), :]
        for d in (1, 3, 2):
            wait_bytes(g1_in[part].at[d], g1_recv.at[part, d])
            total = total + g1_in[part][d]
        g1[part][...] = total
        tile = TILES[part]
        for slot in range(15, 0, -1):
            d1, d2 = COL_OFFS[slot]
            to = COL_OF[neg_col((d1, d2))]
            at = pl.multiple_of(torus.plane_at(part, d1, d2) * tile, tile)
            send(
                g1[part].at[pl.ds(at, tile)], g2_in[part].at[pl.ds(to * tile, tile)],
                x_send.at[11], g2_recv.at[part], torus.plane_peer(part, d1, d2),
            )
    base = c * HALF
    for part in parts:
        tile = TILES[part]
        place = torus.plane_at(part, 0, 0) * tile
        total = g1[part][pl.ds(pl.multiple_of(place, tile), tile), :]
        wait_bytes(g2_in[part].at[pl.ds(tile, 15 * tile)], g2_recv.at[part])
        for slot in range(1, 16):
            total = total + g2_in[part][slot * tile : (slot + 1) * tile, :]
        first = base + STARTS[part] + torus.ring_at(part, 0) * 16 * tile + place
        at = pl.ds(pl.multiple_of(first, tile), tile)
        out[at, :] = total * (1.0 / VIEWS**0.5)
        for slot in range(15, 0, -1):
            d1, d2 = COL_OFFS[slot]
            send(
                out.at[at], out.at[at], x_send.at[12], ag_recv.at[part],
                torus.plane_peer(part, d1, d2),
            )

    for part in parts:
        wait_bytes(out.at[pl.ds(0, 15 * TILES[part])], ag_recv.at[part])
        block = ring_block(part, 0, base)
        for d in (2, 1, 3):
            at = (-d) % 4
            send(
                out.at[block], out.at[block], x_send.at[13], ring_recv.at[part, at],
                torus.ring_peer(part, d),
            )
        send(out.at[block], out.at[block], x_send.at[14], rel_recv.at[part, 0], peer(dc=1))
    for d in (1, 3, 2):
        for part in parts:
            block = ring_block(part, d, base)
            wait_bytes(out.at[block], ring_recv.at[part, d])
            send(out.at[block], out.at[block], x_send.at[14], rel_recv.at[part, d], peer(dc=1))

    for slot in range(1, 16):
        wait_bytes(loss2.at[0], loss_recv2.at[slot])
    total = loss2[0]
    for k in range(1, 16):
        total = total + loss2[k]
    loss_ref[...] = total[0:1, 0:1] * (1.0 / VIEWS)

    other = torus.cs[1] * HALF
    for d in (0, 1, 3, 2):
        for part in parts:
            span = 16 * TILES[part]
            ends = (torus.ys[d], torus.xs[d])
            ring = torus.zs[d] if part == 2 else torus.pick(*(ends if part == 0 else ends[::-1]))
            block = pl.ds(pl.multiple_of(other + STARTS[part] + ring * span, span), span)
            wait_bytes(out.at[block], rel_recv.at[part, d])

    for ref, at in sent:
        wait_bytes(ref, x_send.at[at])


def per_device(features, proj_weight, partner):
    dma = pltpu.SemaphoreType.DMA
    grad, loss = pl.pallas_call(
        kernel,
        out_shape=(
            pltpu.VMEM((D, PROJ), F32),
            pltpu.VMEM((1, 1), F32),
        ),
        in_specs=[
            pl.BlockSpec(memory_space=pl.ANY),
            pl.BlockSpec(memory_space=pl.ANY),
            pl.BlockSpec(memory_space=pl.ANY),
        ],
        out_specs=(pl.BlockSpec(memory_space=pltpu.VMEM), pl.BlockSpec(memory_space=pltpu.VMEM)),
        scratch_shapes=[
            pltpu.VMEM((2, PROJ), jnp.int32),
            pltpu.VMEM((OWN, D), BF16),
            pltpu.VMEM((D, PROJ), BF16),
            pltpu.VMEM((OWN, HALF), BF16),
            pltpu.VMEM((OWN, PROJ), F32),
            pltpu.VMEM((OWN, PROJ), F32),
            pltpu.VMEM((8 * SLOT, PROJ), BF16),
            pltpu.VMEM((16 * OWN, PROJ), BF16),
            pltpu.VMEM((8 * OWN, 16 * OWN), BF16),
            pltpu.VMEM((8 * OWN, PROJ), F32),
            pltpu.VMEM((8, OWN), F32),
            pltpu.VMEM((8, 8, OWN), F32),
            pltpu.VMEM((8, OWN), F32),
            pltpu.VMEM((16, 8, OWN), F32),
            pltpu.VMEM((OWN, 16 * PROJ), BF16),
            pltpu.VMEM((8 * OWN, PROJ), F32),
            pltpu.VMEM((16 * OWN, 2 * PROJ), BF16),
            pltpu.VMEM((8 * OWN, PROJ), F32),
            pltpu.VMEM((4, OWN, PROJ), F32),
            pltpu.VMEM((4, OWN, PROJ), F32),
            pltpu.VMEM((OWN, PROJ), BF16),
            pltpu.VMEM((OWN, PROJ), BF16),
            pltpu.VMEM((HALF, PROJ), F32),
            *[pltpu.VMEM((4, 16 * tile, PROJ), F32) for tile in TILES],
            *[pltpu.VMEM((16 * tile, PROJ), F32) for tile in TILES],
            *[pltpu.VMEM((16 * tile, PROJ), F32) for tile in TILES],
            pltpu.VMEM((8, 8, PROJ), F32),
            pltpu.VMEM((16, 8, PROJ), F32),
            dma((9,)),
            dma((15,)),
            dma((16, 2)),
            dma((8,)),
            dma((1,)),
            dma((8,)),
            dma((16,)),
            dma((8,)),
            dma((16,)),
            dma((4,)),
            dma((4,)),
            dma((1,)),
            dma((3, 4)),
            dma((3,)),
            dma((3,)),
            dma((3, 4)),
            dma((3, 4)),
        ],
        compiler_params=pltpu.CompilerParams(
            collective_id=0, has_side_effects=True, vmem_limit_bytes=56 * 2**20
        ),
        name="simclr_head",
    )(features, proj_weight, partner.reshape(2, PROJ))
    return loss.reshape(()), grad


def solution(mesh):
    placed = (P(("dp", "inner"), None), P(), P(("dp", "inner")))
    return jax.shard_map(
        per_device, mesh=mesh, in_specs=placed, out_specs=(P(), P()), check_vma=False
    )
```

```python
import jax
import jax.numpy as jnp
from jax import lax
from jax.experimental import pallas as pl
from jax.experimental.pallas import tpu as pltpu
from jax.sharding import PartitionSpec as P

MESH = pl.DeviceIdType.MESH
F32 = jnp.float32
BF16 = jnp.bfloat16
VIEWS = 32768
D = 4096
HALF = D // 2
QUARTER = D // 4
PROJ = 128
OWN = 256
RINGS = 7
GROUPS = ((RINGS, 11), (11, 14), (14, 16))
SLOT = OWN + 16
INV_TAU = 5.0
SCALE2 = INV_TAU * 1.4426950408889634
NT = (((1,), (1,)), ((), ()))
TN = (((0,), (0,)), ((), ()))

ROW_OFFS = [(dx, dc) for dc in range(2) for dx in range(4)]
ROW_OF = {off: slot for slot, off in enumerate(ROW_OFFS)}
COL_OFFS = sorted(
    [(dy, dz) for dy in range(4) for dz in range(4)],
    key=lambda o: (0 not in o, min(o[0], 4 - o[0]) + min(o[1], 4 - o[1]), o),
)
COL_OF = {off: slot for slot, off in enumerate(COL_OFFS)}
RING_AXIS = {slot: int(off[0] == 0) for slot, off in enumerate(COL_OFFS) if slot and 0 in off}
TILES = (16, 8, 8)
STARTS = (0, 1024, 1536)


def neg_col(off):
    return ((-off[0]) % 4, (-off[1]) % 4)


def neg_row(off):
    return ((-off[0]) % 4, off[1])


def coords():
    dp, inner = lax.axis_index("dp"), lax.axis_index("inner")
    x = (inner % 2) * 2 + dp // 8
    return x, (dp // 2) % 4, inner // 2, dp % 2


def device_at(x, y, z, c):
    return ((x % 2) * 8 + y * 2 + c, z * 2 + x // 2)


class Torus:
    def __init__(self):
        x, y, z, c = coords()
        self.xs, self.ys, self.zs = ([(v + d) % 4 for d in range(4)] for v in (x, y, z))
        self.cs = [c, 1 - c]
        self.x_dp = [v % 2 * 8 for v in self.xs]
        self.x_inner = [v // 2 for v in self.xs]
        self.y_dp = [v * 2 for v in self.ys]
        self.z_inner = [v * 2 for v in self.zs]

    def peer(self, dx=0, dy=0, dz=0, dc=0):
        return (
            self.x_dp[dx] + self.y_dp[dy] + self.cs[dc],
            self.z_inner[dz] + self.x_inner[dx],
        )

    def pick(self, a, b):
        return a * self.cs[1] + b * self.cs[0]

    def pick_peer(self, a, b):
        return self.pick(a[0], b[0]), self.pick(a[1], b[1])

    def ring_at(self, part, d):
        if part == 2:
            return self.zs[d]
        ends = (self.xs[d], self.ys[d])
        return self.pick(*(ends if part == 0 else ends[::-1]))

    def plane_at(self, part, d1, d2):
        if part == 2:
            return self.xs[d1] * 4 + self.ys[d2]
        ends = (self.ys[d1], self.xs[d1])
        return self.pick(*(ends if part == 0 else ends[::-1])) * 4 + self.zs[d2]

    def ring_peer(self, part, d):
        if part == 2:
            return self.peer(dz=d)
        ends = (self.peer(dx=d), self.peer(dy=d))
        return self.pick_peer(*(ends if part == 0 else ends[::-1]))

    def plane_peer(self, part, d1, d2):
        if part == 2:
            return self.peer(dx=d1, dy=d2)
        ends = (self.peer(dy=d1, dz=d2), self.peer(dx=d1, dz=d2))
        return self.pick_peer(*(ends if part == 0 else ends[::-1]))


def ring_peers():
    offs = [off for d in (2, 1, 3) for off in ((d, 0, 0, 0), (0, d, 0, 0), (0, 0, d, 0))]
    return offs + [(0, 0, 0, 1)]


def send(src, dst, send_sem, recv_sem, device):
    copy = pltpu.make_async_remote_copy(
        src_ref=src, dst_ref=dst, send_sem=send_sem, recv_sem=recv_sem,
        device_id=device, device_id_type=MESH,
    )
    copy.start()


def wait_bytes(ref, sem):
    pltpu.make_async_copy(ref, ref, sem).wait()


def kernel(
    f_hbm, w_hbm, partner_hbm, out, loss_ref,
    partner_ref, feat, weight, feat_sib, u_ref, norm_ref, rows, cols, expo, acc,
    sums, sums_in, wts, wts_in, wide, paired, uw, quad, quad_sib, quad_ring,
    dz_own, dz_sib, grad, g1_in_a, g1_in_b, g1_in_c, g1_a, g1_b, g1_c,
    g2_in_a, g2_in_b, g2_in_c, loss1, loss2,
    load_sem, x_send, col_recv, row_recv, feat_recv, sum_recv, wt_recv, loss_recv1, loss_recv2,
    qs_recv, qr_recv, dz_recv, g1_recv, g2_recv, ag_recv, ring_recv, rel_recv,
):
    sent = [
        (rows.at[pl.ds(0, 7 * SLOT)], 0),
        (cols.at[pl.ds(0, 15 * OWN)], 1),
        (feat_sib, 2),
        (sums_in.at[pl.ds(0, 7)], 3),
        (wts_in.at[pl.ds(0, 15)], 4),
        (loss1.at[pl.ds(0, 7)], 5),
        (quad_sib, 6),
        (quad_ring.at[pl.ds(0, 3)], 7),
        (loss2.at[pl.ds(0, 15)], 8),
        (dz_sib, 9),
        (grad.at[pl.ds(0, 3 * HALF // 4)], 10),
        (grad.at[pl.ds(0, 15 * sum(TILES))], 11),
        (grad.at[pl.ds(0, 15 * sum(TILES))], 12),
        (grad.at[pl.ds(0, 3 * HALF // 4)], 13),
        (grad, 14),
    ]
    torus = Torus()
    peer = torus.peer
    x, y, z, c = torus.xs[0], torus.ys[0], torus.zs[0], torus.cs[0]
    loads = []
    for k in range(4):
        depth = pl.ds(k * QUARTER, QUARTER)
        loads.append(
            (
                pltpu.make_async_copy(w_hbm.at[depth], weight.at[depth], load_sem.at[k]),
                pltpu.make_async_copy(f_hbm.at[:, depth], feat.at[:, depth], load_sem.at[4 + k]),
            )
        )
    load_partner = pltpu.make_async_copy(partner_hbm, partner_ref, load_sem.at[8])
    load_partner.start()
    for pair in loads:
        for load in pair:
            load.start()
    barrier = pltpu.get_barrier_semaphore()
    peers = ring_peers()
    for off in peers:
        pl.semaphore_signal(barrier, inc=1, device_id=peer(*off), device_id_type=MESH)

    load_partner.wait()
    owner_of, place_of = partner_ref[...] // OWN, partner_ref[...] % OWN
    at = lax.broadcasted_iota(jnp.int32, (16, PROJ), 0)
    code = jnp.zeros((16, PROJ), F32)
    for k, row in enumerate((owner_of[0:1], owner_of[1:2], place_of[0:1], place_of[1:2])):
        code = jnp.where(at == k, row.astype(F32), code)
    rows[OWN:SLOT, :] = code.astype(BF16)

    zed = None
    for k, pair in enumerate(loads):
        for load in pair:
            load.wait()
        term = jnp.dot(
            feat[:, k * QUARTER : (k + 1) * QUARTER], weight[k * QUARTER : (k + 1) * QUARTER, :],
            preferred_element_type=F32,
        )
        zed = term if zed is None else zed + term
    norm = jnp.sqrt(jnp.sum(zed * zed, axis=1, keepdims=True) + 1e-06)
    u = zed / norm
    u_ref[...] = u
    norm_ref[...] = jnp.broadcast_to(norm, (OWN, PROJ))
    ub = u.astype(BF16)
    rows[0:OWN, :] = ub
    cols[0:OWN, :] = ub
    pl.semaphore_wait(barrier, len(peers))

    def row_slot(slot):
        return rows.at[pl.ds(slot * SLOT, SLOT)]

    def col_slot(slot):
        return cols.at[pl.ds(slot * OWN, OWN)]

    def col_half(slot, half):
        return cols.at[pl.ds(slot * OWN + half * (OWN // 2), OWN // 2)]

    for dx in (1, 3, 2):
        to = ROW_OF[neg_row((dx, 0))]
        send(row_slot(0), row_slot(to), x_send.at[0], row_recv.at[to], peer(dx=dx))
    send(row_slot(0), row_slot(4), x_send.at[0], row_recv.at[4], peer(dc=1))
    for turn in range(2):
        for d in (1, 3, 2):
            for axis in range(2):
                half = axis ^ turn
                off = (d, 0) if axis == 0 else (0, d)
                to = COL_OF[neg_col(off)]
                send(
                    col_half(0, half), col_half(to, half), x_send.at[1],
                    col_recv.at[to, half], peer(dy=off[0], dz=off[1]),
                )

    def pass_on(axis, d):
        off = (d, 0) if axis == 0 else (0, d)
        slot = COL_OF[off]
        wait_bytes(col_half(slot, axis), col_recv.at[slot, axis])
        for e in (1, 3, 2):
            hop = (0, e) if axis == 0 else (e, 0)
            to = COL_OF[((off[0] - hop[0]) % 4, (off[1] - hop[1]) % 4)]
            send(
                col_half(slot, axis), col_half(to, axis), x_send.at[1],
                col_recv.at[to, axis], peer(dy=hop[0], dz=hop[1]),
            )

    def pass_row(slot):
        wait_bytes(row_slot(slot), row_recv.at[slot])
        send(row_slot(slot), row_slot(4 + slot), x_send.at[0], row_recv.at[4 + slot], peer(dc=1))

    def lanes(e):
        total = e[:, 0:PROJ]
        for q in range(1, e.shape[1] // PROJ):
            total = total + e[:, q * PROJ : (q + 1) * PROJ]
        return total

    def scores(slot, first, end):
        return jnp.exp2(
            lax.dot_general(
                rows[slot * SLOT : slot * SLOT + OWN, :], cols[first * OWN : end * OWN, :], NT,
                preferred_element_type=F32,
            )
            * SCALE2
        )

    def pass1(slot, first, end):
        e = scores(slot, first, end)
        if slot == 0 and first == 0:
            at_row = lax.broadcasted_iota(jnp.int32, e.shape, 0)
            at_col = lax.broadcasted_iota(jnp.int32, e.shape, 1)
            e = jnp.where(at_row == at_col, 0.0, e)
        of = slice(slot * OWN, (slot + 1) * OWN)
        expo[of, first * OWN : end * OWN] = e.astype(BF16)
        if first == 0:
            acc[of, :] = lanes(e)
        else:
            acc[of, :] += lanes(e)

    def wait_ring(slot):
        half = 1 - RING_AXIS[slot]
        wait_bytes(col_half(slot, half), col_recv.at[slot, half])

    for d in (1, 3):
        pass_on(0, d)
        pass_on(1, d)
        pass_row(d)
    pass_on(0, 2)
    pass_on(1, 2)
    wait_bytes(row_slot(4), row_recv.at[4])
    for slot in range(1, 4):
        wait_ring(slot)
    for slot in (0, 4, 1, 3):
        pass1(slot, 0, 4)
    pass_row(2)
    send(
        feat.at[:, pl.ds(pl.multiple_of((1 - c) * HALF, HALF), HALF)], feat_sib,
        x_send.at[2], feat_recv.at[0], peer(dc=1),
    )
    for slot in range(4, RINGS):
        wait_ring(slot)
    for slot in (0, 4, 1, 3):
        pass1(slot, 4, RINGS)
    for slot in (5, 7, 6):
        wait_bytes(row_slot(slot), row_recv.at[slot])
    for slot in (5, 7, 2, 6):
        pass1(slot, 0, RINGS)
    for first, end in GROUPS:
        for slot in range(first, end):
            for half in range(2):
                wait_bytes(col_half(slot, half), col_recv.at[slot, half])
        for slot in range(8):
            pass1(slot, first, end)

    eye = lax.broadcasted_iota(jnp.int32, (PROJ, PROJ), 0) == lax.broadcasted_iota(
        jnp.int32, (PROJ, PROJ), 1
    )

    def to_row(column):
        return jnp.sum(jnp.where(eye, column, 0.0), axis=0, keepdims=True)

    def to_column(*rows_of):
        halves = [
            jnp.sum(jnp.where(eye, row, 0.0), axis=1, keepdims=True) for row in rows_of
        ]
        return jnp.broadcast_to(jnp.concatenate(halves, axis=0), (OWN, PROJ))

    for slot in range(8):
        for h in range(2):
            first = slot * OWN + h * PROJ
            column = jnp.sum(acc[first : first + PROJ, :], axis=1, keepdims=True)
            sums[slot : slot + 1, h * PROJ : (h + 1) * PROJ] = to_row(column)
    for slot in (2, 6, 1, 3, 5, 7, 4):
        dx, dc = ROW_OFFS[slot]
        to = ROW_OF[neg_row((dx, dc))]
        send(sums, sums_in.at[to], x_send.at[3], sum_recv.at[to], peer(dx=dx, dc=dc))

    for slot in range(16):
        block = cols[slot * OWN : (slot + 1) * OWN, :]
        wide[:, slot * PROJ : (slot + 1) * PROJ] = block
        uw[slot * OWN : (slot + 1) * OWN, 0:PROJ] = block
    lane = lax.broadcasted_iota(jnp.int32, (OWN, PROJ), 1).astype(F32)

    def partners(slot, pos):
        code = rows[slot * SLOT + OWN : (slot + 1) * SLOT, :].astype(F32)
        owner = to_column(code[0:1], code[1:2])
        place = to_column(code[2:3], code[3:4])
        hot = jnp.concatenate(
            [jnp.where(place == lane, 1.0, 0.0), jnp.where(place == lane + PROJ, 1.0, 0.0)], axis=1
        ).astype(BF16)
        found = jnp.dot(hot, wide[...], preferred_element_type=F32)
        total = jnp.zeros((OWN, PROJ), F32)
        for k in range(16):
            dy, dz = COL_OFFS[k]
            dp, inner = peer(dy=dy, dz=dz)
            here = (dp * 8 + inner).astype(F32)
            total = total + jnp.where(owner == here, found[:, k * PROJ : (k + 1) * PROJ], 0.0)
        paired[slot * OWN : (slot + 1) * OWN, :] = total
        own = rows[slot * SLOT : slot * SLOT + OWN, :].astype(F32)
        return pos + own * total

    pos = jnp.zeros((OWN, PROJ), F32)
    for slot in range(4):
        pos = partners(slot, pos)

    for slot in range(1, 8):
        wait_bytes(sums_in.at[slot], sum_recv.at[slot])
    for slot in range(8):
        dx, dc = ROW_OFFS[slot]
        total = sums[slot : slot + 1, :]
        for sender in range(1, 8):
            ox, oc = ROW_OFFS[sender]
            at = ROW_OF[((dx - ox) % 4, (dc - oc) % 2)]
            total = total + sums_in[sender, at : at + 1, :]
        for h in range(2):
            wts[slot, h : h + 1, :] = 1.0 / total[:, h * PROJ : (h + 1) * PROJ]
        if slot == 0:
            log_sum = jnp.sum(jnp.log(total))
    for slot in range(1, 16):
        dy, dz = COL_OFFS[slot]
        to = COL_OF[neg_col((dy, dz))]
        send(wts.at[0], wts_in.at[to], x_send.at[4], wt_recv.at[to], peer(dy=dy, dz=dz))

    for slot in range(4, 8):
        pos = partners(slot, pos)
    loss_part = log_sum - INV_TAU * jnp.sum(pos)
    me1 = x * 2 + c
    loss1[me1] = jnp.full((1, PROJ), loss_part, F32)
    for slot in range(1, 8):
        dx, dc = ROW_OFFS[slot]
        to = ROW_OF[neg_row((dx, dc))]
        send(loss1.at[me1], loss1.at[me1], x_send.at[5], loss_recv1.at[to], peer(dx=dx, dc=dc))

    def weigh(slot, table):
        block = cols[slot * OWN : (slot + 1) * OWN, :]
        uw[slot * OWN : (slot + 1) * OWN, PROJ : 2 * PROJ] = (
            block.astype(F32) * to_column(table[0:1], table[1:2])
        ).astype(BF16)

    weigh(0, wts[0])
    for slot in range(1, 16):
        wait_bytes(wts_in.at[slot], wt_recv.at[slot])
    for slot in range(1, 16):
        weigh(slot, wts_in[slot])

    def product(slot):
        return jnp.dot(
            expo[slot * OWN : (slot + 1) * OWN, :], uw[...], preferred_element_type=F32
        )

    def terms(slot, both):
        w = to_column(wts[slot, 0:1, :], wts[slot, 1:2, :])
        return (
            w * both[:, 0:PROJ] + both[:, PROJ : 2 * PROJ]
            - 2.0 * paired[slot * OWN : (slot + 1) * OWN, :]
        )

    def quad_slot(slot):
        return quad.at[pl.ds(slot * OWN, OWN)]

    slot, both = None, None
    for later in (6, 5, 7, 2, 4, 1, 3, 0, None):
        if slot is not None and slot < 4:
            wait_bytes(quad_sib.at[slot], qs_recv.at[slot])
        both_later = None if later is None else product(later)
        if slot is not None:
            part = terms(slot, both)
            if slot < 4:
                part = part + quad_sib[slot]
            quad[slot * OWN : (slot + 1) * OWN, :] = part
            if slot > 3:
                send(
                    quad_slot(slot), quad_sib.at[slot - 4], x_send.at[6], qs_recv.at[slot - 4],
                    peer(dc=1),
                )
            elif slot > 0:
                to = (-slot) % 4
                send(quad_slot(slot), quad_ring.at[to], x_send.at[7], qr_recv.at[to], peer(dx=slot))
        slot, both = later, both_later

    summed = quad[0:OWN, :]
    for d in (1, 3, 2):
        wait_bytes(quad_ring.at[d], qr_recv.at[d])
        summed = summed + quad_ring[d]
    du = INV_TAU * summed
    uu = u_ref[...]
    dz_own[...] = (
        (du - uu * jnp.sum(uu * du, axis=1, keepdims=True)) / norm_ref[...]
    ).astype(BF16)
    send(dz_own, dz_sib, x_send.at[9], dz_recv.at[0], peer(dc=1))

    mine = pl.multiple_of(c * HALF, HALF)
    grad[...] = lax.dot_general(
        feat[:, pl.ds(mine, HALF)], dz_own[...], TN, preferred_element_type=F32
    )
    wait_bytes(feat_sib, feat_recv.at[0])
    wait_bytes(dz_sib, dz_recv.at[0])
    g1_in, g1, g2_in = (g1_in_a, g1_in_b, g1_in_c), (g1_a, g1_b, g1_c), (g2_in_a, g2_in_b, g2_in_c)
    parts = (2, 1, 0)

    def ring_block(part, d, base=0):
        span = 16 * TILES[part]
        first = base + STARTS[part] + torus.ring_at(part, d) * span
        return pl.ds(pl.multiple_of(first, span), span)

    for part in (0, 1, 2):
        of = slice(STARTS[part], STARTS[part] + 64 * TILES[part])
        grad[of, :] += lax.dot_general(feat_sib[:, of], dz_sib[...], TN, preferred_element_type=F32)
        for d in (2, 1, 3):
            at = (-d) % 4
            send(
                grad.at[ring_block(part, d)], g1_in[part].at[at],
                x_send.at[10], g1_recv.at[part, at], torus.ring_peer(part, d),
            )

    for slot in range(1, 8):
        wait_bytes(loss1.at[0], loss_recv1.at[slot])
    total = loss1[0]
    for k in range(1, 8):
        total = total + loss1[k]
    me2 = y * 4 + z
    loss2[me2] = total
    for slot in range(1, 16):
        dy, dz = COL_OFFS[slot]
        to = COL_OF[neg_col((dy, dz))]
        send(loss2.at[me2], loss2.at[me2], x_send.at[8], loss_recv2.at[to], peer(dy=dy, dz=dz))

    for part in parts:
        total = grad[ring_block(part, 0), :]
        for d in (1, 3, 2):
            wait_bytes(g1_in[part].at[d], g1_recv.at[part, d])
            total = total + g1_in[part][d]
        g1[part][...] = total
        tile = TILES[part]
        for slot in range(15, 0, -1):
            d1, d2 = COL_OFFS[slot]
            to = COL_OF[neg_col((d1, d2))]
            at = pl.multiple_of(torus.plane_at(part, d1, d2) * tile, tile)
            send(
                g1[part].at[pl.ds(at, tile)], g2_in[part].at[pl.ds(to * tile, tile)],
                x_send.at[11], g2_recv.at[part], torus.plane_peer(part, d1, d2),
            )
    base = c * HALF
    for part in parts:
        tile = TILES[part]
        place = torus.plane_at(part, 0, 0) * tile
        total = g1[part][pl.ds(pl.multiple_of(place, tile), tile), :]
        wait_bytes(g2_in[part].at[pl.ds(tile, 15 * tile)], g2_recv.at[part])
        for slot in range(1, 16):
            total = total + g2_in[part][slot * tile : (slot + 1) * tile, :]
        first = base + STARTS[part] + torus.ring_at(part, 0) * 16 * tile + place
        at = pl.ds(pl.multiple_of(first, tile), tile)
        out[at, :] = total * (1.0 / VIEWS**0.5)
        for slot in range(15, 0, -1):
            d1, d2 = COL_OFFS[slot]
            send(
                out.at[at], out.at[at], x_send.at[12], ag_recv.at[part],
                torus.plane_peer(part, d1, d2),
            )

    for part in parts:
        wait_bytes(out.at[pl.ds(0, 15 * TILES[part])], ag_recv.at[part])
        block = ring_block(part, 0, base)
        for d in (2, 1, 3):
            at = (-d) % 4
            send(
                out.at[block], out.at[block], x_send.at[13], ring_recv.at[part, at],
                torus.ring_peer(part, d),
            )
        send(out.at[block], out.at[block], x_send.at[14], rel_recv.at[part, 0], peer(dc=1))
    for d in (1, 3, 2):
        for part in parts:
            block = ring_block(part, d, base)
            wait_bytes(out.at[block], ring_recv.at[part, d])
            send(out.at[block], out.at[block], x_send.at[14], rel_recv.at[part, d], peer(dc=1))

    for slot in range(1, 16):
        wait_bytes(loss2.at[0], loss_recv2.at[slot])
    total = loss2[0]
    for k in range(1, 16):
        total = total + loss2[k]
    loss_ref[...] = total[0:1, 0:1] * (1.0 / VIEWS)

    other = torus.cs[1] * HALF
    for d in (0, 1, 3, 2):
        for part in parts:
            span = 16 * TILES[part]
            ends = (torus.ys[d], torus.xs[d])
            ring = torus.zs[d] if part == 2 else torus.pick(*(ends if part == 0 else ends[::-1]))
            block = pl.ds(pl.multiple_of(other + STARTS[part] + ring * span, span), span)
            wait_bytes(out.at[block], rel_recv.at[part, d])

    for ref, at in sent:
        wait_bytes(ref, x_send.at[at])


def per_device(features, proj_weight, partner):
    dma = pltpu.SemaphoreType.DMA
    grad, loss = pl.pallas_call(
        kernel,
        out_shape=(
            pltpu.VMEM((D, PROJ), F32),
            pltpu.VMEM((1, 1), F32),
        ),
        in_specs=[
            pl.BlockSpec(memory_space=pl.ANY),
            pl.BlockSpec(memory_space=pl.ANY),
            pl.BlockSpec(memory_space=pl.ANY),
        ],
        out_specs=(pl.BlockSpec(memory_space=pltpu.VMEM), pl.BlockSpec(memory_space=pltpu.VMEM)),
        scratch_shapes=[
            pltpu.VMEM((2, PROJ), jnp.int32),
            pltpu.VMEM((OWN, D), BF16),
            pltpu.VMEM((D, PROJ), BF16),
            pltpu.VMEM((OWN, HALF), BF16),
            pltpu.VMEM((OWN, PROJ), F32),
            pltpu.VMEM((OWN, PROJ), F32),
            pltpu.VMEM((8 * SLOT, PROJ), BF16),
            pltpu.VMEM((16 * OWN, PROJ), BF16),
            pltpu.VMEM((8 * OWN, 16 * OWN), BF16),
            pltpu.VMEM((8 * OWN, PROJ), F32),
            pltpu.VMEM((8, OWN), F32),
            pltpu.VMEM((8, 8, OWN), F32),
            pltpu.VMEM((8, 2, PROJ), F32),
            pltpu.VMEM((16, 2, PROJ), F32),
            pltpu.VMEM((OWN, 16 * PROJ), BF16),
            pltpu.VMEM((8 * OWN, PROJ), F32),
            pltpu.VMEM((16 * OWN, 2 * PROJ), BF16),
            pltpu.VMEM((8 * OWN, PROJ), F32),
            pltpu.VMEM((4, OWN, PROJ), F32),
            pltpu.VMEM((4, OWN, PROJ), F32),
            pltpu.VMEM((OWN, PROJ), BF16),
            pltpu.VMEM((OWN, PROJ), BF16),
            pltpu.VMEM((HALF, PROJ), F32),
            *[pltpu.VMEM((4, 16 * tile, PROJ), F32) for tile in TILES],
            *[pltpu.VMEM((16 * tile, PROJ), F32) for tile in TILES],
            *[pltpu.VMEM((16 * tile, PROJ), F32) for tile in TILES],
            pltpu.VMEM((8, 1, PROJ), F32),
            pltpu.VMEM((16, 1, PROJ), F32),
            dma((9,)),
            dma((15,)),
            dma((16, 2)),
            dma((8,)),
            dma((1,)),
            dma((8,)),
            dma((16,)),
            dma((8,)),
            dma((16,)),
            dma((4,)),
            dma((4,)),
            dma((1,)),
            dma((3, 4)),
            dma((3,)),
            dma((3,)),
            dma((3, 4)),
            dma((3, 4)),
        ],
        compiler_params=pltpu.CompilerParams(
            collective_id=0, has_side_effects=True, vmem_limit_bytes=56 * 2**20
        ),
        name="simclr_head",
    )(features, proj_weight, partner.reshape(2, PROJ))
    return loss.reshape(()), grad


def solution(mesh):
    placed = (P(("dp", "inner"), None), P(), P(("dp", "inner")))
    return jax.shard_map(
        per_device, mesh=mesh, in_specs=placed, out_specs=(P(), P()), check_vma=False
    )
```

```python
import jax
import jax.numpy as jnp
from jax import lax
from jax.experimental import pallas as pl
from jax.experimental.pallas import tpu as pltpu
from jax.sharding import PartitionSpec as P

MESH = pl.DeviceIdType.MESH
F32 = jnp.float32
BF16 = jnp.bfloat16
VIEWS = 32768
D = 4096
HALF = D // 2
QUARTER = D // 4
PROJ = 128
OWN = 256
RINGS = 7
GROUPS = ((RINGS, 11), (11, 14), (14, 16))
SLOT = OWN + 16
INV_TAU = 5.0
SCALE2 = INV_TAU * 1.4426950408889634
NT = (((1,), (1,)), ((), ()))
TN = (((0,), (0,)), ((), ()))

ROW_OFFS = [(dx, dc) for dc in range(2) for dx in range(4)]
ROW_OF = {off: slot for slot, off in enumerate(ROW_OFFS)}
COL_OFFS = sorted(
    [(dy, dz) for dy in range(4) for dz in range(4)],
    key=lambda o: (0 not in o, min(o[0], 4 - o[0]) + min(o[1], 4 - o[1]), o),
)
COL_OF = {off: slot for slot, off in enumerate(COL_OFFS)}
RING_AXIS = {slot: int(off[0] == 0) for slot, off in enumerate(COL_OFFS) if slot and 0 in off}
TILES = (16, 8, 8)
STARTS = (0, 1024, 1536)


def neg_col(off):
    return ((-off[0]) % 4, (-off[1]) % 4)


def neg_row(off):
    return ((-off[0]) % 4, off[1])


def coords():
    dp, inner = lax.axis_index("dp"), lax.axis_index("inner")
    x = (inner % 2) * 2 + dp // 8
    return x, (dp // 2) % 4, inner // 2, dp % 2


def device_at(x, y, z, c):
    return ((x % 2) * 8 + y * 2 + c, z * 2 + x // 2)


class Torus:
    def __init__(self):
        x, y, z, c = coords()
        self.xs, self.ys, self.zs = ([(v + d) % 4 for d in range(4)] for v in (x, y, z))
        self.cs = [c, 1 - c]
        self.x_dp = [v % 2 * 8 for v in self.xs]
        self.x_inner = [v // 2 for v in self.xs]
        self.y_dp = [v * 2 for v in self.ys]
        self.z_inner = [v * 2 for v in self.zs]

    def peer(self, dx=0, dy=0, dz=0, dc=0):
        return (
            self.x_dp[dx] + self.y_dp[dy] + self.cs[dc],
            self.z_inner[dz] + self.x_inner[dx],
        )

    def pick(self, a, b):
        return a * self.cs[1] + b * self.cs[0]

    def pick_peer(self, a, b):
        return self.pick(a[0], b[0]), self.pick(a[1], b[1])

    def ring_at(self, part, d):
        if part == 2:
            return self.zs[d]
        ends = (self.xs[d], self.ys[d])
        return self.pick(*(ends if part == 0 else ends[::-1]))

    def row_at(self, part, d1):
        if part == 2:
            return self.xs[d1]
        ends = (self.ys[d1], self.xs[d1])
        return self.pick(*(ends if part == 0 else ends[::-1]))

    def plane_at(self, part, d1, d2):
        if part == 2:
            return self.xs[d1] * 4 + self.ys[d2]
        ends = (self.ys[d1], self.xs[d1])
        return self.pick(*(ends if part == 0 else ends[::-1])) * 4 + self.zs[d2]

    def ring_peer(self, part, d):
        if part == 2:
            return self.peer(dz=d)
        ends = (self.peer(dx=d), self.peer(dy=d))
        return self.pick_peer(*(ends if part == 0 else ends[::-1]))

    def plane_peer(self, part, d1, d2):
        if part == 2:
            return self.peer(dx=d1, dy=d2)
        ends = (self.peer(dy=d1, dz=d2), self.peer(dx=d1, dz=d2))
        return self.pick_peer(*(ends if part == 0 else ends[::-1]))


def ring_peers():
    offs = [off for d in (2, 1, 3) for off in ((d, 0, 0, 0), (0, d, 0, 0), (0, 0, d, 0))]
    return offs + [(0, 0, 0, 1)]


def send(src, dst, send_sem, recv_sem, device):
    copy = pltpu.make_async_remote_copy(
        src_ref=src, dst_ref=dst, send_sem=send_sem, recv_sem=recv_sem,
        device_id=device, device_id_type=MESH,
    )
    copy.start()


def wait_bytes(ref, sem):
    pltpu.make_async_copy(ref, ref, sem).wait()


def kernel(
    f_hbm, w_hbm, partner_hbm, out, loss_ref,
    partner_ref, feat, weight, feat_sib, u_ref, norm_ref, rows, cols, expo, acc,
    sums, sums_in, wts, wts_in, wide, paired, uw, w_rows, quad, quad_sib, quad_ring,
    dz_own, dz_sib, grad, g1_in_a, g1_in_b, g1_in_c, g1_a, g1_b, g1_c,
    g2_in_a, g2_in_b, g2_in_c, loss1, loss2,
    load_sem, x_send, col_recv, row_recv, feat_recv, sum_recv, wt_recv, loss_recv1, loss_recv2,
    qs_recv, qr_recv, dz_recv, g1_recv, g2_recv, ag_recv, ring_recv, rel_recv,
):
    sent = [
        (rows.at[pl.ds(0, 7 * SLOT)], 0),
        (cols.at[pl.ds(0, 15 * OWN)], 1),
        (feat_sib, 2),
        (sums_in.at[pl.ds(0, 7)], 3),
        (wts_in.at[pl.ds(0, 15)], 4),
        (loss1.at[pl.ds(0, 7)], 5),
        (quad_sib, 6),
        (quad_ring.at[pl.ds(0, 3)], 7),
        (loss2.at[pl.ds(0, 15)], 8),
        (dz_sib, 9),
        (grad.at[pl.ds(0, 3 * HALF // 4)], 10),
        (grad.at[pl.ds(0, 15 * sum(TILES))], 11),
        (grad.at[pl.ds(0, 15 * sum(TILES))], 12),
        (grad.at[pl.ds(0, 3 * HALF // 4)], 13),
        (grad, 14),
    ]
    torus = Torus()
    peer = torus.peer
    x, y, z, c = torus.xs[0], torus.ys[0], torus.zs[0], torus.cs[0]
    loads = []
    for k in range(4):
        depth = pl.ds(k * QUARTER, QUARTER)
        loads.append(
            (
                pltpu.make_async_copy(w_hbm.at[depth], weight.at[depth], load_sem.at[k]),
                pltpu.make_async_copy(f_hbm.at[:, depth], feat.at[:, depth], load_sem.at[4 + k]),
            )
        )
    load_partner = pltpu.make_async_copy(partner_hbm, partner_ref, load_sem.at[8])
    load_partner.start()
    for pair in loads:
        for load in pair:
            load.start()
    barrier = pltpu.get_barrier_semaphore()
    peers = ring_peers()
    for off in peers:
        pl.semaphore_signal(barrier, inc=1, device_id=peer(*off), device_id_type=MESH)

    load_partner.wait()
    owner_of, place_of = partner_ref[...] // OWN, partner_ref[...] % OWN
    at = lax.broadcasted_iota(jnp.int32, (16, PROJ), 0)
    code = jnp.zeros((16, PROJ), F32)
    for k, row in enumerate((owner_of[0:1], owner_of[1:2], place_of[0:1], place_of[1:2])):
        code = jnp.where(at == k, row.astype(F32), code)
    rows[OWN:SLOT, :] = code.astype(BF16)

    zed = None
    for k, pair in enumerate(loads):
        for load in pair:
            load.wait()
        term = jnp.dot(
            feat[:, k * QUARTER : (k + 1) * QUARTER], weight[k * QUARTER : (k + 1) * QUARTER, :],
            preferred_element_type=F32,
        )
        zed = term if zed is None else zed + term
    norm = jnp.sqrt(jnp.sum(zed * zed, axis=1, keepdims=True) + 1e-06)
    u = zed / norm
    u_ref[...] = u
    norm_ref[...] = jnp.broadcast_to(norm, (OWN, PROJ))
    ub = u.astype(BF16)
    rows[0:OWN, :] = ub
    cols[0:OWN, :] = ub
    pl.semaphore_wait(barrier, len(peers))

    def row_slot(slot):
        return rows.at[pl.ds(slot * SLOT, SLOT)]

    def col_slot(slot):
        return cols.at[pl.ds(slot * OWN, OWN)]

    def col_half(slot, half):
        return cols.at[pl.ds(slot * OWN + half * (OWN // 2), OWN // 2)]

    for dx in (1, 3, 2):
        to = ROW_OF[neg_row((dx, 0))]
        send(row_slot(0), row_slot(to), x_send.at[0], row_recv.at[to], peer(dx=dx))
    send(row_slot(0), row_slot(4), x_send.at[0], row_recv.at[4], peer(dc=1))
    for turn in range(2):
        for d in (1, 3, 2):
            for axis in range(2):
                half = axis ^ turn
                off = (d, 0) if axis == 0 else (0, d)
                to = COL_OF[neg_col(off)]
                send(
                    col_half(0, half), col_half(to, half), x_send.at[1],
                    col_recv.at[to, half], peer(dy=off[0], dz=off[1]),
                )

    def pass_on(axis, d):
        off = (d, 0) if axis == 0 else (0, d)
        slot = COL_OF[off]
        wait_bytes(col_half(slot, axis), col_recv.at[slot, axis])
        for e in (1, 3, 2):
            hop = (0, e) if axis == 0 else (e, 0)
            to = COL_OF[((off[0] - hop[0]) % 4, (off[1] - hop[1]) % 4)]
            send(
                col_half(slot, axis), col_half(to, axis), x_send.at[1],
                col_recv.at[to, axis], peer(dy=hop[0], dz=hop[1]),
            )

    def pass_row(slot):
        wait_bytes(row_slot(slot), row_recv.at[slot])
        send(row_slot(slot), row_slot(4 + slot), x_send.at[0], row_recv.at[4 + slot], peer(dc=1))

    def lanes(e):
        total = e[:, 0:PROJ]
        for q in range(1, e.shape[1] // PROJ):
            total = total + e[:, q * PROJ : (q + 1) * PROJ]
        return total

    def scores(slot, first, end):
        return jnp.exp2(
            lax.dot_general(
                rows[slot * SLOT : slot * SLOT + OWN, :], cols[first * OWN : end * OWN, :], NT,
                preferred_element_type=F32,
            )
            * SCALE2
        )

    def pass1(slot, first, end):
        e = scores(slot, first, end)
        if slot == 0 and first == 0:
            at_row = lax.broadcasted_iota(jnp.int32, e.shape, 0)
            at_col = lax.broadcasted_iota(jnp.int32, e.shape, 1)
            e = jnp.where(at_row == at_col, 0.0, e)
        of = slice(slot * OWN, (slot + 1) * OWN)
        expo[of, first * OWN : end * OWN] = e.astype(BF16)
        if first == 0:
            acc[of, :] = lanes(e)
        else:
            acc[of, :] += lanes(e)

    def wait_ring(slot):
        half = 1 - RING_AXIS[slot]
        wait_bytes(col_half(slot, half), col_recv.at[slot, half])

    for d in (1, 3):
        pass_on(0, d)
        pass_on(1, d)
        pass_row(d)
    pass_on(0, 2)
    pass_on(1, 2)
    wait_bytes(row_slot(4), row_recv.at[4])
    for slot in range(1, 4):
        wait_ring(slot)
    for slot in (0, 4, 1, 3):
        pass1(slot, 0, 4)
    pass_row(2)
    send(
        feat.at[:, pl.ds(pl.multiple_of((1 - c) * HALF, HALF), HALF)], feat_sib,
        x_send.at[2], feat_recv.at[0], peer(dc=1),
    )
    for slot in range(4, RINGS):
        wait_ring(slot)
    for slot in (0, 4, 1, 3):
        pass1(slot, 4, RINGS)
    for slot in (5, 7, 6):
        wait_bytes(row_slot(slot), row_recv.at[slot])
    for slot in (5, 7, 2, 6):
        pass1(slot, 0, RINGS)
    for first, end in GROUPS:
        for slot in range(first, end):
            for half in range(2):
                wait_bytes(col_half(slot, half), col_recv.at[slot, half])
        for slot in range(8):
            pass1(slot, first, end)

    eye = lax.broadcasted_iota(jnp.int32, (PROJ, PROJ), 0) == lax.broadcasted_iota(
        jnp.int32, (PROJ, PROJ), 1
    )

    def to_row(column):
        return jnp.sum(jnp.where(eye, column, 0.0), axis=0, keepdims=True)

    def to_column(*rows_of):
        halves = [
            jnp.sum(jnp.where(eye, row, 0.0), axis=1, keepdims=True) for row in rows_of
        ]
        return jnp.broadcast_to(jnp.concatenate(halves, axis=0), (OWN, PROJ))

    for slot in range(8):
        for h in range(2):
            first = slot * OWN + h * PROJ
            column = jnp.sum(acc[first : first + PROJ, :], axis=1, keepdims=True)
            sums[slot : slot + 1, h * PROJ : (h + 1) * PROJ] = to_row(column)
    for slot in (2, 6, 1, 3, 5, 7, 4):
        dx, dc = ROW_OFFS[slot]
        to = ROW_OF[neg_row((dx, dc))]
        send(sums, sums_in.at[to], x_send.at[3], sum_recv.at[to], peer(dx=dx, dc=dc))

    for slot in range(16):
        block = cols[slot * OWN : (slot + 1) * OWN, :]
        wide[:, slot * PROJ : (slot + 1) * PROJ] = block
        uw[slot * OWN : (slot + 1) * OWN, 0:PROJ] = block
    lane = lax.broadcasted_iota(jnp.int32, (OWN, PROJ), 1).astype(F32)

    def partners(slot, pos):
        code = rows[slot * SLOT + OWN : (slot + 1) * SLOT, :].astype(F32)
        owner = to_column(code[0:1], code[1:2])
        place = to_column(code[2:3], code[3:4])
        hot = jnp.concatenate(
            [jnp.where(place == lane, 1.0, 0.0), jnp.where(place == lane + PROJ, 1.0, 0.0)], axis=1
        ).astype(BF16)
        found = jnp.dot(hot, wide[...], preferred_element_type=F32)
        total = jnp.zeros((OWN, PROJ), F32)
        for k in range(16):
            dy, dz = COL_OFFS[k]
            dp, inner = peer(dy=dy, dz=dz)
            here = (dp * 8 + inner).astype(F32)
            total = total + jnp.where(owner == here, found[:, k * PROJ : (k + 1) * PROJ], 0.0)
        paired[slot * OWN : (slot + 1) * OWN, :] = total
        own = rows[slot * SLOT : slot * SLOT + OWN, :].astype(F32)
        return pos + own * total

    pos = jnp.zeros((OWN, PROJ), F32)
    for slot in range(4):
        pos = partners(slot, pos)

    for slot in range(1, 8):
        wait_bytes(sums_in.at[slot], sum_recv.at[slot])
    for slot in range(8):
        dx, dc = ROW_OFFS[slot]
        total = sums[slot : slot + 1, :]
        for sender in range(1, 8):
            ox, oc = ROW_OFFS[sender]
            at = ROW_OF[((dx - ox) % 4, (dc - oc) % 2)]
            total = total + sums_in[sender, at : at + 1, :]
        for h in range(2):
            wts[slot, h : h + 1, :] = 1.0 / total[:, h * PROJ : (h + 1) * PROJ]
        if slot == 0:
            log_sum = jnp.sum(jnp.log(total))
    for slot in range(1, 16):
        dy, dz = COL_OFFS[slot]
        to = COL_OF[neg_col((dy, dz))]
        send(wts.at[0], wts_in.at[to], x_send.at[4], wt_recv.at[to], peer(dy=dy, dz=dz))

    for slot in range(4, 8):
        pos = partners(slot, pos)
    for slot in range(8):
        w_rows[slot * OWN : (slot + 1) * OWN, :] = to_column(wts[slot, 0:1, :], wts[slot, 1:2, :])
    loss_part = log_sum - INV_TAU * jnp.sum(pos)
    me1 = x * 2 + c
    loss1[me1] = jnp.full((1, PROJ), loss_part, F32)
    for slot in range(1, 8):
        dx, dc = ROW_OFFS[slot]
        to = ROW_OF[neg_row((dx, dc))]
        send(loss1.at[me1], loss1.at[me1], x_send.at[5], loss_recv1.at[to], peer(dx=dx, dc=dc))

    def weigh(slot, table):
        block = cols[slot * OWN : (slot + 1) * OWN, :]
        uw[slot * OWN : (slot + 1) * OWN, PROJ : 2 * PROJ] = (
            block.astype(F32) * to_column(table[0:1], table[1:2])
        ).astype(BF16)

    weigh(0, wts[0])
    for slot in range(1, 16):
        wait_bytes(wts_in.at[slot], wt_recv.at[slot])
    for slot in range(1, 16):
        weigh(slot, wts_in[slot])

    def product(slot):
        return jnp.dot(
            expo[slot * OWN : (slot + 1) * OWN, :], uw[...], preferred_element_type=F32
        )

    def terms(slot, both):
        w = w_rows[slot * OWN : (slot + 1) * OWN, :]
        return (
            w * both[:, 0:PROJ] + both[:, PROJ : 2 * PROJ]
            - 2.0 * paired[slot * OWN : (slot + 1) * OWN, :]
        )

    def quad_slot(slot):
        return quad.at[pl.ds(slot * OWN, OWN)]

    def finish(slot, both):
        quad[slot * OWN : (slot + 1) * OWN, :] = terms(slot, both)
        if slot > 3:
            send(
                quad_slot(slot), quad_sib.at[slot - 4], x_send.at[6], qs_recv.at[slot - 4],
                peer(dc=1),
            )

    def complete(slot):
        quad[slot * OWN : (slot + 1) * OWN, :] += quad_sib[slot]
        if slot:
            to = (-slot) % 4
            send(quad_slot(slot), quad_ring.at[to], x_send.at[7], qr_recv.at[to], peer(dx=slot))

    slot, both, ready = None, None, None
    for later in (6, 2, 5, 1, 7, 3, 4, 0):
        if ready is not None:
            wait_bytes(quad_sib.at[ready], qs_recv.at[ready])
        both_later = product(later)
        if ready is not None:
            complete(ready)
        if slot is not None:
            finish(slot, both)
        ready = slot if slot is not None and slot < 4 else None
        slot, both = later, both_later
    finish(slot, both)
    wait_bytes(quad_sib.at[slot], qs_recv.at[slot])
    complete(slot)

    summed = quad[0:OWN, :]
    for d in (1, 3, 2):
        wait_bytes(quad_ring.at[d], qr_recv.at[d])
        summed = summed + quad_ring[d]
    du = INV_TAU * summed
    uu = u_ref[...]
    dz_own[...] = (
        (du - uu * jnp.sum(uu * du, axis=1, keepdims=True)) / norm_ref[...]
    ).astype(BF16)
    send(dz_own, dz_sib, x_send.at[9], dz_recv.at[0], peer(dc=1))

    mine = pl.multiple_of(c * HALF, HALF)
    grad[...] = lax.dot_general(
        feat[:, pl.ds(mine, HALF)], dz_own[...], TN, preferred_element_type=F32
    )
    wait_bytes(feat_sib, feat_recv.at[0])
    wait_bytes(dz_sib, dz_recv.at[0])
    g1_in, g1, g2_in = (g1_in_a, g1_in_b, g1_in_c), (g1_a, g1_b, g1_c), (g2_in_a, g2_in_b, g2_in_c)
    parts = (2, 1, 0)

    def ring_block(part, d, base=0):
        span = 16 * TILES[part]
        first = base + STARTS[part] + torus.ring_at(part, d) * span
        return pl.ds(pl.multiple_of(first, span), span)

    def block_row(part, d1):
        span = 4 * TILES[part]
        return pl.ds(pl.multiple_of(torus.row_at(part, d1) * span, span), span)

    def plane_row(part, d, d1, base=0):
        span = 4 * TILES[part]
        first = base + STARTS[part] + torus.ring_at(part, d) * 4 * span
        return pl.ds(pl.multiple_of(first + torus.row_at(part, d1) * span, span), span)

    for part in (0, 1, 2):
        of = slice(STARTS[part], STARTS[part] + 64 * TILES[part])
        grad[of, :] += lax.dot_general(feat_sib[:, of], dz_sib[...], TN, preferred_element_type=F32)
        for d1 in (2, 1, 3, 0):
            for d in (2, 1, 3):
                at = (-d) % 4
                send(
                    grad.at[plane_row(part, d, d1)], g1_in[part].at[at, block_row(part, d1)],
                    x_send.at[10], g1_recv.at[part, at, d1], torus.ring_peer(part, d),
                )

    for slot in range(1, 8):
        wait_bytes(loss1.at[0], loss_recv1.at[slot])
    total = loss1[0]
    for k in range(1, 8):
        total = total + loss1[k]
    me2 = y * 4 + z
    loss2[me2] = total
    for slot in range(1, 16):
        dy, dz = COL_OFFS[slot]
        to = COL_OF[neg_col((dy, dz))]
        send(loss2.at[me2], loss2.at[me2], x_send.at[8], loss_recv2.at[to], peer(dy=dy, dz=dz))

    for d1 in (2, 1, 3, 0):
        for part in parts:
            rows_of = block_row(part, d1)
            total = grad[plane_row(part, 0, d1), :]
            for d in (1, 3, 2):
                wait_bytes(g1_in[part].at[d, rows_of], g1_recv.at[part, d, d1])
                total = total + g1_in[part][d, rows_of, :]
            g1[part][rows_of, :] = total
            tile = TILES[part]
            for d2 in (2, 1, 3, 0):
                if not (d1 or d2):
                    continue
                to = COL_OF[neg_col((d1, d2))]
                at = pl.multiple_of(torus.plane_at(part, d1, d2) * tile, tile)
                send(
                    g1[part].at[pl.ds(at, tile)], g2_in[part].at[pl.ds(to * tile, tile)],
                    x_send.at[11], g2_recv.at[part], torus.plane_peer(part, d1, d2),
                )
    base = c * HALF
    for part in parts:
        tile = TILES[part]
        place = torus.plane_at(part, 0, 0) * tile
        total = g1[part][pl.ds(pl.multiple_of(place, tile), tile), :]
        wait_bytes(g2_in[part].at[pl.ds(tile, 15 * tile)], g2_recv.at[part])
        for slot in range(1, 16):
            total = total + g2_in[part][slot * tile : (slot + 1) * tile, :]
        first = base + STARTS[part] + torus.ring_at(part, 0) * 16 * tile + place
        at = pl.ds(pl.multiple_of(first, tile), tile)
        out[at, :] = total * (1.0 / VIEWS**0.5)
        for slot in range(15, 0, -1):
            d1, d2 = COL_OFFS[slot]
            send(
                out.at[at], out.at[at], x_send.at[12], ag_recv.at[part, (-d1) % 4],
                torus.plane_peer(part, d1, d2),
            )

    for d1 in (0, 1, 3, 2):
        for part in parts:
            wait_bytes(out.at[pl.ds(0, (4 if d1 else 3) * TILES[part])], ag_recv.at[part, d1])
            block = plane_row(part, 0, d1, base)
            for d in (2, 1, 3):
                send(
                    out.at[block], out.at[block], x_send.at[13],
                    ring_recv.at[part, (-d) % 4, d1], torus.ring_peer(part, d),
                )
    for part in parts:
        block = ring_block(part, 0, base)
        send(out.at[block], out.at[block], x_send.at[14], rel_recv.at[part, 0], peer(dc=1))
    for d1 in (0, 1, 3, 2):
        for d in (1, 3, 2):
            for part in parts:
                block = plane_row(part, d, d1, base)
                wait_bytes(out.at[block], ring_recv.at[part, d, d1])
                send(out.at[block], out.at[block], x_send.at[14], rel_recv.at[part, d], peer(dc=1))

    for slot in range(1, 16):
        wait_bytes(loss2.at[0], loss_recv2.at[slot])
    total = loss2[0]
    for k in range(1, 16):
        total = total + loss2[k]
    loss_ref[...] = total[0:1, 0:1] * (1.0 / VIEWS)

    other = torus.cs[1] * HALF
    for d in (0, 1, 3, 2):
        for part in parts:
            span = 16 * TILES[part]
            ends = (torus.ys[d], torus.xs[d])
            ring = torus.zs[d] if part == 2 else torus.pick(*(ends if part == 0 else ends[::-1]))
            block = pl.ds(pl.multiple_of(other + STARTS[part] + ring * span, span), span)
            wait_bytes(out.at[block], rel_recv.at[part, d])

    for ref, at in sent:
        wait_bytes(ref, x_send.at[at])


def per_device(features, proj_weight, partner):
    dma = pltpu.SemaphoreType.DMA
    grad, loss = pl.pallas_call(
        kernel,
        out_shape=(
            pltpu.VMEM((D, PROJ), F32),
            pltpu.VMEM((1, 1), F32),
        ),
        in_specs=[
            pl.BlockSpec(memory_space=pl.ANY),
            pl.BlockSpec(memory_space=pl.ANY),
            pl.BlockSpec(memory_space=pl.ANY),
        ],
        out_specs=(pl.BlockSpec(memory_space=pltpu.VMEM), pl.BlockSpec(memory_space=pltpu.VMEM)),
        scratch_shapes=[
            pltpu.VMEM((2, PROJ), jnp.int32),
            pltpu.VMEM((OWN, D), BF16),
            pltpu.VMEM((D, PROJ), BF16),
            pltpu.VMEM((OWN, HALF), BF16),
            pltpu.VMEM((OWN, PROJ), F32),
            pltpu.VMEM((OWN, PROJ), F32),
            pltpu.VMEM((8 * SLOT, PROJ), BF16),
            pltpu.VMEM((16 * OWN, PROJ), BF16),
            pltpu.VMEM((8 * OWN, 16 * OWN), BF16),
            pltpu.VMEM((8 * OWN, PROJ), F32),
            pltpu.VMEM((8, OWN), F32),
            pltpu.VMEM((8, 8, OWN), F32),
            pltpu.VMEM((8, 2, PROJ), F32),
            pltpu.VMEM((16, 2, PROJ), F32),
            pltpu.VMEM((OWN, 16 * PROJ), BF16),
            pltpu.VMEM((8 * OWN, PROJ), F32),
            pltpu.VMEM((16 * OWN, 2 * PROJ), BF16),
            pltpu.VMEM((8 * OWN, PROJ), F32),
            pltpu.VMEM((8 * OWN, PROJ), F32),
            pltpu.VMEM((4, OWN, PROJ), F32),
            pltpu.VMEM((4, OWN, PROJ), F32),
            pltpu.VMEM((OWN, PROJ), BF16),
            pltpu.VMEM((OWN, PROJ), BF16),
            pltpu.VMEM((HALF, PROJ), F32),
            *[pltpu.VMEM((4, 16 * tile, PROJ), F32) for tile in TILES],
            *[pltpu.VMEM((16 * tile, PROJ), F32) for tile in TILES],
            *[pltpu.VMEM((16 * tile, PROJ), F32) for tile in TILES],
            pltpu.VMEM((8, 1, PROJ), F32),
            pltpu.VMEM((16, 1, PROJ), F32),
            dma((9,)),
            dma((15,)),
            dma((16, 2)),
            dma((8,)),
            dma((1,)),
            dma((8,)),
            dma((16,)),
            dma((8,)),
            dma((16,)),
            dma((4,)),
            dma((4,)),
            dma((1,)),
            dma((3, 4, 4)),
            dma((3,)),
            dma((3, 4)),
            dma((3, 4, 4)),
            dma((3, 4)),
        ],
        compiler_params=pltpu.CompilerParams(
            collective_id=0, has_side_effects=True, vmem_limit_bytes=56 * 2**20
        ),
        name="simclr_head",
    )(features, proj_weight, partner.reshape(2, PROJ))
    return loss.reshape(()), grad


def solution(mesh):
    placed = (P(("dp", "inner"), None), P(), P(("dp", "inner")))
    return jax.shard_map(
        per_device, mesh=mesh, in_specs=placed, out_specs=(P(), P()), check_vma=False
    )
```

```python
import jax
import jax.numpy as jnp
from jax import lax
from jax.experimental import pallas as pl
from jax.experimental.pallas import tpu as pltpu
from jax.sharding import PartitionSpec as P

MESH = pl.DeviceIdType.MESH
F32 = jnp.float32
BF16 = jnp.bfloat16
VIEWS = 32768
D = 4096
HALF = D // 2
QUARTER = D // 4
PROJ = 128
OWN = 256
RINGS = 7
GROUPS = ((RINGS, 11), (11, 14), (14, 16))
SLOT = OWN + 16
INV_TAU = 5.0
SCALE2 = INV_TAU * 1.4426950408889634
NT = (((1,), (1,)), ((), ()))
TN = (((0,), (0,)), ((), ()))

ROW_OFFS = [(dx, dc) for dc in range(2) for dx in range(4)]
ROW_OF = {off: slot for slot, off in enumerate(ROW_OFFS)}
COL_OFFS = sorted(
    [(dy, dz) for dy in range(4) for dz in range(4)],
    key=lambda o: (0 not in o, min(o[0], 4 - o[0]) + min(o[1], 4 - o[1]), o),
)
COL_OF = {off: slot for slot, off in enumerate(COL_OFFS)}
RING_AXIS = {slot: int(off[0] == 0) for slot, off in enumerate(COL_OFFS) if slot and 0 in off}
TILES = (16, 8, 8)
STARTS = (0, 1024, 1536)


def neg_col(off):
    return ((-off[0]) % 4, (-off[1]) % 4)


def neg_row(off):
    return ((-off[0]) % 4, off[1])


def coords():
    dp, inner = lax.axis_index("dp"), lax.axis_index("inner")
    x = (inner % 2) * 2 + dp // 8
    return x, (dp // 2) % 4, inner // 2, dp % 2


def device_at(x, y, z, c):
    return ((x % 2) * 8 + y * 2 + c, z * 2 + x // 2)


class Torus:
    def __init__(self):
        x, y, z, c = coords()
        self.xs, self.ys, self.zs = ([(v + d) % 4 for d in range(4)] for v in (x, y, z))
        self.cs = [c, 1 - c]
        self.x_dp = [v % 2 * 8 for v in self.xs]
        self.x_inner = [v // 2 for v in self.xs]
        self.y_dp = [v * 2 for v in self.ys]
        self.z_inner = [v * 2 for v in self.zs]

    def peer(self, dx=0, dy=0, dz=0, dc=0):
        return (
            self.x_dp[dx] + self.y_dp[dy] + self.cs[dc],
            self.z_inner[dz] + self.x_inner[dx],
        )

    def pick(self, a, b):
        return a * self.cs[1] + b * self.cs[0]

    def pick_peer(self, a, b):
        return self.pick(a[0], b[0]), self.pick(a[1], b[1])

    def ring_at(self, part, d):
        if part == 2:
            return self.zs[d]
        ends = (self.xs[d], self.ys[d])
        return self.pick(*(ends if part == 0 else ends[::-1]))

    def row_at(self, part, d1):
        if part == 2:
            return self.xs[d1]
        ends = (self.ys[d1], self.xs[d1])
        return self.pick(*(ends if part == 0 else ends[::-1]))

    def plane_at(self, part, d1, d2):
        if part == 2:
            return self.xs[d1] * 4 + self.ys[d2]
        ends = (self.ys[d1], self.xs[d1])
        return self.pick(*(ends if part == 0 else ends[::-1])) * 4 + self.zs[d2]

    def ring_peer(self, part, d):
        if part == 2:
            return self.peer(dz=d)
        ends = (self.peer(dx=d), self.peer(dy=d))
        return self.pick_peer(*(ends if part == 0 else ends[::-1]))

    def plane_peer(self, part, d1, d2):
        if part == 2:
            return self.peer(dx=d1, dy=d2)
        ends = (self.peer(dy=d1, dz=d2), self.peer(dx=d1, dz=d2))
        return self.pick_peer(*(ends if part == 0 else ends[::-1]))


def ring_peers():
    offs = [off for d in (2, 1, 3) for off in ((d, 0, 0, 0), (0, d, 0, 0), (0, 0, d, 0))]
    return offs + [(0, 0, 0, 1)]


def send(src, dst, send_sem, recv_sem, device):
    copy = pltpu.make_async_remote_copy(
        src_ref=src, dst_ref=dst, send_sem=send_sem, recv_sem=recv_sem,
        device_id=device, device_id_type=MESH,
    )
    copy.start()


def wait_bytes(ref, sem):
    pltpu.make_async_copy(ref, ref, sem).wait()


def kernel(
    f_hbm, w_hbm, partner_hbm, out, loss_ref,
    partner_ref, feat, weight, feat_sib, u_ref, norm_ref, rows, cols, expo, acc,
    sums, sums_in, wts, wts_in, wide, paired, uw, w_rows, quad, quad_sib, quad_ring,
    dz_own, dz_sib, grad, g1_in_a, g1_in_b, g1_in_c, g1_a, g1_b, g1_c,
    g2_in_a, g2_in_b, g2_in_c, loss1, loss2,
    load_sem, x_send, col_recv, row_recv, feat_recv, sum_recv, wt_recv, loss_recv1, loss_recv2,
    qs_recv, qr_recv, dz_recv, g1_recv, g2_recv, ag_recv, ring_recv, rel_recv,
):
    sent = [
        (rows.at[pl.ds(0, 7 * SLOT)], 0),
        (cols.at[pl.ds(0, 15 * OWN)], 1),
        (feat_sib, 2),
        (sums_in.at[pl.ds(0, 7)], 3),
        (wts_in.at[pl.ds(0, 15)], 4),
        (loss1.at[pl.ds(0, 7)], 5),
        (quad_sib, 6),
        (quad_ring.at[pl.ds(0, 3)], 7),
        (loss2.at[pl.ds(0, 15)], 8),
        (dz_sib, 9),
        (grad.at[pl.ds(0, 3 * HALF // 4)], 10),
        (grad.at[pl.ds(0, 15 * sum(TILES))], 11),
        (grad.at[pl.ds(0, 15 * sum(TILES))], 12),
        (grad.at[pl.ds(0, 3 * HALF // 4)], 13),
        (grad, 14),
    ]
    torus = Torus()
    peer = torus.peer
    x, y, z, c = torus.xs[0], torus.ys[0], torus.zs[0], torus.cs[0]
    loads = []
    for k in range(4):
        depth = pl.ds(k * QUARTER, QUARTER)
        loads.append(
            (
                pltpu.make_async_copy(w_hbm.at[depth], weight.at[depth], load_sem.at[k]),
                pltpu.make_async_copy(f_hbm.at[:, depth], feat.at[:, depth], load_sem.at[4 + k]),
            )
        )
    load_partner = pltpu.make_async_copy(partner_hbm, partner_ref, load_sem.at[8])
    load_partner.start()
    for pair in loads:
        for load in pair:
            load.start()
    barrier = pltpu.get_barrier_semaphore()
    peers = ring_peers()
    for off in peers:
        pl.semaphore_signal(barrier, inc=1, device_id=peer(*off), device_id_type=MESH)

    load_partner.wait()
    owner_of, place_of = partner_ref[...] // OWN, partner_ref[...] % OWN
    at = lax.broadcasted_iota(jnp.int32, (16, PROJ), 0)
    code = jnp.zeros((16, PROJ), F32)
    for k, row in enumerate((owner_of[0:1], owner_of[1:2], place_of[0:1], place_of[1:2])):
        code = jnp.where(at == k, row.astype(F32), code)
    rows[OWN:SLOT, :] = code.astype(BF16)

    zed = None
    for k, pair in enumerate(loads):
        for load in pair:
            load.wait()
        term = jnp.dot(
            feat[:, k * QUARTER : (k + 1) * QUARTER], weight[k * QUARTER : (k + 1) * QUARTER, :],
            preferred_element_type=F32,
        )
        zed = term if zed is None else zed + term
    norm = jnp.sqrt(jnp.sum(zed * zed, axis=1, keepdims=True) + 1e-06)
    u = zed / norm
    u_ref[...] = u
    norm_ref[...] = jnp.broadcast_to(norm, (OWN, PROJ))
    ub = u.astype(BF16)
    rows[0:OWN, :] = ub
    cols[0:OWN, :] = ub
    pl.semaphore_wait(barrier, len(peers))

    def row_slot(slot):
        return rows.at[pl.ds(slot * SLOT, SLOT)]

    def col_slot(slot):
        return cols.at[pl.ds(slot * OWN, OWN)]

    def col_half(slot, half):
        return cols.at[pl.ds(slot * OWN + half * (OWN // 2), OWN // 2)]

    for dx in (1, 3, 2):
        to = ROW_OF[neg_row((dx, 0))]
        send(row_slot(0), row_slot(to), x_send.at[0], row_recv.at[to], peer(dx=dx))
    send(row_slot(0), row_slot(4), x_send.at[0], row_recv.at[4], peer(dc=1))
    for turn in range(2):
        for d in (1, 3, 2):
            for axis in range(2):
                half = axis ^ turn
                off = (d, 0) if axis == 0 else (0, d)
                to = COL_OF[neg_col(off)]
                send(
                    col_half(0, half), col_half(to, half), x_send.at[1],
                    col_recv.at[to, half], peer(dy=off[0], dz=off[1]),
                )

    def pass_on(axis, d):
        off = (d, 0) if axis == 0 else (0, d)
        slot = COL_OF[off]
        wait_bytes(col_half(slot, axis), col_recv.at[slot, axis])
        for e in (1, 3, 2):
            hop = (0, e) if axis == 0 else (e, 0)
            to = COL_OF[((off[0] - hop[0]) % 4, (off[1] - hop[1]) % 4)]
            send(
                col_half(slot, axis), col_half(to, axis), x_send.at[1],
                col_recv.at[to, axis], peer(dy=hop[0], dz=hop[1]),
            )

    def pass_row(slot):
        wait_bytes(row_slot(slot), row_recv.at[slot])
        send(row_slot(slot), row_slot(4 + slot), x_send.at[0], row_recv.at[4 + slot], peer(dc=1))

    def lanes(e):
        total = e[:, 0:PROJ]
        for q in range(1, e.shape[1] // PROJ):
            total = total + e[:, q * PROJ : (q + 1) * PROJ]
        return total

    def scores(slot, first, end):
        return jnp.exp2(
            lax.dot_general(
                rows[slot * SLOT : slot * SLOT + OWN, :], cols[first * OWN : end * OWN, :], NT,
                preferred_element_type=F32,
            )
            * SCALE2
        )

    def pass1(slot, first, end):
        e = scores(slot, first, end)
        if slot == 0 and first == 0:
            at_row = lax.broadcasted_iota(jnp.int32, e.shape, 0)
            at_col = lax.broadcasted_iota(jnp.int32, e.shape, 1)
            e = jnp.where(at_row == at_col, 0.0, e)
        of = slice(slot * OWN, (slot + 1) * OWN)
        expo[of, first * OWN : end * OWN] = e.astype(BF16)
        if first == 0:
            acc[of, :] = lanes(e)
        else:
            acc[of, :] += lanes(e)

    def wait_ring(slot):
        half = 1 - RING_AXIS[slot]
        wait_bytes(col_half(slot, half), col_recv.at[slot, half])

    for d in (1, 3):
        pass_on(0, d)
        pass_on(1, d)
        pass_row(d)
    pass_on(0, 2)
    pass_on(1, 2)
    wait_bytes(row_slot(4), row_recv.at[4])
    for slot in range(1, 4):
        wait_ring(slot)
    for slot in (0, 4, 1, 3):
        pass1(slot, 0, 4)
    pass_row(2)
    send(
        feat.at[:, pl.ds(pl.multiple_of((1 - c) * HALF, HALF), HALF)], feat_sib,
        x_send.at[2], feat_recv.at[0], peer(dc=1),
    )
    for slot in range(4, RINGS):
        wait_ring(slot)
    for slot in (0, 4, 1, 3):
        pass1(slot, 4, RINGS)
    for slot in (5, 7, 6):
        wait_bytes(row_slot(slot), row_recv.at[slot])
    for slot in (5, 7, 2, 6):
        pass1(slot, 0, RINGS)
    for first, end in GROUPS:
        for slot in range(first, end):
            for half in range(2):
                wait_bytes(col_half(slot, half), col_recv.at[slot, half])
        for slot in range(8):
            pass1(slot, first, end)

    eye = lax.broadcasted_iota(jnp.int32, (PROJ, PROJ), 0) == lax.broadcasted_iota(
        jnp.int32, (PROJ, PROJ), 1
    )

    def to_row(column):
        return jnp.sum(jnp.where(eye, column, 0.0), axis=0, keepdims=True)

    def to_column(*rows_of):
        halves = [
            jnp.sum(jnp.where(eye, row, 0.0), axis=1, keepdims=True) for row in rows_of
        ]
        return jnp.broadcast_to(jnp.concatenate(halves, axis=0), (OWN, PROJ))

    for slot in range(8):
        for h in range(2):
            first = slot * OWN + h * PROJ
            column = jnp.sum(acc[first : first + PROJ, :], axis=1, keepdims=True)
            sums[slot : slot + 1, h * PROJ : (h + 1) * PROJ] = to_row(column)
    for slot in (2, 6, 1, 3, 5, 7, 4):
        dx, dc = ROW_OFFS[slot]
        to = ROW_OF[neg_row((dx, dc))]
        send(sums, sums_in.at[to], x_send.at[3], sum_recv.at[to], peer(dx=dx, dc=dc))

    for slot in range(16):
        block = cols[slot * OWN : (slot + 1) * OWN, :]
        wide[:, slot * PROJ : (slot + 1) * PROJ] = block
        uw[slot * OWN : (slot + 1) * OWN, 0:PROJ] = block
    lane = lax.broadcasted_iota(jnp.int32, (OWN, PROJ), 1).astype(F32)

    def partners(slot, pos):
        code = rows[slot * SLOT + OWN : (slot + 1) * SLOT, :].astype(F32)
        owner = to_column(code[0:1], code[1:2])
        place = to_column(code[2:3], code[3:4])
        hot = jnp.concatenate(
            [jnp.where(place == lane, 1.0, 0.0), jnp.where(place == lane + PROJ, 1.0, 0.0)], axis=1
        ).astype(BF16)
        found = jnp.dot(hot, wide[...], preferred_element_type=F32)
        total = jnp.zeros((OWN, PROJ), F32)
        for k in range(16):
            dy, dz = COL_OFFS[k]
            dp, inner = peer(dy=dy, dz=dz)
            here = (dp * 8 + inner).astype(F32)
            total = total + jnp.where(owner == here, found[:, k * PROJ : (k + 1) * PROJ], 0.0)
        paired[slot * OWN : (slot + 1) * OWN, :] = total
        own = rows[slot * SLOT : slot * SLOT + OWN, :].astype(F32)
        return pos + own * total

    pos = jnp.zeros((OWN, PROJ), F32)
    for slot in range(4):
        pos = partners(slot, pos)

    for slot in range(1, 8):
        wait_bytes(sums_in.at[slot], sum_recv.at[slot])
    for slot in range(8):
        dx, dc = ROW_OFFS[slot]
        total = sums[slot : slot + 1, :]
        for sender in range(1, 8):
            ox, oc = ROW_OFFS[sender]
            at = ROW_OF[((dx - ox) % 4, (dc - oc) % 2)]
            total = total + sums_in[sender, at : at + 1, :]
        for h in range(2):
            wts[slot, h : h + 1, :] = 1.0 / total[:, h * PROJ : (h + 1) * PROJ]
        if slot == 0:
            log_sum = jnp.sum(jnp.log(total))
    for slot in range(1, 16):
        dy, dz = COL_OFFS[slot]
        to = COL_OF[neg_col((dy, dz))]
        send(wts.at[0], wts_in.at[to], x_send.at[4], wt_recv.at[to], peer(dy=dy, dz=dz))

    for slot in range(4, 8):
        pos = partners(slot, pos)
    for slot in range(8):
        w_rows[slot * OWN : (slot + 1) * OWN, :] = to_column(wts[slot, 0:1, :], wts[slot, 1:2, :])
    loss_part = log_sum - INV_TAU * jnp.sum(pos)
    me1 = x * 2 + c
    loss1[me1] = jnp.full((1, PROJ), loss_part, F32)
    for slot in range(1, 8):
        dx, dc = ROW_OFFS[slot]
        to = ROW_OF[neg_row((dx, dc))]
        send(loss1.at[me1], loss1.at[me1], x_send.at[5], loss_recv1.at[to], peer(dx=dx, dc=dc))

    def weigh(slot, table):
        block = cols[slot * OWN : (slot + 1) * OWN, :]
        uw[slot * OWN : (slot + 1) * OWN, PROJ : 2 * PROJ] = (
            block.astype(F32) * to_column(table[0:1], table[1:2])
        ).astype(BF16)

    weigh(0, wts[0])
    for slot in range(1, 16):
        wait_bytes(wts_in.at[slot], wt_recv.at[slot])
    for slot in range(1, 16):
        weigh(slot, wts_in[slot])

    def product(slot):
        return jnp.dot(
            expo[slot * OWN : (slot + 1) * OWN, :], uw[...], preferred_element_type=F32
        )

    def terms(slot, both):
        w = w_rows[slot * OWN : (slot + 1) * OWN, :]
        return (
            w * both[:, 0:PROJ] + both[:, PROJ : 2 * PROJ]
            - 2.0 * paired[slot * OWN : (slot + 1) * OWN, :]
        )

    def quad_slot(slot):
        return quad.at[pl.ds(slot * OWN, OWN)]

    def finish(slot, both):
        quad[slot * OWN : (slot + 1) * OWN, :] = terms(slot, both)
        if slot > 3:
            send(
                quad_slot(slot), quad_sib.at[slot - 4], x_send.at[6], qs_recv.at[slot - 4],
                peer(dc=1),
            )

    def complete(slot):
        quad[slot * OWN : (slot + 1) * OWN, :] += quad_sib[slot]
        if slot:
            to = (-slot) % 4
            send(quad_slot(slot), quad_ring.at[to], x_send.at[7], qr_recv.at[to], peer(dx=slot))

    def add_sibling(slot):
        wait_bytes(quad_sib.at[slot], qs_recv.at[slot])
        complete(slot)

    finish(6, product(6))
    finish(2, product(2))
    add_sibling(2)
    slot, both = 5, product(5)
    for later in (7, 1, 3):
        both_later = product(later)
        finish(slot, both)
        slot, both = later, both_later
    add_sibling(1)
    finish(3, both)
    add_sibling(3)
    both, both_later = product(4), product(0)
    finish(4, both)
    finish(0, both_later)
    add_sibling(0)

    summed = quad[0:OWN, :]
    for d in (1, 3, 2):
        wait_bytes(quad_ring.at[d], qr_recv.at[d])
        summed = summed + quad_ring[d]
    du = INV_TAU * summed
    uu = u_ref[...]
    dz_own[...] = (
        (du - uu * jnp.sum(uu * du, axis=1, keepdims=True)) / norm_ref[...]
    ).astype(BF16)
    send(dz_own, dz_sib, x_send.at[9], dz_recv.at[0], peer(dc=1))

    mine = pl.multiple_of(c * HALF, HALF)
    grad[...] = lax.dot_general(
        feat[:, pl.ds(mine, HALF)], dz_own[...], TN, preferred_element_type=F32
    )
    wait_bytes(feat_sib, feat_recv.at[0])
    wait_bytes(dz_sib, dz_recv.at[0])
    g1_in, g1, g2_in = (g1_in_a, g1_in_b, g1_in_c), (g1_a, g1_b, g1_c), (g2_in_a, g2_in_b, g2_in_c)
    parts = (2, 1, 0)

    def ring_block(part, d, base=0):
        span = 16 * TILES[part]
        first = base + STARTS[part] + torus.ring_at(part, d) * span
        return pl.ds(pl.multiple_of(first, span), span)

    def block_row(part, d1):
        span = 4 * TILES[part]
        return pl.ds(pl.multiple_of(torus.row_at(part, d1) * span, span), span)

    def plane_row(part, d, d1, base=0):
        span = 4 * TILES[part]
        first = base + STARTS[part] + torus.ring_at(part, d) * 4 * span
        return pl.ds(pl.multiple_of(first + torus.row_at(part, d1) * span, span), span)

    for part in (0, 1, 2):
        of = slice(STARTS[part], STARTS[part] + 64 * TILES[part])
        grad[of, :] += lax.dot_general(feat_sib[:, of], dz_sib[...], TN, preferred_element_type=F32)
        for d1 in (2, 1, 3, 0):
            for d in (2, 1, 3):
                at = (-d) % 4
                send(
                    grad.at[plane_row(part, d, d1)], g1_in[part].at[at, block_row(part, d1)],
                    x_send.at[10], g1_recv.at[part, at, d1], torus.ring_peer(part, d),
                )

    for slot in range(1, 8):
        wait_bytes(loss1.at[0], loss_recv1.at[slot])
    total = loss1[0]
    for k in range(1, 8):
        total = total + loss1[k]
    me2 = y * 4 + z
    loss2[me2] = total
    for slot in range(1, 16):
        dy, dz = COL_OFFS[slot]
        to = COL_OF[neg_col((dy, dz))]
        send(loss2.at[me2], loss2.at[me2], x_send.at[8], loss_recv2.at[to], peer(dy=dy, dz=dz))

    for d1 in (2, 1, 3, 0):
        for part in parts:
            rows_of = block_row(part, d1)
            total = grad[plane_row(part, 0, d1), :]
            for d in (1, 3, 2):
                wait_bytes(g1_in[part].at[d, rows_of], g1_recv.at[part, d, d1])
                total = total + g1_in[part][d, rows_of, :]
            g1[part][rows_of, :] = total
            tile = TILES[part]
            for d2 in (2, 1, 3, 0):
                if not (d1 or d2):
                    continue
                to = COL_OF[neg_col((d1, d2))]
                at = pl.multiple_of(torus.plane_at(part, d1, d2) * tile, tile)
                send(
                    g1[part].at[pl.ds(at, tile)], g2_in[part].at[pl.ds(to * tile, tile)],
                    x_send.at[11], g2_recv.at[part], torus.plane_peer(part, d1, d2),
                )
    base = c * HALF
    for part in parts:
        tile = TILES[part]
        place = torus.plane_at(part, 0, 0) * tile
        total = g1[part][pl.ds(pl.multiple_of(place, tile), tile), :]
        wait_bytes(g2_in[part].at[pl.ds(tile, 15 * tile)], g2_recv.at[part])
        for slot in range(1, 16):
            total = total + g2_in[part][slot * tile : (slot + 1) * tile, :]
        first = base + STARTS[part] + torus.ring_at(part, 0) * 16 * tile + place
        at = pl.ds(pl.multiple_of(first, tile), tile)
        out[at, :] = total * (1.0 / VIEWS**0.5)
        for slot in range(15, 0, -1):
            d1, d2 = COL_OFFS[slot]
            send(
                out.at[at], out.at[at], x_send.at[12], ag_recv.at[part, (-d1) % 4],
                torus.plane_peer(part, d1, d2),
            )

    for d1 in (0, 1, 3, 2):
        for part in parts:
            wait_bytes(out.at[pl.ds(0, (4 if d1 else 3) * TILES[part])], ag_recv.at[part, d1])
            block = plane_row(part, 0, d1, base)
            for d in (2, 1, 3):
                send(
                    out.at[block], out.at[block], x_send.at[13],
                    ring_recv.at[part, (-d) % 4, d1], torus.ring_peer(part, d),
                )
    for part in parts:
        block = ring_block(part, 0, base)
        send(out.at[block], out.at[block], x_send.at[14], rel_recv.at[part, 0], peer(dc=1))
    for d1 in (0, 1, 3, 2):
        for d in (1, 3, 2):
            for part in parts:
                block = plane_row(part, d, d1, base)
                wait_bytes(out.at[block], ring_recv.at[part, d, d1])
                send(out.at[block], out.at[block], x_send.at[14], rel_recv.at[part, d], peer(dc=1))

    for slot in range(1, 16):
        wait_bytes(loss2.at[0], loss_recv2.at[slot])
    total = loss2[0]
    for k in range(1, 16):
        total = total + loss2[k]
    loss_ref[...] = total[0:1, 0:1] * (1.0 / VIEWS)

    other = torus.cs[1] * HALF
    for d in (0, 1, 3, 2):
        for part in parts:
            span = 16 * TILES[part]
            ends = (torus.ys[d], torus.xs[d])
            ring = torus.zs[d] if part == 2 else torus.pick(*(ends if part == 0 else ends[::-1]))
            block = pl.ds(pl.multiple_of(other + STARTS[part] + ring * span, span), span)
            wait_bytes(out.at[block], rel_recv.at[part, d])

    for ref, at in sent:
        wait_bytes(ref, x_send.at[at])


def per_device(features, proj_weight, partner):
    dma = pltpu.SemaphoreType.DMA
    grad, loss = pl.pallas_call(
        kernel,
        out_shape=(
            pltpu.VMEM((D, PROJ), F32),
            pltpu.VMEM((1, 1), F32),
        ),
        in_specs=[
            pl.BlockSpec(memory_space=pl.ANY),
            pl.BlockSpec(memory_space=pl.ANY),
            pl.BlockSpec(memory_space=pl.ANY),
        ],
        out_specs=(pl.BlockSpec(memory_space=pltpu.VMEM), pl.BlockSpec(memory_space=pltpu.VMEM)),
        scratch_shapes=[
            pltpu.VMEM((2, PROJ), jnp.int32),
            pltpu.VMEM((OWN, D), BF16),
            pltpu.VMEM((D, PROJ), BF16),
            pltpu.VMEM((OWN, HALF), BF16),
            pltpu.VMEM((OWN, PROJ), F32),
            pltpu.VMEM((OWN, PROJ), F32),
            pltpu.VMEM((8 * SLOT, PROJ), BF16),
            pltpu.VMEM((16 * OWN, PROJ), BF16),
            pltpu.VMEM((8 * OWN, 16 * OWN), BF16),
            pltpu.VMEM((8 * OWN, PROJ), F32),
            pltpu.VMEM((8, OWN), F32),
            pltpu.VMEM((8, 8, OWN), F32),
            pltpu.VMEM((8, 2, PROJ), F32),
            pltpu.VMEM((16, 2, PROJ), F32),
            pltpu.VMEM((OWN, 16 * PROJ), BF16),
            pltpu.VMEM((8 * OWN, PROJ), F32),
            pltpu.VMEM((16 * OWN, 2 * PROJ), BF16),
            pltpu.VMEM((8 * OWN, PROJ), F32),
            pltpu.VMEM((8 * OWN, PROJ), F32),
            pltpu.VMEM((4, OWN, PROJ), F32),
            pltpu.VMEM((4, OWN, PROJ), F32),
            pltpu.VMEM((OWN, PROJ), BF16),
            pltpu.VMEM((OWN, PROJ), BF16),
            pltpu.VMEM((HALF, PROJ), F32),
            *[pltpu.VMEM((4, 16 * tile, PROJ), F32) for tile in TILES],
            *[pltpu.VMEM((16 * tile, PROJ), F32) for tile in TILES],
            *[pltpu.VMEM((16 * tile, PROJ), F32) for tile in TILES],
            pltpu.VMEM((8, 1, PROJ), F32),
            pltpu.VMEM((16, 1, PROJ), F32),
            dma((9,)),
            dma((15,)),
            dma((16, 2)),
            dma((8,)),
            dma((1,)),
            dma((8,)),
            dma((16,)),
            dma((8,)),
            dma((16,)),
            dma((4,)),
            dma((4,)),
            dma((1,)),
            dma((3, 4, 4)),
            dma((3,)),
            dma((3, 4)),
            dma((3, 4, 4)),
            dma((3, 4)),
        ],
        compiler_params=pltpu.CompilerParams(
            collective_id=0, has_side_effects=True, vmem_limit_bytes=56 * 2**20
        ),
        name="simclr_head",
    )(features, proj_weight, partner.reshape(2, PROJ))
    return loss.reshape(()), grad


def solution(mesh):
    placed = (P(("dp", "inner"), None), P(), P(("dp", "inner")))
    return jax.shard_map(
        per_device, mesh=mesh, in_specs=placed, out_specs=(P(), P()), check_vma=False
    )
```

```python
import jax
import jax.numpy as jnp
from jax import lax
from jax.experimental import pallas as pl
from jax.experimental.pallas import tpu as pltpu
from jax.sharding import PartitionSpec as P

MESH = pl.DeviceIdType.MESH
F32 = jnp.float32
BF16 = jnp.bfloat16
VIEWS = 32768
D = 4096
HALF = D // 2
QUARTER = D // 4
PROJ = 128
OWN = 256
RINGS = 7
GROUPS = ((RINGS, 11), (11, 14), (14, 16))
SLOT = OWN + 16
INV_TAU = 5.0
SCALE2 = INV_TAU * 1.4426950408889634
NT = (((1,), (1,)), ((), ()))
TN = (((0,), (0,)), ((), ()))

ROW_OFFS = [(dx, dc) for dc in range(2) for dx in range(4)]
ROW_OF = {off: slot for slot, off in enumerate(ROW_OFFS)}
COL_OFFS = sorted(
    [(dy, dz) for dy in range(4) for dz in range(4)],
    key=lambda o: (0 not in o, min(o[0], 4 - o[0]) + min(o[1], 4 - o[1]), o),
)
COL_OF = {off: slot for slot, off in enumerate(COL_OFFS)}
RING_AXIS = {slot: int(off[0] == 0) for slot, off in enumerate(COL_OFFS) if slot and 0 in off}
TILES = (16, 8, 8)
STARTS = (0, 1024, 1536)


def neg_col(off):
    return ((-off[0]) % 4, (-off[1]) % 4)


def neg_row(off):
    return ((-off[0]) % 4, off[1])


def coords():
    dp, inner = lax.axis_index("dp"), lax.axis_index("inner")
    x = (inner % 2) * 2 + dp // 8
    return x, (dp // 2) % 4, inner // 2, dp % 2


def device_at(x, y, z, c):
    return ((x % 2) * 8 + y * 2 + c, z * 2 + x // 2)


class Torus:
    def __init__(self):
        x, y, z, c = coords()
        self.xs, self.ys, self.zs = ([(v + d) % 4 for d in range(4)] for v in (x, y, z))
        self.cs = [c, 1 - c]
        self.x_dp = [v % 2 * 8 for v in self.xs]
        self.x_inner = [v // 2 for v in self.xs]
        self.y_dp = [v * 2 for v in self.ys]
        self.z_inner = [v * 2 for v in self.zs]

    def peer(self, dx=0, dy=0, dz=0, dc=0):
        return (
            self.x_dp[dx] + self.y_dp[dy] + self.cs[dc],
            self.z_inner[dz] + self.x_inner[dx],
        )

    def pick(self, a, b):
        return a * self.cs[1] + b * self.cs[0]

    def pick_peer(self, a, b):
        return self.pick(a[0], b[0]), self.pick(a[1], b[1])

    def ring_at(self, part, d):
        if part == 2:
            return self.zs[d]
        ends = (self.xs[d], self.ys[d])
        return self.pick(*(ends if part == 0 else ends[::-1]))

    def row_at(self, part, d1):
        if part == 2:
            return self.xs[d1]
        ends = (self.ys[d1], self.xs[d1])
        return self.pick(*(ends if part == 0 else ends[::-1]))

    def plane_at(self, part, d1, d2):
        if part == 2:
            return self.xs[d1] * 4 + self.ys[d2]
        ends = (self.ys[d1], self.xs[d1])
        return self.pick(*(ends if part == 0 else ends[::-1])) * 4 + self.zs[d2]

    def ring_peer(self, part, d):
        if part == 2:
            return self.peer(dz=d)
        ends = (self.peer(dx=d), self.peer(dy=d))
        return self.pick_peer(*(ends if part == 0 else ends[::-1]))

    def plane_peer(self, part, d1, d2):
        if part == 2:
            return self.peer(dx=d1, dy=d2)
        ends = (self.peer(dy=d1, dz=d2), self.peer(dx=d1, dz=d2))
        return self.pick_peer(*(ends if part == 0 else ends[::-1]))


def ring_peers():
    offs = [off for d in (2, 1, 3) for off in ((d, 0, 0, 0), (0, d, 0, 0), (0, 0, d, 0))]
    return offs + [(0, 0, 0, 1)]


def send(src, dst, send_sem, recv_sem, device):
    copy = pltpu.make_async_remote_copy(
        src_ref=src, dst_ref=dst, send_sem=send_sem, recv_sem=recv_sem,
        device_id=device, device_id_type=MESH,
    )
    copy.start()


def wait_bytes(ref, sem):
    pltpu.make_async_copy(ref, ref, sem).wait()


def kernel(
    f_hbm, w_hbm, partner_hbm, out, loss_ref,
    partner_ref, feat, weight, feat_sib, u_ref, norm_ref, rows, cols, expo, acc,
    sums, sums_in, wts, wts_in, wide, paired, uw, w_rows, quad, quad_sib, quad_ring,
    dz_own, dz_sib, grad, g1_in_a, g1_in_b, g1_in_c, g1_a, g1_b, g1_c,
    g2_in_a, g2_in_b, g2_in_c, loss1, loss2,
    load_sem, x_send, col_recv, row_recv, feat_recv, sum_recv, wt_recv, loss_recv1, loss_recv2,
    qs_recv, qr_recv, dz_recv, g1_recv, g2_recv, ag_recv, ring_recv, rel_recv,
):
    sent = [
        (rows.at[pl.ds(0, 7 * SLOT)], 0),
        (cols.at[pl.ds(0, 15 * OWN)], 1),
        (feat_sib, 2),
        (sums_in.at[pl.ds(0, 7)], 3),
        (wts_in.at[pl.ds(0, 15)], 4),
        (loss1.at[pl.ds(0, 7)], 5),
        (quad_sib, 6),
        (quad_ring.at[pl.ds(0, 3)], 7),
        (loss2.at[pl.ds(0, 15)], 8),
        (dz_sib, 9),
        (grad.at[pl.ds(0, 3 * HALF // 4)], 10),
        (grad.at[pl.ds(0, 15 * sum(TILES))], 11),
        (grad.at[pl.ds(0, 15 * sum(TILES))], 12),
        (grad.at[pl.ds(0, 3 * HALF // 4)], 13),
        (grad, 14),
    ]
    torus = Torus()
    peer = torus.peer
    x, y, z, c = torus.xs[0], torus.ys[0], torus.zs[0], torus.cs[0]
    loads = []
    for k in range(4):
        depth = pl.ds(k * QUARTER, QUARTER)
        loads.append(
            (
                pltpu.make_async_copy(w_hbm.at[depth], weight.at[depth], load_sem.at[k]),
                pltpu.make_async_copy(f_hbm.at[:, depth], feat.at[:, depth], load_sem.at[4 + k]),
            )
        )
    barrier = pltpu.get_barrier_semaphore()
    peers = ring_peers()
    for off in peers:
        pl.semaphore_signal(barrier, inc=1, device_id=peer(*off), device_id_type=MESH)

    load_partner = pltpu.make_async_copy(partner_hbm, partner_ref, load_sem.at[8])
    load_partner.start()
    for pair in loads:
        for load in pair:
            load.start()
    load_partner.wait()
    owner_of, place_of = partner_ref[...] // OWN, partner_ref[...] % OWN
    at = lax.broadcasted_iota(jnp.int32, (16, PROJ), 0)
    code = jnp.zeros((16, PROJ), F32)
    for k, row in enumerate((owner_of[0:1], owner_of[1:2], place_of[0:1], place_of[1:2])):
        code = jnp.where(at == k, row.astype(F32), code)
    rows[OWN:SLOT, :] = code.astype(BF16)

    zed = None
    for k, pair in enumerate(loads):
        for load in pair:
            load.wait()
        term = jnp.dot(
            feat[:, k * QUARTER : (k + 1) * QUARTER], weight[k * QUARTER : (k + 1) * QUARTER, :],
            preferred_element_type=F32,
        )
        zed = term if zed is None else zed + term
    norm = jnp.sqrt(jnp.sum(zed * zed, axis=1, keepdims=True) + 1e-06)
    u = zed / norm
    u_ref[...] = u
    norm_ref[...] = jnp.broadcast_to(norm, (OWN, PROJ))
    ub = u.astype(BF16)
    rows[0:OWN, :] = ub
    cols[0:OWN, :] = ub
    pl.semaphore_wait(barrier, len(peers))

    def row_slot(slot):
        return rows.at[pl.ds(slot * SLOT, SLOT)]

    def col_slot(slot):
        return cols.at[pl.ds(slot * OWN, OWN)]

    def col_half(slot, half):
        return cols.at[pl.ds(slot * OWN + half * (OWN // 2), OWN // 2)]

    for dx in (1, 3, 2):
        to = ROW_OF[neg_row((dx, 0))]
        send(row_slot(0), row_slot(to), x_send.at[0], row_recv.at[to], peer(dx=dx))
    send(row_slot(0), row_slot(4), x_send.at[0], row_recv.at[4], peer(dc=1))
    for turn in range(2):
        for d in (1, 3, 2):
            for axis in range(2):
                half = axis ^ turn
                off = (d, 0) if axis == 0 else (0, d)
                to = COL_OF[neg_col(off)]
                send(
                    col_half(0, half), col_half(to, half), x_send.at[1],
                    col_recv.at[to, half], peer(dy=off[0], dz=off[1]),
                )

    def pass_on(axis, d):
        off = (d, 0) if axis == 0 else (0, d)
        slot = COL_OF[off]
        wait_bytes(col_half(slot, axis), col_recv.at[slot, axis])
        for e in (1, 3, 2):
            hop = (0, e) if axis == 0 else (e, 0)
            to = COL_OF[((off[0] - hop[0]) % 4, (off[1] - hop[1]) % 4)]
            send(
                col_half(slot, axis), col_half(to, axis), x_send.at[1],
                col_recv.at[to, axis], peer(dy=hop[0], dz=hop[1]),
            )

    def pass_row(slot):
        wait_bytes(row_slot(slot), row_recv.at[slot])
        send(row_slot(slot), row_slot(4 + slot), x_send.at[0], row_recv.at[4 + slot], peer(dc=1))

    def lanes(e):
        total = e[:, 0:PROJ]
        for q in range(1, e.shape[1] // PROJ):
            total = total + e[:, q * PROJ : (q + 1) * PROJ]
        return total

    def scores(slot, first, end):
        return jnp.exp2(
            lax.dot_general(
                rows[slot * SLOT : slot * SLOT + OWN, :], cols[first * OWN : end * OWN, :], NT,
                preferred_element_type=F32,
            )
            * SCALE2
        )

    def pass1(slot, first, end):
        e = scores(slot, first, end)
        if slot == 0 and first == 0:
            at_row = lax.broadcasted_iota(jnp.int32, e.shape, 0)
            at_col = lax.broadcasted_iota(jnp.int32, e.shape, 1)
            e = jnp.where(at_row == at_col, 0.0, e)
        of = slice(slot * OWN, (slot + 1) * OWN)
        expo[of, first * OWN : end * OWN] = e.astype(BF16)
        if first == 0:
            acc[of, :] = lanes(e)
        else:
            acc[of, :] += lanes(e)

    def wait_ring(slot):
        half = 1 - RING_AXIS[slot]
        wait_bytes(col_half(slot, half), col_recv.at[slot, half])

    for d in (1, 3):
        pass_on(0, d)
        pass_on(1, d)
        pass_row(d)
    pass_on(0, 2)
    pass_on(1, 2)
    wait_bytes(row_slot(4), row_recv.at[4])
    for slot in range(1, 4):
        wait_ring(slot)
    for slot in (0, 4, 1, 3):
        pass1(slot, 0, 4)
    pass_row(2)
    send(
        feat.at[:, pl.ds(pl.multiple_of((1 - c) * HALF, HALF), HALF)], feat_sib,
        x_send.at[2], feat_recv.at[0], peer(dc=1),
    )
    for slot in range(4, RINGS):
        wait_ring(slot)
    for slot in (0, 4, 1, 3):
        pass1(slot, 4, RINGS)
    for slot in (5, 7, 6):
        wait_bytes(row_slot(slot), row_recv.at[slot])
    for slot in (5, 7, 2, 6):
        pass1(slot, 0, RINGS)
    for first, end in GROUPS:
        for slot in range(first, end):
            for half in range(2):
                wait_bytes(col_half(slot, half), col_recv.at[slot, half])
        for slot in range(8):
            pass1(slot, first, end)

    eye = lax.broadcasted_iota(jnp.int32, (PROJ, PROJ), 0) == lax.broadcasted_iota(
        jnp.int32, (PROJ, PROJ), 1
    )

    def to_row(column):
        return jnp.sum(jnp.where(eye, column, 0.0), axis=0, keepdims=True)

    def to_column(*rows_of):
        halves = [
            jnp.sum(jnp.where(eye, row, 0.0), axis=1, keepdims=True) for row in rows_of
        ]
        return jnp.broadcast_to(jnp.concatenate(halves, axis=0), (OWN, PROJ))

    for slot in range(8):
        for h in range(2):
            first = slot * OWN + h * PROJ
            column = jnp.sum(acc[first : first + PROJ, :], axis=1, keepdims=True)
            sums[slot : slot + 1, h * PROJ : (h + 1) * PROJ] = to_row(column)
    for slot in (2, 6, 1, 3, 5, 7, 4):
        dx, dc = ROW_OFFS[slot]
        to = ROW_OF[neg_row((dx, dc))]
        send(sums, sums_in.at[to], x_send.at[3], sum_recv.at[to], peer(dx=dx, dc=dc))

    for slot in range(16):
        block = cols[slot * OWN : (slot + 1) * OWN, :]
        wide[:, slot * PROJ : (slot + 1) * PROJ] = block
        uw[slot * OWN : (slot + 1) * OWN, 0:PROJ] = block
    lane = lax.broadcasted_iota(jnp.int32, (OWN, PROJ), 1).astype(F32)

    def partners(slot, pos):
        code = rows[slot * SLOT + OWN : (slot + 1) * SLOT, :].astype(F32)
        owner = to_column(code[0:1], code[1:2])
        place = to_column(code[2:3], code[3:4])
        hot = jnp.concatenate(
            [jnp.where(place == lane, 1.0, 0.0), jnp.where(place == lane + PROJ, 1.0, 0.0)], axis=1
        ).astype(BF16)
        found = jnp.dot(hot, wide[...], preferred_element_type=F32)
        total = jnp.zeros((OWN, PROJ), F32)
        for k in range(16):
            dy, dz = COL_OFFS[k]
            dp, inner = peer(dy=dy, dz=dz)
            here = (dp * 8 + inner).astype(F32)
            total = total + jnp.where(owner == here, found[:, k * PROJ : (k + 1) * PROJ], 0.0)
        paired[slot * OWN : (slot + 1) * OWN, :] = total
        own = rows[slot * SLOT : slot * SLOT + OWN, :].astype(F32)
        return pos + own * total

    pos = jnp.zeros((OWN, PROJ), F32)
    for slot in range(4):
        pos = partners(slot, pos)

    for slot in range(1, 8):
        wait_bytes(sums_in.at[slot], sum_recv.at[slot])
    for slot in range(8):
        dx, dc = ROW_OFFS[slot]
        total = sums[slot : slot + 1, :]
        for sender in range(1, 8):
            ox, oc = ROW_OFFS[sender]
            at = ROW_OF[((dx - ox) % 4, (dc - oc) % 2)]
            total = total + sums_in[sender, at : at + 1, :]
        for h in range(2):
            wts[slot, h : h + 1, :] = 1.0 / total[:, h * PROJ : (h + 1) * PROJ]
        if slot == 0:
            log_sum = jnp.sum(jnp.log(total))
    for slot in range(1, 16):
        dy, dz = COL_OFFS[slot]
        to = COL_OF[neg_col((dy, dz))]
        send(wts.at[0], wts_in.at[to], x_send.at[4], wt_recv.at[to], peer(dy=dy, dz=dz))

    for slot in range(4, 8):
        pos = partners(slot, pos)
    for slot in range(8):
        w_rows[slot * OWN : (slot + 1) * OWN, :] = to_column(wts[slot, 0:1, :], wts[slot, 1:2, :])
    loss_part = log_sum - INV_TAU * jnp.sum(pos)
    me1 = x * 2 + c
    loss1[me1] = jnp.full((1, PROJ), loss_part, F32)
    for slot in range(1, 8):
        dx, dc = ROW_OFFS[slot]
        to = ROW_OF[neg_row((dx, dc))]
        send(loss1.at[me1], loss1.at[me1], x_send.at[5], loss_recv1.at[to], peer(dx=dx, dc=dc))

    def weigh(slot, table):
        block = cols[slot * OWN : (slot + 1) * OWN, :]
        uw[slot * OWN : (slot + 1) * OWN, PROJ : 2 * PROJ] = (
            block.astype(F32) * to_column(table[0:1], table[1:2])
        ).astype(BF16)

    weigh(0, wts[0])
    for slot in range(1, 16):
        wait_bytes(wts_in.at[slot], wt_recv.at[slot])
    for slot in range(1, 16):
        weigh(slot, wts_in[slot])

    def product(slot):
        return jnp.dot(
            expo[slot * OWN : (slot + 1) * OWN, :], uw[...], preferred_element_type=F32
        )

    def terms(slot, both):
        w = w_rows[slot * OWN : (slot + 1) * OWN, :]
        return (
            w * both[:, 0:PROJ] + both[:, PROJ : 2 * PROJ]
            - 2.0 * paired[slot * OWN : (slot + 1) * OWN, :]
        )

    def quad_slot(slot):
        return quad.at[pl.ds(slot * OWN, OWN)]

    def finish(slot, both):
        quad[slot * OWN : (slot + 1) * OWN, :] = terms(slot, both)
        if slot > 3:
            send(
                quad_slot(slot), quad_sib.at[slot - 4], x_send.at[6], qs_recv.at[slot - 4],
                peer(dc=1),
            )

    def complete(slot):
        quad[slot * OWN : (slot + 1) * OWN, :] += quad_sib[slot]
        if slot:
            to = (-slot) % 4
            send(quad_slot(slot), quad_ring.at[to], x_send.at[7], qr_recv.at[to], peer(dx=slot))

    def add_sibling(slot):
        wait_bytes(quad_sib.at[slot], qs_recv.at[slot])
        complete(slot)

    finish(6, product(6))
    finish(2, product(2))
    add_sibling(2)
    slot, both = 5, product(5)
    for later in (7, 1, 3):
        both_later = product(later)
        finish(slot, both)
        slot, both = later, both_later
    add_sibling(1)
    finish(3, both)
    add_sibling(3)
    both, both_later = product(4), product(0)
    finish(4, both)
    finish(0, both_later)
    add_sibling(0)

    summed = quad[0:OWN, :]
    for d in (1, 3, 2):
        wait_bytes(quad_ring.at[d], qr_recv.at[d])
        summed = summed + quad_ring[d]
    du = INV_TAU * summed
    uu = u_ref[...]
    dz_own[...] = (
        (du - uu * jnp.sum(uu * du, axis=1, keepdims=True)) / norm_ref[...]
    ).astype(BF16)
    send(dz_own, dz_sib, x_send.at[9], dz_recv.at[0], peer(dc=1))

    mine = pl.multiple_of(c * HALF, HALF)
    grad[...] = lax.dot_general(
        feat[:, pl.ds(mine, HALF)], dz_own[...], TN, preferred_element_type=F32
    )
    wait_bytes(feat_sib, feat_recv.at[0])
    wait_bytes(dz_sib, dz_recv.at[0])
    g1_in, g1, g2_in = (g1_in_a, g1_in_b, g1_in_c), (g1_a, g1_b, g1_c), (g2_in_a, g2_in_b, g2_in_c)
    parts = (2, 1, 0)

    def ring_block(part, d, base=0):
        span = 16 * TILES[part]
        first = base + STARTS[part] + torus.ring_at(part, d) * span
        return pl.ds(pl.multiple_of(first, span), span)

    def block_row(part, d1):
        span = 4 * TILES[part]
        return pl.ds(pl.multiple_of(torus.row_at(part, d1) * span, span), span)

    def plane_row(part, d, d1, base=0):
        span = 4 * TILES[part]
        first = base + STARTS[part] + torus.ring_at(part, d) * 4 * span
        return pl.ds(pl.multiple_of(first + torus.row_at(part, d1) * span, span), span)

    for part in (0, 1, 2):
        of = slice(STARTS[part], STARTS[part] + 64 * TILES[part])
        grad[of, :] += lax.dot_general(feat_sib[:, of], dz_sib[...], TN, preferred_element_type=F32)
        for d1 in (2, 1, 3, 0):
            for d in (2, 1, 3):
                at = (-d) % 4
                send(
                    grad.at[plane_row(part, d, d1)], g1_in[part].at[at, block_row(part, d1)],
                    x_send.at[10], g1_recv.at[part, at, d1], torus.ring_peer(part, d),
                )

    for d1 in (2, 1, 3, 0):
        for part in parts:
            rows_of = block_row(part, d1)
            total = grad[plane_row(part, 0, d1), :]
            for d in (1, 3, 2):
                wait_bytes(g1_in[part].at[d, rows_of], g1_recv.at[part, d, d1])
                total = total + g1_in[part][d, rows_of, :]
            g1[part][rows_of, :] = total
            tile = TILES[part]
            for d2 in (2, 1, 3, 0):
                if not (d1 or d2):
                    continue
                to = COL_OF[neg_col((d1, d2))]
                at = pl.multiple_of(torus.plane_at(part, d1, d2) * tile, tile)
                send(
                    g1[part].at[pl.ds(at, tile)], g2_in[part].at[pl.ds(to * tile, tile)],
                    x_send.at[11], g2_recv.at[part], torus.plane_peer(part, d1, d2),
                )
    for slot in range(1, 8):
        wait_bytes(loss1.at[0], loss_recv1.at[slot])
    total = loss1[0]
    for k in range(1, 8):
        total = total + loss1[k]
    me2 = y * 4 + z
    loss2[me2] = total
    for slot in range(1, 16):
        dy, dz = COL_OFFS[slot]
        to = COL_OF[neg_col((dy, dz))]
        send(loss2.at[me2], loss2.at[me2], x_send.at[8], loss_recv2.at[to], peer(dy=dy, dz=dz))

    base = c * HALF
    for part in parts:
        tile = TILES[part]
        place = torus.plane_at(part, 0, 0) * tile
        total = g1[part][pl.ds(pl.multiple_of(place, tile), tile), :]
        wait_bytes(g2_in[part].at[pl.ds(tile, 15 * tile)], g2_recv.at[part])
        for slot in range(1, 16):
            total = total + g2_in[part][slot * tile : (slot + 1) * tile, :]
        first = base + STARTS[part] + torus.ring_at(part, 0) * 16 * tile + place
        at = pl.ds(pl.multiple_of(first, tile), tile)
        out[at, :] = total * (1.0 / VIEWS**0.5)
        for slot in sorted(range(1, 16), key=lambda k: (COL_OFFS[k][0] != 0, -k)):
            d1, d2 = COL_OFFS[slot]
            send(
                out.at[at], out.at[at], x_send.at[12], ag_recv.at[part, (-d1) % 4],
                torus.plane_peer(part, d1, d2),
            )

    for d1 in (0, 1, 3, 2):
        for part in parts:
            wait_bytes(out.at[pl.ds(0, (4 if d1 else 3) * TILES[part])], ag_recv.at[part, d1])
            block = plane_row(part, 0, d1, base)
            for d in (2, 1, 3):
                send(
                    out.at[block], out.at[block], x_send.at[13],
                    ring_recv.at[part, (-d) % 4, d1], torus.ring_peer(part, d),
                )
    for part in parts:
        block = ring_block(part, 0, base)
        send(out.at[block], out.at[block], x_send.at[14], rel_recv.at[part, 0], peer(dc=1))
    for d1 in (0, 1, 3, 2):
        for d in (1, 3, 2):
            for part in parts:
                block = plane_row(part, d, d1, base)
                wait_bytes(out.at[block], ring_recv.at[part, d, d1])
                send(out.at[block], out.at[block], x_send.at[14], rel_recv.at[part, d], peer(dc=1))

    for slot in range(1, 16):
        wait_bytes(loss2.at[0], loss_recv2.at[slot])
    total = loss2[0]
    for k in range(1, 16):
        total = total + loss2[k]
    loss_ref[...] = total[0:1, 0:1] * (1.0 / VIEWS)

    other = torus.cs[1] * HALF
    for d in (0, 1, 3, 2):
        for part in parts:
            span = 16 * TILES[part]
            ends = (torus.ys[d], torus.xs[d])
            ring = torus.zs[d] if part == 2 else torus.pick(*(ends if part == 0 else ends[::-1]))
            block = pl.ds(pl.multiple_of(other + STARTS[part] + ring * span, span), span)
            wait_bytes(out.at[block], rel_recv.at[part, d])

    for ref, at in sent:
        wait_bytes(ref, x_send.at[at])


def per_device(features, proj_weight, partner):
    dma = pltpu.SemaphoreType.DMA
    grad, loss = pl.pallas_call(
        kernel,
        out_shape=(
            pltpu.VMEM((D, PROJ), F32),
            pltpu.VMEM((1, 1), F32),
        ),
        in_specs=[
            pl.BlockSpec(memory_space=pl.ANY),
            pl.BlockSpec(memory_space=pl.ANY),
            pl.BlockSpec(memory_space=pl.ANY),
        ],
        out_specs=(pl.BlockSpec(memory_space=pltpu.VMEM), pl.BlockSpec(memory_space=pltpu.VMEM)),
        scratch_shapes=[
            pltpu.VMEM((2, PROJ), jnp.int32),
            pltpu.VMEM((OWN, D), BF16),
            pltpu.VMEM((D, PROJ), BF16),
            pltpu.VMEM((OWN, HALF), BF16),
            pltpu.VMEM((OWN, PROJ), F32),
            pltpu.VMEM((OWN, PROJ), F32),
            pltpu.VMEM((8 * SLOT, PROJ), BF16),
            pltpu.VMEM((16 * OWN, PROJ), BF16),
            pltpu.VMEM((8 * OWN, 16 * OWN), BF16),
            pltpu.VMEM((8 * OWN, PROJ), F32),
            pltpu.VMEM((8, OWN), F32),
            pltpu.VMEM((8, 8, OWN), F32),
            pltpu.VMEM((8, 2, PROJ), F32),
            pltpu.VMEM((16, 2, PROJ), F32),
            pltpu.VMEM((OWN, 16 * PROJ), BF16),
            pltpu.VMEM((8 * OWN, PROJ), F32),
            pltpu.VMEM((16 * OWN, 2 * PROJ), BF16),
            pltpu.VMEM((8 * OWN, PROJ), F32),
            pltpu.VMEM((8 * OWN, PROJ), F32),
            pltpu.VMEM((4, OWN, PROJ), F32),
            pltpu.VMEM((4, OWN, PROJ), F32),
            pltpu.VMEM((OWN, PROJ), BF16),
            pltpu.VMEM((OWN, PROJ), BF16),
            pltpu.VMEM((HALF, PROJ), F32),
            *[pltpu.VMEM((4, 16 * tile, PROJ), F32) for tile in TILES],
            *[pltpu.VMEM((16 * tile, PROJ), F32) for tile in TILES],
            *[pltpu.VMEM((16 * tile, PROJ), F32) for tile in TILES],
            pltpu.VMEM((8, 1, PROJ), F32),
            pltpu.VMEM((16, 1, PROJ), F32),
            dma((9,)),
            dma((15,)),
            dma((16, 2)),
            dma((8,)),
            dma((1,)),
            dma((8,)),
            dma((16,)),
            dma((8,)),
            dma((16,)),
            dma((4,)),
            dma((4,)),
            dma((1,)),
            dma((3, 4, 4)),
            dma((3,)),
            dma((3, 4)),
            dma((3, 4, 4)),
            dma((3, 4)),
        ],
        compiler_params=pltpu.CompilerParams(
            collective_id=0, has_side_effects=True, vmem_limit_bytes=56 * 2**20
        ),
        name="simclr_head",
    )(features, proj_weight, partner.reshape(2, PROJ))
    return loss.reshape(()), grad


def solution(mesh):
    placed = (P(("dp", "inner"), None), P(), P(("dp", "inner")))
    return jax.shard_map(
        per_device, mesh=mesh, in_specs=placed, out_specs=(P(), P()), check_vma=False
    )
```

```python
import jax
import jax.numpy as jnp
from jax import lax
from jax.experimental import pallas as pl
from jax.experimental.pallas import tpu as pltpu
from jax.sharding import PartitionSpec as P

MESH = pl.DeviceIdType.MESH
F32 = jnp.float32
BF16 = jnp.bfloat16
VIEWS = 32768
D = 4096
HALF = D // 2
QUARTER = D // 4
PROJ = 128
OWN = 256
RINGS = 7
GROUPS = ((RINGS, 11), (11, 16))
SLOT = OWN + 16
INV_TAU = 5.0
SCALE2 = INV_TAU * 1.4426950408889634
NT = (((1,), (1,)), ((), ()))
TN = (((0,), (0,)), ((), ()))

ROW_OFFS = [(dx, dc) for dc in range(2) for dx in range(4)]
ROW_OF = {off: slot for slot, off in enumerate(ROW_OFFS)}
COL_OFFS = sorted(
    [(dy, dz) for dy in range(4) for dz in range(4)],
    key=lambda o: (0 not in o, min(o[0], 4 - o[0]) + min(o[1], 4 - o[1]), o),
)
COL_OF = {off: slot for slot, off in enumerate(COL_OFFS)}
RING_AXIS = {slot: int(off[0] == 0) for slot, off in enumerate(COL_OFFS) if slot and 0 in off}
TILES = (16, 8, 8)
STARTS = (0, 1024, 1536)


def neg_col(off):
    return ((-off[0]) % 4, (-off[1]) % 4)


def neg_row(off):
    return ((-off[0]) % 4, off[1])


def coords():
    dp, inner = lax.axis_index("dp"), lax.axis_index("inner")
    x = (inner % 2) * 2 + dp // 8
    return x, (dp // 2) % 4, inner // 2, dp % 2


def device_at(x, y, z, c):
    return ((x % 2) * 8 + y * 2 + c, z * 2 + x // 2)


class Torus:
    def __init__(self):
        x, y, z, c = coords()
        self.xs, self.ys, self.zs = ([(v + d) % 4 for d in range(4)] for v in (x, y, z))
        self.cs = [c, 1 - c]
        self.x_dp = [v % 2 * 8 for v in self.xs]
        self.x_inner = [v // 2 for v in self.xs]
        self.y_dp = [v * 2 for v in self.ys]
        self.z_inner = [v * 2 for v in self.zs]

    def peer(self, dx=0, dy=0, dz=0, dc=0):
        return (
            self.x_dp[dx] + self.y_dp[dy] + self.cs[dc],
            self.z_inner[dz] + self.x_inner[dx],
        )

    def pick(self, a, b):
        return a * self.cs[1] + b * self.cs[0]

    def pick_peer(self, a, b):
        return self.pick(a[0], b[0]), self.pick(a[1], b[1])

    def ring_at(self, part, d):
        if part == 2:
            return self.zs[d]
        ends = (self.xs[d], self.ys[d])
        return self.pick(*(ends if part == 0 else ends[::-1]))

    def row_at(self, part, d1):
        if part == 2:
            return self.xs[d1]
        ends = (self.ys[d1], self.xs[d1])
        return self.pick(*(ends if part == 0 else ends[::-1]))

    def plane_at(self, part, d1, d2):
        if part == 2:
            return self.xs[d1] * 4 + self.ys[d2]
        ends = (self.ys[d1], self.xs[d1])
        return self.pick(*(ends if part == 0 else ends[::-1])) * 4 + self.zs[d2]

    def ring_peer(self, part, d):
        if part == 2:
            return self.peer(dz=d)
        ends = (self.peer(dx=d), self.peer(dy=d))
        return self.pick_peer(*(ends if part == 0 else ends[::-1]))

    def plane_peer(self, part, d1, d2):
        if part == 2:
            return self.peer(dx=d1, dy=d2)
        ends = (self.peer(dy=d1, dz=d2), self.peer(dx=d1, dz=d2))
        return self.pick_peer(*(ends if part == 0 else ends[::-1]))


def ring_peers():
    offs = [off for d in (2, 1, 3) for off in ((d, 0, 0, 0), (0, d, 0, 0), (0, 0, d, 0))]
    return offs + [(0, 0, 0, 1)]


def send(src, dst, send_sem, recv_sem, device):
    copy = pltpu.make_async_remote_copy(
        src_ref=src, dst_ref=dst, send_sem=send_sem, recv_sem=recv_sem,
        device_id=device, device_id_type=MESH,
    )
    copy.start()


def wait_bytes(ref, sem):
    pltpu.make_async_copy(ref, ref, sem).wait()


def kernel(
    f_hbm, w_hbm, partner_hbm, out, loss_ref,
    partner_ref, feat, weight, feat_sib, u_ref, norm_ref, rows, cols, expo, acc,
    sums, sums_in, wts, wts_in, wide, paired, uw, w_rows, quad, quad_sib, quad_ring,
    dz_own, dz_sib, grad, g1_in_a, g1_in_b, g1_in_c, g1_a, g1_b, g1_c,
    g2_in_a, g2_in_b, g2_in_c, loss1, loss2,
    load_sem, x_send, col_recv, row_recv, feat_recv, sum_recv, wt_recv, loss_recv1, loss_recv2,
    qs_recv, qr_recv, dz_recv, g1_recv, g2_recv, ag_recv, ring_recv, rel_recv,
):
    sent = [
        (rows.at[pl.ds(0, 7 * SLOT)], 0),
        (cols.at[pl.ds(0, 15 * OWN)], 1),
        (feat_sib, 2),
        (sums_in.at[pl.ds(0, 7)], 3),
        (wts_in.at[pl.ds(0, 15)], 4),
        (loss1.at[pl.ds(0, 7)], 5),
        (quad_sib, 6),
        (quad_ring.at[pl.ds(0, 3)], 7),
        (loss2.at[pl.ds(0, 15)], 8),
        (dz_sib, 9),
        (grad.at[pl.ds(0, 3 * HALF // 4)], 10),
        (grad.at[pl.ds(0, 15 * sum(TILES))], 11),
        (grad.at[pl.ds(0, 15 * sum(TILES))], 12),
        (grad.at[pl.ds(0, 3 * HALF // 4)], 13),
        (grad, 14),
    ]
    torus = Torus()
    peer = torus.peer
    x, y, z, c = torus.xs[0], torus.ys[0], torus.zs[0], torus.cs[0]
    loads = []
    for k in range(4):
        depth = pl.ds(k * QUARTER, QUARTER)
        loads.append(
            (
                pltpu.make_async_copy(w_hbm.at[depth], weight.at[depth], load_sem.at[k]),
                pltpu.make_async_copy(f_hbm.at[:, depth], feat.at[:, depth], load_sem.at[4 + k]),
            )
        )
    barrier = pltpu.get_barrier_semaphore()
    peers = ring_peers()
    for off in peers:
        pl.semaphore_signal(barrier, inc=1, device_id=peer(*off), device_id_type=MESH)

    load_partner = pltpu.make_async_copy(partner_hbm, partner_ref, load_sem.at[8])
    load_partner.start()
    for pair in loads:
        for load in pair:
            load.start()
    load_partner.wait()
    owner_of, place_of = partner_ref[...] // OWN, partner_ref[...] % OWN
    at = lax.broadcasted_iota(jnp.int32, (16, PROJ), 0)
    code = jnp.zeros((16, PROJ), F32)
    for k, row in enumerate((owner_of[0:1], owner_of[1:2], place_of[0:1], place_of[1:2])):
        code = jnp.where(at == k, row.astype(F32), code)
    rows[OWN:SLOT, :] = code.astype(BF16)

    zed = None
    for k, pair in enumerate(loads):
        for load in pair:
            load.wait()
        term = jnp.dot(
            feat[:, k * QUARTER : (k + 1) * QUARTER], weight[k * QUARTER : (k + 1) * QUARTER, :],
            preferred_element_type=F32,
        )
        zed = term if zed is None else zed + term
    norm = jnp.sqrt(jnp.sum(zed * zed, axis=1, keepdims=True) + 1e-06)
    u = zed / norm
    u_ref[...] = u
    norm_ref[...] = jnp.broadcast_to(norm, (OWN, PROJ))
    ub = u.astype(BF16)
    rows[0:OWN, :] = ub
    cols[0:OWN, :] = ub
    pl.semaphore_wait(barrier, len(peers))

    def row_slot(slot):
        return rows.at[pl.ds(slot * SLOT, SLOT)]

    def col_slot(slot):
        return cols.at[pl.ds(slot * OWN, OWN)]

    def col_half(slot, half):
        return cols.at[pl.ds(slot * OWN + half * (OWN // 2), OWN // 2)]

    for dx in (1, 3, 2):
        to = ROW_OF[neg_row((dx, 0))]
        send(row_slot(0), row_slot(to), x_send.at[0], row_recv.at[to], peer(dx=dx))
    send(row_slot(0), row_slot(4), x_send.at[0], row_recv.at[4], peer(dc=1))
    for turn in range(2):
        for d in (1, 3, 2):
            for axis in range(2):
                half = axis ^ turn
                off = (d, 0) if axis == 0 else (0, d)
                to = COL_OF[neg_col(off)]
                send(
                    col_half(0, half), col_half(to, half), x_send.at[1],
                    col_recv.at[to, half], peer(dy=off[0], dz=off[1]),
                )

    def pass_on(axis, d):
        off = (d, 0) if axis == 0 else (0, d)
        slot = COL_OF[off]
        wait_bytes(col_half(slot, axis), col_recv.at[slot, axis])
        for e in (1, 3, 2):
            hop = (0, e) if axis == 0 else (e, 0)
            to = COL_OF[((off[0] - hop[0]) % 4, (off[1] - hop[1]) % 4)]
            send(
                col_half(slot, axis), col_half(to, axis), x_send.at[1],
                col_recv.at[to, axis], peer(dy=hop[0], dz=hop[1]),
            )

    def pass_row(slot):
        wait_bytes(row_slot(slot), row_recv.at[slot])
        send(row_slot(slot), row_slot(4 + slot), x_send.at[0], row_recv.at[4 + slot], peer(dc=1))

    def lanes(e):
        total = e[:, 0:PROJ]
        for q in range(1, e.shape[1] // PROJ):
            total = total + e[:, q * PROJ : (q + 1) * PROJ]
        return total

    def scores(slot, first, end):
        return jnp.exp2(
            lax.dot_general(
                rows[slot * SLOT : slot * SLOT + OWN, :], cols[first * OWN : end * OWN, :], NT,
                preferred_element_type=F32,
            )
            * SCALE2
        )

    def pass1(slot, first, end):
        e = scores(slot, first, end)
        if slot == 0 and first == 0:
            at_row = lax.broadcasted_iota(jnp.int32, e.shape, 0)
            at_col = lax.broadcasted_iota(jnp.int32, e.shape, 1)
            e = jnp.where(at_row == at_col, 0.0, e)
        of = slice(slot * OWN, (slot + 1) * OWN)
        expo[of, first * OWN : end * OWN] = e.astype(BF16)
        if first == 0:
            acc[of, :] = lanes(e)
        else:
            acc[of, :] += lanes(e)

    def wait_ring(slot):
        half = 1 - RING_AXIS[slot]
        wait_bytes(col_half(slot, half), col_recv.at[slot, half])

    for d in (1, 3):
        pass_on(0, d)
        pass_on(1, d)
        pass_row(d)
    pass_on(0, 2)
    pass_on(1, 2)
    wait_bytes(row_slot(4), row_recv.at[4])
    for slot in range(1, 4):
        wait_ring(slot)
    for slot in (0, 4, 1, 3):
        pass1(slot, 0, 4)
    pass_row(2)
    send(
        feat.at[:, pl.ds(pl.multiple_of((1 - c) * HALF, HALF), HALF)], feat_sib,
        x_send.at[2], feat_recv.at[0], peer(dc=1),
    )
    for slot in range(4, RINGS):
        wait_ring(slot)
    for slot in (0, 4, 1, 3):
        pass1(slot, 4, RINGS)
    for slot in (5, 7, 6):
        wait_bytes(row_slot(slot), row_recv.at[slot])
    for slot in (5, 7, 2, 6):
        pass1(slot, 0, RINGS)
    for first, end in GROUPS:
        for slot in range(first, end):
            for half in range(2):
                wait_bytes(col_half(slot, half), col_recv.at[slot, half])
        for slot in range(8):
            pass1(slot, first, end)

    eye = lax.broadcasted_iota(jnp.int32, (PROJ, PROJ), 0) == lax.broadcasted_iota(
        jnp.int32, (PROJ, PROJ), 1
    )

    def to_row(column):
        return jnp.sum(jnp.where(eye, column, 0.0), axis=0, keepdims=True)

    def to_column(*rows_of):
        halves = [
            jnp.sum(jnp.where(eye, row, 0.0), axis=1, keepdims=True) for row in rows_of
        ]
        return jnp.broadcast_to(jnp.concatenate(halves, axis=0), (OWN, PROJ))

    for slot in range(8):
        for h in range(2):
            first = slot * OWN + h * PROJ
            column = jnp.sum(acc[first : first + PROJ, :], axis=1, keepdims=True)
            sums[slot : slot + 1, h * PROJ : (h + 1) * PROJ] = to_row(column)
    for slot in (2, 6, 1, 3, 5, 7, 4):
        dx, dc = ROW_OFFS[slot]
        to = ROW_OF[neg_row((dx, dc))]
        send(sums, sums_in.at[to], x_send.at[3], sum_recv.at[to], peer(dx=dx, dc=dc))

    for slot in range(16):
        block = cols[slot * OWN : (slot + 1) * OWN, :]
        wide[:, slot * PROJ : (slot + 1) * PROJ] = block
        uw[slot * OWN : (slot + 1) * OWN, 0:PROJ] = block
    lane = lax.broadcasted_iota(jnp.int32, (OWN, PROJ), 1).astype(F32)

    def partners(slot, pos):
        code = rows[slot * SLOT + OWN : (slot + 1) * SLOT, :].astype(F32)
        owner = to_column(code[0:1], code[1:2])
        place = to_column(code[2:3], code[3:4])
        hot = jnp.concatenate(
            [jnp.where(place == lane, 1.0, 0.0), jnp.where(place == lane + PROJ, 1.0, 0.0)], axis=1
        ).astype(BF16)
        found = jnp.dot(hot, wide[...], preferred_element_type=F32)
        total = jnp.zeros((OWN, PROJ), F32)
        for k in range(16):
            dy, dz = COL_OFFS[k]
            dp, inner = peer(dy=dy, dz=dz)
            here = (dp * 8 + inner).astype(F32)
            total = total + jnp.where(owner == here, found[:, k * PROJ : (k + 1) * PROJ], 0.0)
        paired[slot * OWN : (slot + 1) * OWN, :] = total
        own = rows[slot * SLOT : slot * SLOT + OWN, :].astype(F32)
        return pos + own * total

    pos = jnp.zeros((OWN, PROJ), F32)
    for slot in range(4):
        pos = partners(slot, pos)

    for slot in range(1, 8):
        wait_bytes(sums_in.at[slot], sum_recv.at[slot])
    for slot in range(8):
        dx, dc = ROW_OFFS[slot]
        total = sums[slot : slot + 1, :]
        for sender in range(1, 8):
            ox, oc = ROW_OFFS[sender]
            at = ROW_OF[((dx - ox) % 4, (dc - oc) % 2)]
            total = total + sums_in[sender, at : at + 1, :]
        for h in range(2):
            wts[slot, h : h + 1, :] = 1.0 / total[:, h * PROJ : (h + 1) * PROJ]
        if slot == 0:
            log_sum = jnp.sum(jnp.log(total))
    for slot in range(1, 16):
        dy, dz = COL_OFFS[slot]
        to = COL_OF[neg_col((dy, dz))]
        send(wts.at[0], wts_in.at[to], x_send.at[4], wt_recv.at[to], peer(dy=dy, dz=dz))

    for slot in range(4, 8):
        pos = partners(slot, pos)
    for slot in range(8):
        w_rows[slot * OWN : (slot + 1) * OWN, :] = to_column(wts[slot, 0:1, :], wts[slot, 1:2, :])
    loss_part = log_sum - INV_TAU * jnp.sum(pos)
    me1 = x * 2 + c
    loss1[me1] = jnp.full((1, PROJ), loss_part, F32)
    for slot in range(1, 8):
        dx, dc = ROW_OFFS[slot]
        to = ROW_OF[neg_row((dx, dc))]
        send(loss1.at[me1], loss1.at[me1], x_send.at[5], loss_recv1.at[to], peer(dx=dx, dc=dc))

    def weigh(slot, table):
        block = cols[slot * OWN : (slot + 1) * OWN, :]
        uw[slot * OWN : (slot + 1) * OWN, PROJ : 2 * PROJ] = (
            block.astype(F32) * to_column(table[0:1], table[1:2])
        ).astype(BF16)

    weigh(0, wts[0])
    for slot in range(1, 16):
        wait_bytes(wts_in.at[slot], wt_recv.at[slot])
    for slot in range(1, 16):
        weigh(slot, wts_in[slot])

    def product(slot):
        return jnp.dot(
            expo[slot * OWN : (slot + 1) * OWN, :], uw[...], preferred_element_type=F32
        )

    def terms(slot, both):
        w = w_rows[slot * OWN : (slot + 1) * OWN, :]
        return (
            w * both[:, 0:PROJ] + both[:, PROJ : 2 * PROJ]
            - 2.0 * paired[slot * OWN : (slot + 1) * OWN, :]
        )

    def quad_slot(slot):
        return quad.at[pl.ds(slot * OWN, OWN)]

    def finish(slot, both):
        quad[slot * OWN : (slot + 1) * OWN, :] = terms(slot, both)
        if slot > 3:
            send(
                quad_slot(slot), quad_sib.at[slot - 4], x_send.at[6], qs_recv.at[slot - 4],
                peer(dc=1),
            )

    def complete(slot):
        quad[slot * OWN : (slot + 1) * OWN, :] += quad_sib[slot]
        if slot:
            to = (-slot) % 4
            send(quad_slot(slot), quad_ring.at[to], x_send.at[7], qr_recv.at[to], peer(dx=slot))

    def add_sibling(slot):
        wait_bytes(quad_sib.at[slot], qs_recv.at[slot])
        complete(slot)

    finish(6, product(6))
    finish(2, product(2))
    add_sibling(2)
    slot, both = 5, product(5)
    for later in (7, 1, 3):
        both_later = product(later)
        finish(slot, both)
        slot, both = later, both_later
    add_sibling(1)
    finish(3, both)
    add_sibling(3)
    both, both_later = product(4), product(0)
    finish(4, both)
    finish(0, both_later)
    add_sibling(0)

    summed = quad[0:OWN, :]
    for d in (1, 3, 2):
        wait_bytes(quad_ring.at[d], qr_recv.at[d])
        summed = summed + quad_ring[d]
    du = INV_TAU * summed
    uu = u_ref[...]
    dz_own[...] = (
        (du - uu * jnp.sum(uu * du, axis=1, keepdims=True)) / norm_ref[...]
    ).astype(BF16)
    send(dz_own, dz_sib, x_send.at[9], dz_recv.at[0], peer(dc=1))

    mine = pl.multiple_of(c * HALF, HALF)
    grad[...] = lax.dot_general(
        feat[:, pl.ds(mine, HALF)], dz_own[...], TN, preferred_element_type=F32
    )
    wait_bytes(feat_sib, feat_recv.at[0])
    wait_bytes(dz_sib, dz_recv.at[0])
    g1_in, g1, g2_in = (g1_in_a, g1_in_b, g1_in_c), (g1_a, g1_b, g1_c), (g2_in_a, g2_in_b, g2_in_c)
    parts = (2, 1, 0)

    def ring_block(part, d, base=0):
        span = 16 * TILES[part]
        first = base + STARTS[part] + torus.ring_at(part, d) * span
        return pl.ds(pl.multiple_of(first, span), span)

    def block_row(part, d1):
        span = 4 * TILES[part]
        return pl.ds(pl.multiple_of(torus.row_at(part, d1) * span, span), span)

    def plane_row(part, d, d1, base=0):
        span = 4 * TILES[part]
        first = base + STARTS[part] + torus.ring_at(part, d) * 4 * span
        return pl.ds(pl.multiple_of(first + torus.row_at(part, d1) * span, span), span)

    for part in (0, 1, 2):
        of = slice(STARTS[part], STARTS[part] + 64 * TILES[part])
        grad[of, :] += lax.dot_general(feat_sib[:, of], dz_sib[...], TN, preferred_element_type=F32)
        for d1 in (2, 1, 3, 0):
            for d in (2, 1, 3):
                at = (-d) % 4
                send(
                    grad.at[plane_row(part, d, d1)], g1_in[part].at[at, block_row(part, d1)],
                    x_send.at[10], g1_recv.at[part, at, d1], torus.ring_peer(part, d),
                )

    for d1 in (2, 1, 3, 0):
        for part in parts:
            rows_of = block_row(part, d1)
            total = grad[plane_row(part, 0, d1), :]
            for d in (1, 3, 2):
                wait_bytes(g1_in[part].at[d, rows_of], g1_recv.at[part, d, d1])
                total = total + g1_in[part][d, rows_of, :]
            g1[part][rows_of, :] = total
            tile = TILES[part]
            for d2 in (2, 1, 3, 0):
                if not (d1 or d2):
                    continue
                to = COL_OF[neg_col((d1, d2))]
                at = pl.multiple_of(torus.plane_at(part, d1, d2) * tile, tile)
                send(
                    g1[part].at[pl.ds(at, tile)], g2_in[part].at[pl.ds(to * tile, tile)],
                    x_send.at[11], g2_recv.at[part], torus.plane_peer(part, d1, d2),
                )
    for slot in range(1, 8):
        wait_bytes(loss1.at[0], loss_recv1.at[slot])
    total = loss1[0]
    for k in range(1, 8):
        total = total + loss1[k]
    me2 = y * 4 + z
    loss2[me2] = total
    for slot in range(1, 16):
        dy, dz = COL_OFFS[slot]
        to = COL_OF[neg_col((dy, dz))]
        send(loss2.at[me2], loss2.at[me2], x_send.at[8], loss_recv2.at[to], peer(dy=dy, dz=dz))

    base = c * HALF
    for part in parts:
        tile = TILES[part]
        place = torus.plane_at(part, 0, 0) * tile
        total = g1[part][pl.ds(pl.multiple_of(place, tile), tile), :]
        wait_bytes(g2_in[part].at[pl.ds(tile, 15 * tile)], g2_recv.at[part])
        for slot in range(1, 16):
            total = total + g2_in[part][slot * tile : (slot + 1) * tile, :]
        first = base + STARTS[part] + torus.ring_at(part, 0) * 16 * tile + place
        at = pl.ds(pl.multiple_of(first, tile), tile)
        out[at, :] = total * (1.0 / VIEWS**0.5)
        for slot in sorted(range(1, 16), key=lambda k: (COL_OFFS[k][0] != 0, -k)):
            d1, d2 = COL_OFFS[slot]
            send(
                out.at[at], out.at[at], x_send.at[12], ag_recv.at[part, (-d1) % 4],
                torus.plane_peer(part, d1, d2),
            )

    for d1 in (0, 1, 3, 2):
        for part in parts:
            wait_bytes(out.at[pl.ds(0, (4 if d1 else 3) * TILES[part])], ag_recv.at[part, d1])
            block = plane_row(part, 0, d1, base)
            for d in (2, 1, 3):
                send(
                    out.at[block], out.at[block], x_send.at[13],
                    ring_recv.at[part, (-d) % 4, d1], torus.ring_peer(part, d),
                )
    for part in parts:
        block = ring_block(part, 0, base)
        send(out.at[block], out.at[block], x_send.at[14], rel_recv.at[part, 0], peer(dc=1))
    for d1 in (0, 1, 3, 2):
        for d in (1, 3, 2):
            for part in parts:
                block = plane_row(part, d, d1, base)
                wait_bytes(out.at[block], ring_recv.at[part, d, d1])
                send(out.at[block], out.at[block], x_send.at[14], rel_recv.at[part, d], peer(dc=1))

    for slot in range(1, 16):
        wait_bytes(loss2.at[0], loss_recv2.at[slot])
    total = loss2[0]
    for k in range(1, 16):
        total = total + loss2[k]
    loss_ref[...] = total[0:1, 0:1] * (1.0 / VIEWS)

    other = torus.cs[1] * HALF
    for d in (0, 1, 3, 2):
        for part in parts:
            span = 16 * TILES[part]
            ends = (torus.ys[d], torus.xs[d])
            ring = torus.zs[d] if part == 2 else torus.pick(*(ends if part == 0 else ends[::-1]))
            block = pl.ds(pl.multiple_of(other + STARTS[part] + ring * span, span), span)
            wait_bytes(out.at[block], rel_recv.at[part, d])

    for ref, at in sent:
        wait_bytes(ref, x_send.at[at])


def per_device(features, proj_weight, partner):
    dma = pltpu.SemaphoreType.DMA
    grad, loss = pl.pallas_call(
        kernel,
        out_shape=(
            pltpu.VMEM((D, PROJ), F32),
            pltpu.VMEM((1, 1), F32),
        ),
        in_specs=[
            pl.BlockSpec(memory_space=pl.ANY),
            pl.BlockSpec(memory_space=pl.ANY),
            pl.BlockSpec(memory_space=pl.ANY),
        ],
        out_specs=(pl.BlockSpec(memory_space=pltpu.VMEM), pl.BlockSpec(memory_space=pltpu.VMEM)),
        scratch_shapes=[
            pltpu.VMEM((2, PROJ), jnp.int32),
            pltpu.VMEM((OWN, D), BF16),
            pltpu.VMEM((D, PROJ), BF16),
            pltpu.VMEM((OWN, HALF), BF16),
            pltpu.VMEM((OWN, PROJ), F32),
            pltpu.VMEM((OWN, PROJ), F32),
            pltpu.VMEM((8 * SLOT, PROJ), BF16),
            pltpu.VMEM((16 * OWN, PROJ), BF16),
            pltpu.VMEM((8 * OWN, 16 * OWN), BF16),
            pltpu.VMEM((8 * OWN, PROJ), F32),
            pltpu.VMEM((8, OWN), F32),
            pltpu.VMEM((8, 8, OWN), F32),
            pltpu.VMEM((8, 2, PROJ), F32),
            pltpu.VMEM((16, 2, PROJ), F32),
            pltpu.VMEM((OWN, 16 * PROJ), BF16),
            pltpu.VMEM((8 * OWN, PROJ), F32),
            pltpu.VMEM((16 * OWN, 2 * PROJ), BF16),
            pltpu.VMEM((8 * OWN, PROJ), F32),
            pltpu.VMEM((8 * OWN, PROJ), F32),
            pltpu.VMEM((4, OWN, PROJ), F32),
            pltpu.VMEM((4, OWN, PROJ), F32),
            pltpu.VMEM((OWN, PROJ), BF16),
            pltpu.VMEM((OWN, PROJ), BF16),
            pltpu.VMEM((HALF, PROJ), F32),
            *[pltpu.VMEM((4, 16 * tile, PROJ), F32) for tile in TILES],
            *[pltpu.VMEM((16 * tile, PROJ), F32) for tile in TILES],
            *[pltpu.VMEM((16 * tile, PROJ), F32) for tile in TILES],
            pltpu.VMEM((8, 1, PROJ), F32),
            pltpu.VMEM((16, 1, PROJ), F32),
            dma((9,)),
            dma((15,)),
            dma((16, 2)),
            dma((8,)),
            dma((1,)),
            dma((8,)),
            dma((16,)),
            dma((8,)),
            dma((16,)),
            dma((4,)),
            dma((4,)),
            dma((1,)),
            dma((3, 4, 4)),
            dma((3,)),
            dma((3, 4)),
            dma((3, 4, 4)),
            dma((3, 4)),
        ],
        compiler_params=pltpu.CompilerParams(
            collective_id=0, has_side_effects=True, vmem_limit_bytes=56 * 2**20
        ),
        name="simclr_head",
    )(features, proj_weight, partner.reshape(2, PROJ))
    return loss.reshape(()), grad


def solution(mesh):
    placed = (P(("dp", "inner"), None), P(), P(("dp", "inner")))
    return jax.shard_map(
        per_device, mesh=mesh, in_specs=placed, out_specs=(P(), P()), check_vma=False
    )
```
